128 devices in a mesh: dp: 32 (over y, z, x_lo), blk: 4 (over x_hi, core).
Axes of the slice: x: 4 (x_hi: 2, x_lo: 2; x = x_hi * 2 + x_lo), y: 4, z: 4, core: 2. Of those that a mesh axis runs over, the one named last changes fastest.
Arguments:
- hidden_in: bfloat16 [64, 1024, 512], P('dp', 'blk'), may hold values from -6 to 6
- gene_ids: int32 [64, 1024], P('dp', 'blk'), may hold values from 0 to 60696
- unknown_count: int32 [64], P('dp'), may hold values from 256 to 768, as said below
- gene_scale: float32 [60697], replicated, may hold values from 0.5 to 2
- w_inputs: bfloat16 [2, 512, 1536], replicated, may hold values from -0.25 to 0.25
- b_query: float32 [2, 512], replicated, may hold values from -3 to 3
- b_value: float32 [2, 512], replicated, may hold values from -3 to 3
- w_output: bfloat16 [2, 512, 512], replicated, may hold values from -4 to 4
- b_output: float32 [2, 512], replicated, may hold values from -3 to 3
- gain_one: float32 [2, 512], replicated, may hold values from 0.5 to 1.5
- shift_one: float32 [2, 512], replicated, may hold values from -2 to 2
- w_up: bfloat16 [2, 512, 512], replicated, may hold values from -0.25 to 0.25
- b_up: float32 [2, 512], replicated, may hold values from -3 to 3
- w_down: bfloat16 [2, 512, 512], replicated, may hold values from -0.25 to 0.25
- b_down: float32 [2, 512], replicated, may hold values from -3 to 3
- gain_two: float32 [2, 512], replicated, may hold values from 0.5 to 1.5
- shift_two: float32 [2, 512], replicated, may hold values from -2 to 2
- cotangent: bfloat16 [64, 1024, 512], P('dp', 'blk'), may hold values from -6 to 6
Outputs:
- layer_out: float32 [64, 1024, 512], P('dp', 'blk')
- grad_hidden: float32 [64, 1024, 512], P('dp', 'blk')
- grad_gene_scale: float32 [60697], replicated
- grad_w_inputs: float32 [2, 512, 1536], replicated
- grad_b_query: float32 [2, 512], replicated
- grad_b_value: float32 [2, 512], replicated
- grad_w_output: float32 [2, 512, 512], replicated
- grad_b_output: float32 [2, 512], replicated
- grad_gain_one: float32 [2, 512], replicated
- grad_shift_one: float32 [2, 512], replicated
- grad_w_up: float32 [2, 512, 512], replicated
- grad_b_up: float32 [2, 512], replicated
- grad_w_down: float32 [2, 512, 512], replicated
- grad_b_down: float32 [2, 512], replicated
- grad_gain_two: float32 [2, 512], replicated
- grad_shift_two: float32 [2, 512], replicated
The draws below stay inside these ranges and needn't reach their ends.
Inputs may be any that keep to these rules, and one draw needn't show every extreme that they name: The last unknown_count[c] of cell c's 1024 tokens are its unknown genes; the others are known.
All inputs are finite; a program needn't handle non-finite values.
Results may differ from the reference program's by a relative error of at most 0.019.
The reference program's roundings to bfloat16 on the way count: a program that leaves them out, or rounds other values in their place, can miss the bound.
Values may be sent and summed in bfloat16 or wider, within the bound.
A program may use at most 192 MiB of HBM per device.

```python
import math
import jax
import jax.numpy as jnp
import numpy as np
from jax import lax

D = 512
HEADS = 8
HDIM = 64
FF = 512
VOCAB = 60697
GENES = 1024
CELLS = 64


def draw_unknown_count(key, part):
    key = jax.random.fold_in(key, 11)
    fewest = GENES // 4
    largest = 3 * GENES // 4
    counts = jax.random.randint(key, (CELLS,), fewest, largest + 1, dtype=jnp.int32)
    places = jax.random.permutation(jax.random.fold_in(key, 1), CELLS)
    counts = counts.at[places[0]].set(fewest)
    counts = counts.at[places[1]].set(largest)
    return counts.astype(jnp.int32)


def touch_ends(entries, key, low, high):
    dims = entries.shape
    place = [jax.random.randint(jax.random.fold_in(key, axis), (), 0, dims[axis]) for axis in range(len(dims))]
    entries = entries.at[tuple(place)].set(low)
    longest = dims.index(max(dims))
    place[longest] = (place[longest] + 1) % dims[longest]
    return entries.at[tuple(place)].set(high)


def shard_levels(own_key, shape, cuts, least, high):
    level = 1.0
    for axis_at, shards_of in cuts:
        heights = jax.random.uniform(jax.random.fold_in(jax.random.fold_in(own_key, 6), axis_at), (shards_of,), jnp.float32, least / len(cuts), high / len(cuts))
        level = level * jnp.repeat(jnp.exp(heights), shape[axis_at] // shards_of).reshape((-1,) + (1,) * (len(shape) - 1 - axis_at))
    return level


def rank_bounds(amount, slope):
    loads = [(1 << 20) // math.isqrt(grade ** slope) + 1 for grade in range(1, amount + 1)]
    width = 1 + sum(loads) // (1 << 30)
    return np.cumsum(np.array([max(1, weight // width) for weight in loads]))


def skewed_ids(own_key, dims, count, lean):
    listing = rank_bounds(count, lean)
    lot = jax.random.randint(jax.random.fold_in(own_key, 1), dims, 0, int(listing[count - 1]))
    rank = jnp.searchsorted(jnp.asarray(listing, jnp.int32), lot, side="right")
    return jax.random.permutation(jax.random.fold_in(own_key, 2), count)[rank].astype(jnp.int32)


def bell_draw(key, extent, scale, reach, shards=(), kind=jnp.bfloat16):
    entries = jax.random.normal(key, extent, jnp.float32) * scale
    if len(shards) > 0:
        entries = shard_levels(key, extent, shards, -0.22, 0.18) * entries
    return jnp.clip(entries, min=-reach, max=reach).astype(kind)


def setup_inputs(seed: int = 0) -> dict:
    arg_keys = jax.random.split(jax.random.key(seed), 19)
    hidden_in = bell_draw(arg_keys[0], (CELLS, GENES, D), 1.0, 6.0, ((0, 32), (1, 4)))
    gene_ids = touch_ends(skewed_ids(arg_keys[1], (CELLS, GENES), VOCAB, 2), jax.random.fold_in(arg_keys[1], 3), 0, VOCAB - 1).astype(jnp.int32)
    unknown_count = draw_unknown_count(jax.random.fold_in(arg_keys[18], 71), 0)
    gene_scale = jnp.clip(jnp.exp(jax.random.uniform(arg_keys[3], (VOCAB,), jnp.float32, math.log(0.5), math.log(2.0))), 0.5, 2.0)
    w_inputs = bell_draw(arg_keys[4], (2, D, 3 * D), D ** -0.5, 0.25)
    b_query = bell_draw(arg_keys[5], (2, D), 0.5, 3.0, (), jnp.float32)
    b_value = bell_draw(arg_keys[6], (2, D), 0.5, 3.0, (), jnp.float32)
    w_output = bell_draw(arg_keys[7], (2, D, D), (max(1, D // 256)) ** -0.5, 4.0)
    b_output = bell_draw(arg_keys[8], (2, D), 0.5, 3.0, (), jnp.float32)
    gain_one = jnp.clip(1.0 + 0.1 * jax.random.normal(arg_keys[9], (2, D), jnp.float32), 0.5, 1.5)
    shift_one = bell_draw(arg_keys[10], (2, D), 0.3, 2.0, (), jnp.float32)
    w_up = bell_draw(arg_keys[11], (2, D, FF), D ** -0.5, 0.25)
    b_up = bell_draw(arg_keys[12], (2, FF), 0.5, 3.0, (), jnp.float32)
    w_down = bell_draw(arg_keys[13], (2, FF, D), FF ** -0.5, 0.25)
    b_down = bell_draw(arg_keys[14], (2, D), 0.5, 3.0, (), jnp.float32)
    gain_two = jnp.clip(1.0 + 0.1 * jax.random.normal(arg_keys[15], (2, D), jnp.float32), 0.5, 1.5)
    shift_two = bell_draw(arg_keys[16], (2, D), 0.3, 2.0, (), jnp.float32)
    cotangent = bell_draw(arg_keys[17], (CELLS, GENES, D), 1.0, 6.0, ((0, 32), (1, 4)))
    return dict(hidden_in=hidden_in, gene_ids=gene_ids, unknown_count=unknown_count, gene_scale=gene_scale, w_inputs=w_inputs, b_query=b_query, b_value=b_value, w_output=w_output, b_output=b_output, gain_one=gain_one, shift_one=shift_one, w_up=w_up, b_up=b_up, w_down=w_down, b_down=b_down, gain_two=gain_two, shift_two=shift_two, cotangent=cotangent)


@jax.custom_vjp
def low(v):
    return lax.optimization_barrier(v.astype(jnp.bfloat16)).astype(jnp.float32)

@jax.custom_vjp
def low_back(v):
    return v

def low_keep(v):
    return (low(v), None)

def low_pass(kept, grad):
    return (grad,)

def back_keep(v):
    return (v, None)

def back_low(kept, grad):
    return (low(grad),)
low.defvjp(low_keep, low_pass)
low_back.defvjp(back_keep, back_low)

def product(left, right):
    return jnp.matmul(left, right, precision=lax.Precision.HIGHEST)

def layer_norm(values, gain, shift):
    center = values - lax.optimization_barrier(jnp.mean(values, axis=-1, keepdims=True))
    spread = lax.optimization_barrier(jnp.mean(center * center, axis=-1, keepdims=True))
    return center * lax.rsqrt(spread + 1e-05) * gain + shift

def cell_attention(operands):
    queries, keys, values, known_count = operands
    query_heads = queries.reshape(GENES, HEADS, HDIM)
    key_heads = keys.reshape(GENES, HEADS, HDIM)
    value_heads = values.reshape(GENES, HEADS, HDIM)
    raw_scores = jnp.einsum('qhd,khd->hqk', query_heads, key_heads, precision=lax.Precision.HIGHEST)
    scores = low_back(raw_scores * HDIM ** (-0.5))
    positions = jnp.arange(GENES, dtype=jnp.int32)
    allowed = (positions[None, :] < known_count) | (positions[None, :] == positions[:, None])
    masked = jnp.where(allowed[None], scores, -1e+30)
    row_max = lax.optimization_barrier(jnp.max(masked, axis=-1, keepdims=True))
    exponent = jnp.exp(masked - row_max)
    probabilities = low(exponent / lax.optimization_barrier(jnp.sum(exponent, axis=-1, keepdims=True)))
    mixed = jnp.einsum('hqk,khd->qhd', probabilities, value_heads, precision=lax.Precision.HIGHEST)
    return mixed.reshape(GENES, D)

def layer_forward(stream, layer_params, known_count):
    w_inputs, b_query, b_value, w_output, b_output, gain_one, shift_one, w_up, b_up, w_down, b_down, gain_two, shift_two = layer_params
    flat_in = stream.reshape(-1, D)
    packed = product(low(flat_in), w_inputs)
    queries = low_back(low(packed[:, :D] + b_query))
    keys = low_back(low(packed[:, D:2 * D]))
    values = low_back(low(packed[:, 2 * D:] + b_value))
    mixed = lax.map(jax.checkpoint(cell_attention), (queries.reshape(CELLS, GENES, D), keys.reshape(CELLS, GENES, D), values.reshape(CELLS, GENES, D), known_count))
    attended = low_back(product(low_back(low(mixed.reshape(-1, D))), w_output) + b_output)
    normed = layer_norm(flat_in + attended, gain_one, shift_one)
    inner_pre = low_back(product(low(normed), w_up) + b_up)
    branch = low_back(product(low(jax.nn.gelu(inner_pre, approximate=False)), w_down) + b_down)
    return layer_norm(normed + branch, gain_two, shift_two).reshape(stream.shape)

def reference(hidden_in, gene_ids, unknown_count, gene_scale, w_inputs, b_query, b_value, w_output, b_output, gain_one, shift_one, w_up, b_up, w_down, b_down, gain_two, shift_two, cotangent):
    known_count = (GENES - unknown_count).astype(jnp.int32)
    params = tuple((member.astype(jnp.float32) for member in (w_inputs, b_query, b_value, w_output, b_output, gain_one, shift_one, w_up, b_up, w_down, b_down, gain_two, shift_two)))

    def forward(hidden, scale_table, weights):
        stream = hidden * scale_table[gene_ids][..., None]
        for layer_index in range(2):
            layer_params = tuple((member[layer_index] for member in weights))
            stream = layer_forward(stream, layer_params, known_count)
        return stream
    layer_out, backward = jax.vjp(forward, hidden_in.astype(jnp.float32), gene_scale, params)
    grad_hidden, grad_scale, grad_params = backward(cotangent.astype(jnp.float32))
    return (layer_out, grad_hidden, grad_scale, grad_params[0], grad_params[1], grad_params[2], grad_params[3], grad_params[4], grad_params[5], grad_params[6], grad_params[7], grad_params[8], grad_params[9], grad_params[10], grad_params[11], grad_params[12])
```

```python
import jax
import jax.numpy as jnp
from jax import lax
from jax.experimental import pallas as pl
from jax.experimental.pallas import tpu as pltpu
from jax.sharding import PartitionSpec as P

HEADS = 8
HDIM = 64
VECTORS = (1, 2, 4, 5, 6, 8, 10, 11, 12)


MESH = pl.DeviceIdType.MESH
AXIS_ORDER = ((0, 1, 2), (1, 2, 0), (2, 0, 1))
PART_ROWS = 1024
HALF_ROWS = 3 * PART_ROWS
BATCH_ROWS = 2 * HALF_ROWS
STEP_ROWS = (256, 64, 16)
EXTRA_ROWS = 192
EXTRA_HALF = EXTRA_ROWS // 2
EXTRA_PIECE = EXTRA_HALF // 4


class Place:
    def __init__(self):
        dp = lax.axis_index("dp")
        blk = lax.axis_index("blk")
        self.y = dp // 8
        self.z = (dp // 2) % 4
        self.x_lo = dp % 2
        self.x_hi = blk // 2
        self.core = blk % 2
        self.coord = (self.x_hi * 2 + self.x_lo, self.y, self.z)

    def device(self, coord, core):
        x, y, z = coord
        return ((y * 4 + z) * 2 + x % 2, (x // 2) * 2 + core)

    def sibling(self):
        return self.device(self.coord, 1 - self.core)

    def peer(self, axis, distance):
        coord = list(self.coord)
        coord[axis] = (coord[axis] + distance) % 4
        return self.device(coord, self.core)


def greet(place):
    barrier = pltpu.get_barrier_semaphore()
    others = [place.sibling()]
    for axis in range(3):
        for distance in (1, 2, 3):
            others.append(place.peer(axis, distance))
    for other in others:
        pl.semaphore_signal(barrier, inc=1, device_id=other, device_id_type=MESH)
    pl.semaphore_wait(barrier, len(others))


def remote(src, dst, send_sem, recv_sem, device):
    return pltpu.make_async_remote_copy(
        src_ref=src,
        dst_ref=dst,
        send_sem=send_sem,
        recv_sem=recv_sem,
        device_id=device,
        device_id_type=MESH,
    )


class Reduction:
    def __init__(self, place, batch, result, from_core, from_step, sems):
        self.place = place
        self.batch = batch
        self.result = result
        self.from_core = from_core
        self.from_step = from_step
        self.core_send, self.core_recv, self.step_send, self.step_recv = sems
        self.mine = place.core * HALF_ROWS
        self.other = (1 - place.core) * HALF_ROWS

    def offset(self, part, steps):
        rows = self.mine + part * PART_ROWS
        for step in range(steps):
            rows = rows + self.place.coord[AXIS_ORDER[part][step]] * STEP_ROWS[step]
        return pl.multiple_of(rows, 16)

    def core_copy(self):
        rows = pl.ds(pl.multiple_of(self.other, 16), HALF_ROWS)
        return remote(
            self.batch.at[rows],
            self.from_core,
            self.core_send.at[0],
            self.core_recv.at[0],
            self.place.sibling(),
        )

    def core_start(self):
        self.core_copy().start()

    def core_finish(self):
        self.core_copy().wait()
        size = STEP_ROWS[0]

        def add(i, _):
            here = pl.ds(pl.multiple_of(self.mine + i * size, 16), size)
            there = pl.ds(pl.multiple_of(i * size, 16), size)
            self.batch[here] = (
                self.batch[here].astype(jnp.float32) + self.from_core[there].astype(jnp.float32)
            ).astype(jnp.bfloat16)
            return 0

        lax.fori_loop(0, HALF_ROWS // size, add, 0)

    def slot(self, step, part, distance):
        return (step * 3 + part) * 3 + distance - 1

    def scatter_copies(self, step):
        size = STEP_ROWS[step]
        copies = []
        for part in range(3):
            axis = AXIS_ORDER[part][step]
            base = self.offset(part, step)
            for distance in (1, 2, 3):
                target = (self.place.coord[axis] + distance) % 4
                rows = pl.ds(pl.multiple_of(base + target * size, 16), size)
                slot = self.slot(step, part, distance)
                copies.append(
                    remote(
                        self.batch.at[rows],
                        self.from_step[step].at[part, distance - 1],
                        self.step_send.at[slot],
                        self.step_recv.at[slot],
                        self.place.peer(axis, distance),
                    )
                )
        return copies

    def scatter_start(self, step):
        for copy in self.scatter_copies(step):
            copy.start()

    def scatter_finish(self, step):
        for copy in self.scatter_copies(step):
            copy.wait()
        size = STEP_ROWS[step]
        for part in range(3):
            rows = pl.ds(self.offset(part, step + 1), size)
            total = self.batch[rows].astype(jnp.float32)
            for distance in (1, 2, 3):
                total = total + self.from_step[step][part, distance - 1].astype(jnp.float32)
            target = self.batch if step < 2 else self.result
            target[rows] = total.astype(jnp.bfloat16)

    def gather_copies(self, step):
        size = STEP_ROWS[step]
        copies = []
        for part in range(3):
            axis = AXIS_ORDER[part][step]
            rows = pl.ds(self.offset(part, step + 1), size)
            for distance in (1, 2, 3):
                slot = 27 + self.slot(step, part, distance)
                copies.append(
                    remote(
                        self.result.at[rows],
                        self.result.at[rows],
                        self.step_send.at[slot],
                        self.step_recv.at[slot],
                        self.place.peer(axis, distance),
                    )
                )
        return copies

    def gather_start(self, step):
        for copy in self.gather_copies(step):
            copy.start()

    def gather_finish(self, step):
        for copy in self.gather_copies(step):
            copy.wait()

    def share_copy(self):
        rows = pl.ds(pl.multiple_of(self.mine, 16), HALF_ROWS)
        return remote(
            self.result.at[rows],
            self.result.at[rows],
            self.core_send.at[1],
            self.core_recv.at[1],
            self.place.sibling(),
        )

    def share_start(self):
        self.share_copy().start()

    def share_finish(self):
        self.share_copy().wait()


class ExtraReduction:
    def __init__(self, place, rows_ref, result, from_core, from_x, from_plane, sems):
        self.place = place
        self.ref = rows_ref
        self.result = result
        self.from_core = from_core
        self.from_x = from_x
        self.from_plane = from_plane
        self.send, self.recv = sems
        self.mine = place.core * EXTRA_HALF
        self.other = (1 - place.core) * EXTRA_HALF

    def piece(self, quarter):
        return pl.ds(pl.multiple_of(self.mine + quarter * EXTRA_PIECE, 8), EXTRA_PIECE)

    def core_copy(self):
        rows = pl.ds(pl.multiple_of(self.other, 8), EXTRA_HALF)
        return remote(
            self.ref.at[rows], self.from_core, self.send.at[0], self.recv.at[0], self.place.sibling()
        )

    def core_start(self):
        self.core_copy().start()

    def core_finish(self):
        self.core_copy().wait()
        rows = pl.ds(pl.multiple_of(self.mine, 8), EXTRA_HALF)
        self.ref[rows] = self.ref[rows] + self.from_core[...]

    def x_copies(self):
        copies = []
        for distance in (1, 2, 3):
            target = (self.place.coord[0] + distance) % 4
            copies.append(
                remote(
                    self.ref.at[self.piece(target)],
                    self.from_x.at[distance - 1],
                    self.send.at[distance],
                    self.recv.at[distance],
                    self.place.peer(0, distance),
                )
            )
        return copies

    def x_start(self):
        for copy in self.x_copies():
            copy.start()

    def x_finish(self):
        for copy in self.x_copies():
            copy.wait()
        rows = self.piece(self.place.coord[0])
        self.ref[rows] = self.ref[rows] + self.from_x[0] + self.from_x[1] + self.from_x[2]

    def plane_copies(self, axis):
        copies = []
        mine = self.place.coord[axis]
        rows = self.piece(self.place.coord[0])
        for distance in (1, 2, 3):
            slot = axis * 3 + distance
            copies.append(
                remote(
                    self.ref.at[rows],
                    self.from_plane.at[axis - 1, mine],
                    self.send.at[slot],
                    self.recv.at[slot],
                    self.place.peer(axis, distance),
                )
            )
        return copies

    def plane_start(self, axis):
        for copy in self.plane_copies(axis):
            copy.start()

    def plane_finish(self, axis):
        rows = self.piece(self.place.coord[0])
        self.from_plane[axis - 1, self.place.coord[axis]] = self.ref[rows]
        for copy in self.plane_copies(axis):
            copy.wait()
        terms = [self.from_plane[axis - 1, place] for place in range(4)]
        target = self.ref if axis == 1 else self.result
        target[rows] = (terms[0] + terms[1]) + (terms[2] + terms[3])

    def x_back_copies(self):
        copies = []
        rows = self.piece(self.place.coord[0])
        for distance in (1, 2, 3):
            copies.append(
                remote(
                    self.result.at[rows],
                    self.result.at[rows],
                    self.send.at[9 + distance],
                    self.recv.at[9 + distance],
                    self.place.peer(0, distance),
                )
            )
        return copies

    def x_back_start(self):
        for copy in self.x_back_copies():
            copy.start()

    def x_back_finish(self):
        for copy in self.x_back_copies():
            copy.wait()

    def share_copy(self):
        rows = pl.ds(pl.multiple_of(self.mine, 8), EXTRA_HALF)
        return remote(
            self.result.at[rows], self.result.at[rows], self.send.at[13], self.recv.at[13], self.place.sibling()
        )

    def share_start(self):
        self.share_copy().start()

    def share_finish(self):
        self.share_copy().wait()


def reduction_scratch():
    return [
        pltpu.VMEM((HALF_ROWS, 128), jnp.bfloat16),
        pltpu.VMEM((3, 3, STEP_ROWS[0], 128), jnp.bfloat16),
        pltpu.VMEM((3, 3, STEP_ROWS[1], 128), jnp.bfloat16),
        pltpu.VMEM((3, 3, STEP_ROWS[2], 128), jnp.bfloat16),
        pltpu.SemaphoreType.DMA((2,)),
        pltpu.SemaphoreType.DMA((2,)),
        pltpu.SemaphoreType.DMA((54,)),
        pltpu.SemaphoreType.DMA((54,)),
    ]


def extra_scratch():
    return [
        pltpu.VMEM((EXTRA_HALF, 512), jnp.float32),
        pltpu.VMEM((3, EXTRA_PIECE, 512), jnp.float32),
        pltpu.VMEM((2, 4, EXTRA_PIECE, 512), jnp.float32),
        pltpu.SemaphoreType.DMA((14,)),
        pltpu.SemaphoreType.DMA((14,)),
    ]


def reduce_kernel(*refs):
    count = 4
    batches_in, extra_in, batches, extra = refs[:4]
    held, held_extra = refs[4:6]
    scratch = refs[6:]
    place = Place()
    held[...] = batches_in[...]
    held_extra[...] = extra_in[...]
    work = []
    for index in range(count):
        core, s0, s1, s2, a, b, c, d = scratch[index * 8 : index * 8 + 8]
        work.append(Reduction(place, held.at[index], batches.at[index], core, (s0, s1, s2), (a, b, c, d)))
    core, from_x, from_plane, a, b = scratch[count * 8 :]
    more = ExtraReduction(place, held_extra, extra, core, from_x, from_plane, (a, b))
    greet(place)
    more.core_start()
    for one in work:
        one.core_start()
    more.core_finish()
    more.x_start()
    for one in work:
        one.core_finish()
        one.scatter_start(0)
    more.x_finish()
    more.plane_start(1)
    for step in range(3):
        for one in work:
            one.scatter_finish(step)
            if step < 2:
                one.scatter_start(step + 1)
            else:
                one.gather_start(2)
        if step == 0:
            more.plane_finish(1)
            more.plane_start(2)
        elif step == 1:
            more.plane_finish(2)
            more.x_back_start()
        else:
            more.x_back_finish()
            more.share_start()
    for step in (2, 1, 0):
        for one in work:
            one.gather_finish(step)
            if step > 0:
                one.gather_start(step - 1)
            else:
                one.share_start()
    more.share_finish()
    for one in work:
        one.share_finish()


def reduce_all(batches, extra):
    scratch = [pltpu.VMEM(batches.shape, batches.dtype), pltpu.VMEM(extra.shape, extra.dtype)]
    for _ in range(4):
        scratch += reduction_scratch()
    scratch += extra_scratch()
    vmem = pl.BlockSpec(memory_space=pltpu.VMEM)
    return pl.pallas_call(
        reduce_kernel,
        out_shape=(
            jax.ShapeDtypeStruct(batches.shape, batches.dtype),
            jax.ShapeDtypeStruct(extra.shape, extra.dtype),
        ),
        in_specs=[vmem, vmem],
        out_specs=(vmem, vmem),
        scratch_shapes=scratch,
        compiler_params=pltpu.CompilerParams(
            collective_id=0, has_side_effects=True, vmem_limit_bytes=48 << 20
        ),
    )(batches, extra)


def to_tiles(matrix):
    rows, columns = matrix.shape
    return matrix.reshape(rows, columns // 128, 128).transpose(1, 0, 2).reshape(-1, 128)


def from_tiles(tiles, columns):
    return tiles.reshape(columns // 128, 512, 128).transpose(1, 0, 2).reshape(512, columns)


def layer_norm(values, gain, shift):
    center = values - jnp.mean(values, axis=-1, keepdims=True)
    spread = jnp.mean(center * center, axis=-1, keepdims=True)
    return center * lax.rsqrt(spread + 1e-05) * gain + shift


def gelu_exact(values):
    return jax.nn.gelu(values, approximate=False)


def split_heads(block):
    return block.reshape(block.shape[0], block.shape[1], HEADS, HDIM)


def masked_scores(queries, keys_all, allowed):
    raw_scores = jnp.einsum(
        "cqhd,ckhd->chqk",
        split_heads(queries),
        split_heads(keys_all),
        preferred_element_type=jnp.float32,
    )
    return jnp.where(allowed[:, None], raw_scores * HDIM ** (-0.5), -1e30)


def attend_forward(queries, keys_all, values_all, allowed):
    masked = masked_scores(queries, keys_all, allowed)
    row_max = jnp.max(masked, axis=-1, keepdims=True)
    exponent = jnp.exp(masked - row_max)
    row_sum = jnp.sum(exponent, axis=-1, keepdims=True)
    rounded = (exponent / row_sum).astype(jnp.bfloat16)
    mixed = jnp.einsum(
        "chqk,ckhd->cqhd", rounded, split_heads(values_all), preferred_element_type=jnp.float32
    )
    return (mixed.reshape(queries.shape), row_max, row_sum)


def attend_backward(queries, keys_all, values_all, allowed, row_max, row_sum, grad_mixed):
    score_scale = HDIM ** (-0.5)
    masked = masked_scores(queries, keys_all, allowed)
    probabilities = jnp.exp(masked - row_max) / row_sum
    grad_heads = split_heads(grad_mixed)
    grad_values = jnp.einsum(
        "chqk,cqhd->ckhd",
        probabilities.astype(jnp.bfloat16),
        grad_heads,
        preferred_element_type=jnp.float32,
    )
    grad_probs = jnp.einsum(
        "cqhd,ckhd->chqk", grad_heads, split_heads(values_all), preferred_element_type=jnp.float32
    )
    grad_scores = probabilities * (
        grad_probs - jnp.sum(grad_probs * probabilities, axis=-1, keepdims=True)
    )
    rounded = grad_scores.astype(jnp.bfloat16)
    grad_queries = (
        jnp.einsum(
            "chqk,ckhd->cqhd", rounded, split_heads(keys_all), preferred_element_type=jnp.float32
        )
        * score_scale
    )
    grad_keys = (
        jnp.einsum(
            "chqk,cqhd->ckhd", rounded, split_heads(queries), preferred_element_type=jnp.float32
        )
        * score_scale
    )
    return (
        grad_queries.reshape(queries.shape),
        grad_keys.reshape(keys_all.shape),
        grad_values.reshape(values_all.shape),
    )


def layer_forward(stream, layer_params, allowed):
    (
        w_inputs,
        b_query,
        b_value,
        w_output,
        b_output,
        gain_one,
        shift_one,
        w_up,
        b_up,
        w_down,
        b_down,
        gain_two,
        shift_two,
    ) = layer_params
    cell_count, row_count, model_width = stream.shape
    flat_in = stream.reshape(cell_count * row_count, model_width)
    round_in = flat_in.astype(jnp.bfloat16)
    packed = jnp.dot(round_in, w_inputs, preferred_element_type=jnp.float32)
    queries = (packed[:, :model_width] + b_query).astype(jnp.bfloat16).reshape(stream.shape)
    keys = packed[:, model_width : 2 * model_width].astype(jnp.bfloat16).reshape(stream.shape)
    values = (packed[:, 2 * model_width :] + b_value).astype(jnp.bfloat16).reshape(stream.shape)
    keys_all, values_all = (
        lax.all_gather(keys, "blk", axis=1, tiled=True),
        lax.all_gather(values, "blk", axis=1, tiled=True),
    )
    mixed, row_max, row_sum = attend_forward(queries, keys_all, values_all, allowed)
    mixed_round = mixed.reshape(flat_in.shape).astype(jnp.bfloat16)
    first_sum = flat_in + (
        jnp.dot(mixed_round, w_output, preferred_element_type=jnp.float32) + b_output
    )
    normed = layer_norm(first_sum, gain_one, shift_one)
    normed_round = normed.astype(jnp.bfloat16)
    inner_pre = jnp.dot(normed_round, w_up, preferred_element_type=jnp.float32) + b_up
    active_round = gelu_exact(inner_pre).astype(jnp.bfloat16)
    second = normed + (jnp.dot(active_round, w_down, preferred_element_type=jnp.float32) + b_down)
    output = layer_norm(second, gain_two, shift_two).reshape(stream.shape)
    stored = (
        round_in,
        queries,
        keys,
        values,
        keys_all,
        values_all,
        row_max,
        row_sum,
        mixed_round,
        first_sum,
        normed_round,
        inner_pre,
        active_round,
        second,
    )
    return (output, stored)


def layer_backward(grad_out, stored, layer_params, allowed):
    (
        w_inputs,
        b_query,
        b_value,
        w_output,
        b_output,
        gain_one,
        shift_one,
        w_up,
        b_up,
        w_down,
        b_down,
        gain_two,
        shift_two,
    ) = layer_params
    (
        round_in,
        queries,
        keys,
        values,
        kept_keys,
        kept_values,
        row_max,
        row_sum,
        mixed_round,
        first_sum,
        normed_round,
        inner_pre,
        active_round,
        second,
    ) = stored
    model_width = queries.shape[2]
    norm_value, norm_two_back = jax.vjp(layer_norm, second, gain_two, shift_two)
    grad_second, grad_gain_two, grad_shift_two = norm_two_back(grad_out)
    grad_branch = grad_second.astype(jnp.bfloat16)
    grad_w_down = jnp.einsum(
        "nf,nd->fd", active_round, grad_branch, preferred_element_type=jnp.float32
    )
    grad_b_down = jnp.sum(grad_branch.astype(jnp.float32), axis=0)
    grad_active = jnp.einsum("nd,fd->nf", grad_branch, w_down, preferred_element_type=jnp.float32)
    gelu_value, gelu_back = jax.vjp(gelu_exact, inner_pre)
    grad_inner = gelu_back(grad_active)[0].astype(jnp.bfloat16)
    grad_w_up = jnp.einsum(
        "nd,nf->df", normed_round, grad_inner, preferred_element_type=jnp.float32
    )
    grad_b_up = jnp.sum(grad_inner.astype(jnp.float32), axis=0)
    grad_normed = grad_second + jnp.einsum(
        "nf,df->nd", grad_inner, w_up, preferred_element_type=jnp.float32
    )
    norm_value, norm_one_back = jax.vjp(layer_norm, first_sum, gain_one, shift_one)
    grad_first, grad_gain_one, grad_shift_one = norm_one_back(grad_normed)
    grad_attn = grad_first.astype(jnp.bfloat16)
    grad_w_output = jnp.einsum(
        "nd,ne->de", mixed_round, grad_attn, preferred_element_type=jnp.float32
    )
    grad_b_output = jnp.sum(grad_attn.astype(jnp.float32), axis=0)
    grad_mixed = (
        jnp.einsum("ne,de->nd", grad_attn, w_output, preferred_element_type=jnp.float32)
        .astype(jnp.bfloat16)
        .reshape(queries.shape)
    )
    keys_all, values_all = (
        lax.all_gather(keys, "blk", axis=1, tiled=True),
        lax.all_gather(values, "blk", axis=1, tiled=True),
    )
    grad_queries, grad_keys_all, grad_values_all = attend_backward(
        queries, keys_all, values_all, allowed, row_max, row_sum, grad_mixed
    )
    grad_keys, grad_values = (
        lax.psum_scatter(
            grad_keys_all.astype(jnp.bfloat16), "blk", scatter_dimension=1, tiled=True
        ).astype(jnp.float32),
        lax.psum_scatter(
            grad_values_all.astype(jnp.bfloat16), "blk", scatter_dimension=1, tiled=True
        ).astype(jnp.float32),
    )
    grad_packed = jnp.concatenate(
        [
            grad_queries.astype(jnp.bfloat16),
            grad_keys.astype(jnp.bfloat16),
            grad_values.astype(jnp.bfloat16),
        ],
        axis=-1,
    ).reshape(round_in.shape[0], 3 * model_width)
    grad_w_inputs = jnp.einsum(
        "nd,ne->de", round_in, grad_packed, preferred_element_type=jnp.float32
    )
    grad_b_query = jnp.sum(grad_packed[:, :model_width].astype(jnp.float32), axis=0)
    grad_b_value = jnp.sum(grad_packed[:, 2 * model_width :].astype(jnp.float32), axis=0)
    grad_in = grad_first + jnp.einsum(
        "ne,de->nd", grad_packed, w_inputs, preferred_element_type=jnp.float32
    )
    gradients = (
        grad_w_inputs,
        grad_b_query,
        grad_b_value,
        grad_w_output,
        grad_b_output,
        grad_gain_one,
        grad_shift_one,
        grad_w_up,
        grad_b_up,
        grad_w_down,
        grad_b_down,
        grad_gain_two,
        grad_shift_two,
    )
    return (grad_in, gradients)


def shards(
    hidden_in,
    gene_ids,
    unknown_count,
    gene_scale,
    w_inputs,
    b_query,
    b_value,
    w_output,
    b_output,
    gain_one,
    shift_one,
    w_up,
    b_up,
    w_down,
    b_down,
    gain_two,
    shift_two,
    cotangent,
):
    cell_count, row_count, model_width = hidden_in.shape
    gene_count = row_count * lax.axis_size("blk")
    query_pos = lax.axis_index("blk") * row_count + jnp.arange(row_count, dtype=jnp.int32)
    key_pos = jnp.arange(gene_count, dtype=jnp.int32)
    known_count = gene_count - unknown_count
    allowed = (key_pos[None, None, :] < known_count[:, None, None]) | (
        key_pos[None, None, :] == query_pos[None, :, None]
    )
    params = (
        w_inputs,
        b_query,
        b_value,
        w_output,
        b_output,
        gain_one,
        shift_one,
        w_up,
        b_up,
        w_down,
        b_down,
        gain_two,
        shift_two,
    )
    token_scale = gene_scale[gene_ids]
    hidden = hidden_in.astype(jnp.float32)
    stream = hidden * token_scale[..., None]
    saved = []
    for layer_index in range(2):
        layer_params = tuple((member[layer_index] for member in params))
        stream, stored = layer_forward(stream, layer_params, allowed)
        saved.append(stored)
    grad_stream = cotangent.astype(jnp.float32).reshape(cell_count * row_count, model_width)
    collected = [None, None]
    grad_hidden = None
    for layer_index in (1, 0):
        layer_params = tuple((member[layer_index] for member in params))
        grad_stream, gradients = layer_backward(
            grad_stream, saved[layer_index], layer_params, allowed
        )
        if layer_index == 0:
            grad_start = grad_stream.reshape(cell_count, row_count, model_width)
            grad_hidden = grad_start * token_scale[..., None]
            per_token = jnp.sum(grad_start * hidden, axis=-1)
            gene_grad = (
                jnp.zeros(gene_scale.shape, jnp.float32)
                .at[gene_ids.reshape(-1)]
                .add(per_token.reshape(-1))
            )
            gradients = gradients + (gene_grad,)
        collected[layer_index] = gradients
    batches = []
    for layer_index in (1, 0):
        gradients = collected[layer_index]
        narrow = [gradients[member].astype(jnp.bfloat16) for member in (9, 7, 3, 0)]
        batches.append(jnp.concatenate([to_tiles(matrix) for matrix in narrow[:3]]))
        batches.append(to_tiles(narrow[3]))
    gene_count = gene_scale.shape[0]
    vectors = [collected[layer_index][member] for member in VECTORS for layer_index in (0, 1)]
    extra = jnp.concatenate(
        [jnp.pad(collected[0][13], (0, 120 * 512 - gene_count)).reshape(120, 512)]
        + [vector[None] for vector in vectors]
        + [jnp.zeros((EXTRA_ROWS - 120 - len(vectors), 512), jnp.float32)]
    )
    batches, extra = reduce_all(jnp.stack(batches), extra)
    batches = batches.astype(jnp.float32)
    stacked = [None] * 14
    for place, member in enumerate((9, 7, 3)):
        rows = slice(place * 2048, place * 2048 + 2048)
        stacked[member] = jnp.stack(
            [from_tiles(batches[2, rows], 512), from_tiles(batches[0, rows], 512)]
        )
    stacked[0] = jnp.stack([from_tiles(batches[3], 1536), from_tiles(batches[1], 1536)])
    for place, member in enumerate(VECTORS):
        stacked[member] = extra[120 + 2 * place : 122 + 2 * place]
    stacked[13] = extra[:120].reshape(-1)[:gene_count]
    return (
        stream,
        grad_hidden,
        stacked[13],
        stacked[0],
        stacked[1],
        stacked[2],
        stacked[3],
        stacked[4],
        stacked[5],
        stacked[6],
        stacked[7],
        stacked[8],
        stacked[9],
        stacked[10],
        stacked[11],
        stacked[12],
    )


def solution(mesh):
    placed = (
        P("dp", "blk", None),
        P("dp", "blk"),
        P("dp"),
        P(),
        P(),
        P(),
        P(),
        P(),
        P(),
        P(),
        P(),
        P(),
        P(),
        P(),
        P(),
        P(),
        P(),
        P("dp", "blk", None),
    )
    return jax.shard_map(
        shards,
        mesh=mesh,
        in_specs=placed,
        out_specs=(
            P("dp", "blk", None),
            P("dp", "blk", None),
            P(),
            P(),
            P(),
            P(),
            P(),
            P(),
            P(),
            P(),
            P(),
            P(),
            P(),
            P(),
            P(),
            P(),
        ),
        check_vma=False,
    )
```

```python
import jax
import jax.numpy as jnp
from jax import lax
from jax.experimental import pallas as pl
from jax.experimental.pallas import tpu as pltpu
from jax.sharding import PartitionSpec as P

HEADS = 8
MESH = pl.DeviceIdType.MESH
AXIS_ORDER = ((0, 1, 2), (1, 2, 0), (2, 0, 1))
PART_ROWS = 1024
HALF_ROWS = 3 * PART_ROWS
BATCH_ROWS = 2 * HALF_ROWS
STEP_ROWS = (256, 64, 16)
EXTRA_ROWS = 576
EXTRA_HALF = EXTRA_ROWS // 2
EXTRA_PIECE = EXTRA_HALF // 4


class Place:
    def __init__(self):
        dp = lax.axis_index("dp")
        blk = lax.axis_index("blk")
        self.y = dp // 8
        self.z = (dp // 2) % 4
        self.x_lo = dp % 2
        self.x_hi = blk // 2
        self.core = blk % 2
        self.coord = (self.x_hi * 2 + self.x_lo, self.y, self.z)

    def device(self, coord, core):
        x, y, z = coord
        return ((y * 4 + z) * 2 + x % 2, (x // 2) * 2 + core)

    def sibling(self):
        return self.device(self.coord, 1 - self.core)

    def peer(self, axis, distance):
        coord = list(self.coord)
        coord[axis] = (coord[axis] + distance) % 4
        return self.device(coord, self.core)


def greet(place):
    barrier = pltpu.get_barrier_semaphore()
    others = [place.sibling()]
    for axis in range(3):
        for distance in (1, 2, 3):
            others.append(place.peer(axis, distance))
    for other in others:
        pl.semaphore_signal(barrier, inc=1, device_id=other, device_id_type=MESH)
    pl.semaphore_wait(barrier, len(others))


def remote(src, dst, send_sem, recv_sem, device):
    return pltpu.make_async_remote_copy(
        src_ref=src,
        dst_ref=dst,
        send_sem=send_sem,
        recv_sem=recv_sem,
        device_id=device,
        device_id_type=MESH,
    )


class Reduction:
    def __init__(self, place, batch, result, from_core, from_step, sems):
        self.place = place
        self.batch = batch
        self.result = result
        self.from_core = from_core
        self.from_step = from_step
        self.core_send, self.core_recv, self.step_send, self.step_recv = sems
        self.mine = place.core * HALF_ROWS
        self.other = (1 - place.core) * HALF_ROWS

    def offset(self, part, steps):
        rows = self.mine + part * PART_ROWS
        for step in range(steps):
            rows = rows + self.place.coord[AXIS_ORDER[part][step]] * STEP_ROWS[step]
        return pl.multiple_of(rows, 16)

    def core_copy(self):
        rows = pl.ds(pl.multiple_of(self.other, 16), HALF_ROWS)
        return remote(
            self.batch.at[rows],
            self.from_core,
            self.core_send.at[0],
            self.core_recv.at[0],
            self.place.sibling(),
        )

    def core_start(self):
        self.core_copy().start()

    def core_finish(self):
        self.core_copy().wait()
        size = STEP_ROWS[0]

        def add(i, _):
            here = pl.ds(pl.multiple_of(self.mine + i * size, 16), size)
            there = pl.ds(pl.multiple_of(i * size, 16), size)
            self.batch[here] = (
                self.batch[here].astype(jnp.float32) + self.from_core[there].astype(jnp.float32)
            ).astype(jnp.bfloat16)
            return 0

        lax.fori_loop(0, HALF_ROWS // size, add, 0)

    def slot(self, step, part, distance):
        return (step * 3 + part) * 3 + distance - 1

    def scatter_copies(self, step):
        size = STEP_ROWS[step]
        copies = []
        for part in range(3):
            axis = AXIS_ORDER[part][step]
            base = self.offset(part, step)
            for distance in (1, 2, 3):
                target = (self.place.coord[axis] + distance) % 4
                rows = pl.ds(pl.multiple_of(base + target * size, 16), size)
                slot = self.slot(step, part, distance)
                copies.append(
                    remote(
                        self.batch.at[rows],
                        self.from_step[step].at[part, distance - 1],
                        self.step_send.at[slot],
                        self.step_recv.at[slot],
                        self.place.peer(axis, distance),
                    )
                )
        return copies

    def scatter_start(self, step):
        for copy in self.scatter_copies(step):
            copy.start()

    def scatter_finish(self, step):
        for copy in self.scatter_copies(step):
            copy.wait()
        size = STEP_ROWS[step]
        for part in range(3):
            rows = pl.ds(self.offset(part, step + 1), size)
            total = self.batch[rows].astype(jnp.float32)
            for distance in (1, 2, 3):
                total = total + self.from_step[step][part, distance - 1].astype(jnp.float32)
            self.batch[rows] = total.astype(jnp.bfloat16)

    def gather_copies(self, step):
        size = STEP_ROWS[step]
        copies = []
        for part in range(3):
            axis = AXIS_ORDER[part][step]
            rows = pl.ds(self.offset(part, step + 1), size)
            for distance in (1, 2, 3):
                slot = 27 + self.slot(step, part, distance)
                copies.append(
                    remote(
                        (self.batch if step == 2 else self.result).at[rows],
                        self.result.at[rows],
                        self.step_send.at[slot],
                        self.step_recv.at[slot],
                        self.place.peer(axis, distance),
                    )
                )
            if step == 2:
                copies.append(
                    pltpu.make_async_copy(
                        self.batch.at[rows], self.result.at[rows], self.step_send.at[54 + part]
                    )
                )
        return copies

    def gather_start(self, step):
        for copy in self.gather_copies(step):
            copy.start()

    def gather_finish(self, step):
        for copy in self.gather_copies(step):
            copy.wait()

    def share_copy(self):
        rows = pl.ds(pl.multiple_of(self.mine, 16), HALF_ROWS)
        return remote(
            self.result.at[rows],
            self.result.at[rows],
            self.core_send.at[1],
            self.core_recv.at[1],
            self.place.sibling(),
        )

    def share_start(self):
        self.share_copy().start()

    def share_finish(self):
        self.share_copy().wait()


class ExtraReduction:
    def __init__(self, place, rows_ref, result, from_core, from_x, from_plane, sems):
        self.place = place
        self.ref = rows_ref
        self.result = result
        self.from_core = from_core
        self.from_x = from_x
        self.from_plane = from_plane
        self.send, self.recv = sems
        self.mine = place.core * EXTRA_HALF
        self.other = (1 - place.core) * EXTRA_HALF

    def piece(self, quarter):
        return pl.ds(pl.multiple_of(self.mine + quarter * EXTRA_PIECE, 8), EXTRA_PIECE)

    def core_copy(self):
        rows = pl.ds(pl.multiple_of(self.other, 8), EXTRA_HALF)
        return remote(
            self.ref.at[rows], self.from_core, self.send.at[0], self.recv.at[0], self.place.sibling()
        )

    def core_start(self):
        self.core_copy().start()

    def core_finish(self):
        self.core_copy().wait()
        rows = pl.ds(pl.multiple_of(self.mine, 8), EXTRA_HALF)
        self.ref[rows] = self.ref[rows] + self.from_core[...]

    def x_copies(self):
        copies = []
        for distance in (1, 2, 3):
            target = (self.place.coord[0] + distance) % 4
            copies.append(
                remote(
                    self.ref.at[self.piece(target)],
                    self.from_x.at[distance - 1],
                    self.send.at[distance],
                    self.recv.at[distance],
                    self.place.peer(0, distance),
                )
            )
        return copies

    def x_start(self):
        for copy in self.x_copies():
            copy.start()

    def x_finish(self):
        for copy in self.x_copies():
            copy.wait()
        rows = self.piece(self.place.coord[0])
        self.ref[rows] = self.ref[rows] + self.from_x[0] + self.from_x[1] + self.from_x[2]

    def plane_copies(self, axis):
        copies = []
        mine = self.place.coord[axis]
        rows = self.piece(self.place.coord[0])
        for distance in (1, 2, 3):
            slot = axis * 3 + distance
            copies.append(
                remote(
                    self.ref.at[rows],
                    self.from_plane.at[axis - 1, mine],
                    self.send.at[slot],
                    self.recv.at[slot],
                    self.place.peer(axis, distance),
                )
            )
        return copies

    def plane_start(self, axis):
        for copy in self.plane_copies(axis):
            copy.start()

    def plane_finish(self, axis):
        rows = self.piece(self.place.coord[0])
        self.from_plane[axis - 1, self.place.coord[axis]] = self.ref[rows]
        for copy in self.plane_copies(axis):
            copy.wait()
        terms = [self.from_plane[axis - 1, place] for place in range(4)]
        target = self.ref if axis == 1 else self.result
        target[rows] = (terms[0] + terms[1]) + (terms[2] + terms[3])

    def x_back_copies(self):
        copies = []
        rows = self.piece(self.place.coord[0])
        for distance in (1, 2, 3):
            copies.append(
                remote(
                    self.result.at[rows],
                    self.result.at[rows],
                    self.send.at[9 + distance],
                    self.recv.at[9 + distance],
                    self.place.peer(0, distance),
                )
            )
        return copies

    def x_back_start(self):
        for copy in self.x_back_copies():
            copy.start()

    def x_back_finish(self):
        for copy in self.x_back_copies():
            copy.wait()

    def share_copy(self):
        rows = pl.ds(pl.multiple_of(self.mine, 8), EXTRA_HALF)
        return remote(
            self.result.at[rows], self.result.at[rows], self.send.at[13], self.recv.at[13], self.place.sibling()
        )

    def share_start(self):
        self.share_copy().start()

    def share_finish(self):
        self.share_copy().wait()


ROWS = 512
SLOT = 256
KEYS = 768
GENES = 1024
GENE_ROWS = 480
PAIRS = 4
NEG = -1e30
SCORE_SCALE = 0.125
NN = (((1,), (0,)), ((), ()))
NT = (((1,), (1,)), ((), ()))
TN = (((0,), (0,)), ((), ()))


def dot(left, right, dims):
    return lax.dot_general(left, right, dims, preferred_element_type=jnp.float32)


def low(values):
    return values.astype(jnp.bfloat16)


def wide(values):
    return values.astype(jnp.float32)


def lane(shape):
    return lax.broadcasted_iota(jnp.int32, shape, 1)


def normalize(values):
    center = values - jnp.mean(values, axis=1, keepdims=True)
    root = lax.rsqrt(jnp.mean(center * center, axis=1, keepdims=True) + 1e-05)
    return center * root, root


def norm_back(grad, gain, normal, root):
    u = grad * gain
    mean = jnp.mean(u, axis=1, keepdims=True)
    along = jnp.mean(u * normal, axis=1, keepdims=True)
    return (u - mean - normal * along) * root


def column_sum(values):
    return jnp.sum(values, axis=0, keepdims=True)


def split_three(values):
    first = low(values)
    rest = values - wide(first)
    second = low(rest)
    third = low(rest - wide(second))
    return first, second, third


def model_kernel(
    hidden_in,
    cotangent,
    ids_in,
    unknown,
    table,
    w_inputs,
    w_output,
    w_up,
    w_down,
    b_query,
    b_value,
    b_output,
    gain_one,
    shift_one,
    b_up,
    b_down,
    gain_two,
    shift_two,
    layer_out,
    grad_hidden,
    reduced,
    extra_out,
    kept_probs,
    hidden,
    cot,
    ids,
    scale,
    win,
    wout,
    wup,
    wdown,
    stream,
    x_round,
    queries,
    keys,
    values,
    probs,
    stats,
    mixed,
    normal_one,
    normal_two,
    slope,
    active,
    d_first,
    d_mixed,
    d_packed,
    d_keys,
    d_values,
    part_keys,
    part_values,
    sent,
    received,
    bias,
    self_bias,
    vectors,
    out_round,
    extra,
    batch_a,
    batch_b,
    result_last,
    extra_result,
    load_sems,
    swap_send,
    swap_recv,
    kv_send,
    kv_recv,
    grad_send,
    grad_recv,
    probs_sem,
    out_sems,
    *reduction_refs,
):
    place = Place()
    core, here = place.core, place.x_hi
    there = 1 - here
    partner = place.peer(0, 2)
    sibling = place.sibling()

    def slot_rows(slot):
        return pl.ds(pl.multiple_of(slot * SLOT, SLOT), SLOT)

    def block_rows(slot, which):
        return pl.ds(pl.multiple_of((2 * slot + which) * SLOT, SLOT), SLOT)

    loads = [
        pltpu.make_async_copy(hidden_in.at[here], hidden.at[slot_rows(here)], load_sems.at[0]),
        pltpu.make_async_copy(cotangent.at[here], cot.at[slot_rows(here)], load_sems.at[1]),
    ]
    for layer in range(2):
        for index, (source, target) in enumerate(
            ((w_inputs, win), (w_output, wout), (w_up, wup), (w_down, wdown))
        ):
            loads.append(
                pltpu.make_async_copy(
                    source.at[layer], target.at[layer], load_sems.at[2 + 4 * layer + index]
                )
            )
    for load in loads:
        load.start()
    for cell in range(2):
        ids[cell] = jnp.broadcast_to(ids_in[cell : cell + 1, :], (8, SLOT))
    known = GENES - unknown[here]

    greet(place)

    swap_hidden = remote(
        hidden_in.at[there],
        hidden.at[slot_rows(here)],
        swap_send.at[0],
        swap_recv.at[0],
        partner,
    )
    swap_ids = remote(ids.at[there], ids.at[2], swap_send.at[1], swap_recv.at[1], partner)
    swap_cot = remote(
        cotangent.at[there],
        cot.at[slot_rows(here)],
        swap_send.at[2],
        swap_recv.at[2],
        partner,
    )
    swap_ids.start()
    swap_hidden.start()
    swap_cot.start()

    bias[...] = jnp.where(lane((8, KEYS)) < known, 0.0, NEG)
    for slot in range(2):
        position = (2 * slot + core) * SLOT + lax.broadcasted_iota(jnp.int32, (SLOT, 128), 0)
        self_bias[slot * SLOT : (slot + 1) * SLOT, :] = jnp.where(position >= known, 0.0, NEG)
    part_keys[KEYS:GENES, :] = jnp.zeros((GENES - KEYS, 128), jnp.float32)
    part_values[KEYS:GENES, :] = jnp.zeros((GENES - KEYS, 128), jnp.float32)
    vectors[...] = jnp.zeros_like(vectors)
    extra[...] = jnp.zeros_like(extra)

    def slot_ids(slot):
        row = jnp.where(slot == here, ids[here, 0:1, :], ids[2, 0:1, :])
        high = lax.shift_right_logical(row, 7)
        lowest = lax.bitwise_and(row, 127)
        is_high = lax.broadcasted_iota(jnp.int32, (GENE_ROWS, SLOT), 0) == high
        is_low = lax.broadcasted_iota(jnp.int32, (128, SLOT), 0) == lowest
        return low(jnp.where(is_high, 1.0, 0.0)), is_low

    def gather_scale(slot):
        is_high, is_low = slot_ids(slot)
        total = jnp.zeros((128, SLOT), jnp.float32)
        for piece in split_three(table[...]):
            total = total + dot(piece, is_high, TN)
        row = column_sum(jnp.where(is_low, total, 0.0))
        scale[slot_rows(slot), :] = jnp.transpose(jnp.broadcast_to(row, (128, SLOT)))

    def four(part):
        return jnp.concatenate([part] * 4, axis=1)

    def vector(ref, layer):
        return ref[layer : layer + 1, :]

    def kv_copies(layer, slot):
        rows = block_rows(slot, core)
        return [
            remote(
                ref.at[layer, rows],
                ref.at[layer, rows],
                kv_send.at[layer * 4 + slot * 2 + index],
                kv_recv.at[layer * 4 + slot * 2 + index],
                sibling,
            )
            for index, ref in enumerate((keys, values))
        ]

    def project(layer, slot):
        rows = slot_rows(slot)
        if layer == 0:
            stream[rows, :] = wide(hidden[rows, :]) * four(scale[rows, :])
        x_b = low(stream[rows, :])
        x_round[layer, rows, :] = x_b
        weights = win.at[layer]
        mine = block_rows(slot, core)
        keys[layer, mine, :] = low(dot(x_b, weights[:, 512:1024], NN))
        values[layer, mine, :] = low(
            dot(x_b, weights[:, 1024:1536], NN) + vector(b_value, layer)
        )
        for copy in kv_copies(layer, slot):
            copy.start()
        query = wide(low(dot(x_b, weights[:, 0:512], NN) + vector(b_query, layer)))
        queries[layer, rows, :] = low(query * SCORE_SCALE)

    def own(ref, layer, columns):
        return jnp.concatenate(
            [ref[layer, block_rows(slot, core), columns] for slot in range(2)], axis=0
        )

    def attend(layer):
        first_half = lane((ROWS, 128)) < 64

        def pair_step(pair, _):
            columns = pl.ds(pl.multiple_of(pair * 128, 128), 128)
            q_pair = queries[layer, :, columns]
            k_pair = keys[layer, 0:KEYS, columns]
            v_pair = values[layer, 0:KEYS, columns]
            k_own = own(keys, layer, columns)
            v_own = wide(own(values, layer, columns))
            product = wide(q_pair) * wide(k_own)
            found = []
            for half in range(2):
                inside = first_half if half == 0 else jnp.logical_not(first_half)
                self_score = (
                    jnp.sum(jnp.where(inside, product, 0.0), axis=1, keepdims=True)
                    + self_bias[:, 0:1]
                )
                scores = dot(jnp.where(inside, q_pair, jnp.zeros_like(q_pair)), k_pair, NT)
                scores = scores + bias[0:1, :]
                top = jnp.maximum(jnp.max(scores, axis=1, keepdims=True), self_score)
                exponent = jnp.exp(scores - top)
                self_exponent = jnp.exp(self_score - top)
                inverse = 1.0 / (jnp.sum(exponent, axis=1, keepdims=True) + self_exponent)
                rounded = low(exponent * inverse)
                self_prob = self_exponent * inverse
                probs[2 * pair + half] = rounded
                stats[layer] = jnp.where(
                    lane((ROWS, 128)) == 2 * pair + half, self_prob, stats[layer]
                )
                found.append(dot(rounded, v_pair, NN) + wide(low(self_prob)) * v_own)
            mixed[layer, :, columns] = jnp.where(first_half, found[0], found[1])
            return 0

        lax.fori_loop(0, PAIRS, pair_step, 0)

    def put_stat(layer, rows, index, column):
        stats[layer, rows, :] = jnp.where(lane((SLOT, 128)) == index, column, stats[layer, rows, :])

    def dense_forward(layer, slot):
        rows = slot_rows(slot)
        mixed_b = low(mixed[layer, rows, :])
        first = stream[rows, :] + (dot(mixed_b, wout[layer], NN) + vector(b_output, layer))
        normal, root = normalize(first)
        normal_one[layer, rows, :] = normal
        put_stat(layer, rows, 8, root)
        normed = normal * vector(gain_one, layer) + vector(shift_one, layer)
        inner = dot(low(normed), wup[layer], NN) + vector(b_up, layer)
        share = 0.5 * (1.0 + lax.erf(inner * 0.7071067811865476))
        slope[layer, rows, :] = share + inner * (
            0.3989422804014327 * jnp.exp(inner * inner * -0.5)
        )
        active_b = low(inner * share)
        active[layer, rows, :] = active_b
        second = normed + (dot(active_b, wdown[layer], NN) + vector(b_down, layer))
        normal, root = normalize(second)
        normal_two[layer, rows, :] = normal
        put_stat(layer, rows, 9, root)
        stream[rows, :] = normal * vector(gain_two, layer) + vector(shift_two, layer)

    def add_vector(member, layer, row):
        at = 2 * member + layer
        vectors[at : at + 1, :] = vectors[at : at + 1, :] + row

    def dense_backward(layer, slot):
        rows = slot_rows(slot)
        grad = stream[rows, :]
        normal = normal_two[layer, rows, :]
        add_vector(7, layer, column_sum(grad * normal))
        add_vector(8, layer, column_sum(grad))
        root = stats[layer, rows, :][:, 9:10]
        d_second = norm_back(grad, vector(gain_two, layer), normal, root)
        d_branch = low(d_second)
        d_packed[rows, 0:512] = d_branch
        add_vector(6, layer, column_sum(wide(d_branch)))
        d_inner = low(dot(d_branch, wdown[layer], NT) * slope[layer, rows, :])
        d_packed[rows, 512:1024] = d_inner
        add_vector(5, layer, column_sum(wide(d_inner)))
        d_normed = d_second + dot(d_inner, wup[layer], NT)
        normal = normal_one[layer, rows, :]
        add_vector(3, layer, column_sum(d_normed * normal))
        add_vector(4, layer, column_sum(d_normed))
        root = stats[layer, rows, :][:, 8:9]
        first = norm_back(d_normed, vector(gain_one, layer), normal, root)
        d_first[rows, :] = first
        d_attn = low(first)
        d_packed[rows, 1024:1536] = d_attn
        add_vector(2, layer, column_sum(wide(d_attn)))
        d_mixed[rows, :] = low(dot(d_attn, wout[layer], NT))

    def put_tiles(batch, first_tile, matrix):
        for tile in range(4):
            at = (first_tile + tile) * 512
            batch[at : at + 512, :] = low(matrix[:, tile * 128 : (tile + 1) * 128])

    def dense_weights(layer, batch):
        put_tiles(batch, 0, dot(active[layer], d_packed[:, 0:512], TN))
        normed = normal_one[layer] * vector(gain_one, layer) + vector(shift_one, layer)
        put_tiles(batch, 4, dot(low(normed), d_packed[:, 512:1024], TN))
        put_tiles(batch, 8, dot(low(mixed[layer]), d_packed[:, 1024:1536], TN))

    def grad_copy(layer, pair):
        return remote(
            sent.at[pair],
            received.at[layer, pair],
            grad_send.at[layer * PAIRS + pair],
            grad_recv.at[layer * PAIRS + pair],
            sibling,
        )

    def attend_backward(layer, first_pair, last_pair):
        first_half = lane((ROWS, 128)) < 64
        half_keys = lane((KEYS, 128)) < 64

        def pair_step(pair, _):
            columns = pl.ds(pl.multiple_of(pair * 128, 128), 128)
            q_pair = queries[layer, :, columns]
            k_pair = keys[layer, 0:KEYS, columns]
            v_pair = values[layer, 0:KEYS, columns]
            k_own = wide(own(keys, layer, columns))
            v_own = wide(own(values, layer, columns))
            d_out = d_mixed[:, columns]
            d_wide = wide(d_out)
            with_out = mixed[layer, :, columns] * d_wide
            with_own = v_own * d_wide
            d_q, d_k, d_v, self_score, self_prob = [], [], [], [], []
            for half in range(2):
                inside = first_half if half == 0 else jnp.logical_not(first_half)
                delta = jnp.sum(jnp.where(inside, with_out, 0.0), axis=1, keepdims=True)
                d_self = jnp.sum(jnp.where(inside, with_own, 0.0), axis=1, keepdims=True)
                mine = lane((ROWS, 128)) == 2 * pair + half
                prob = jnp.sum(jnp.where(mine, stats[layer], 0.0), axis=1, keepdims=True)
                d_probs = dot(jnp.where(inside, d_out, jnp.zeros_like(d_out)), v_pair, NT)
                rounded = probs[2 * pair + half]
                d_scores = low(wide(rounded) * (d_probs - delta))
                d_q.append(dot(d_scores, k_pair, NN))
                d_k.append(dot(d_scores, q_pair, TN))
                d_v.append(dot(rounded, d_out, TN))
                self_score.append(wide(low(prob * (d_self - delta))))
                self_prob.append(wide(low(prob)))
            own_score = jnp.where(first_half, self_score[0], self_score[1])
            own_prob = jnp.where(first_half, self_prob[0], self_prob[1])
            d_query = jnp.where(first_half, d_q[0], d_q[1]) + own_score * k_own
            d_packed[:, columns] = low(d_query * SCORE_SCALE)
            part_keys[0:KEYS, :] = jnp.where(half_keys, d_k[0], d_k[1])
            part_values[0:KEYS, :] = jnp.where(half_keys, d_v[0], d_v[1])
            own_keys = own_score * wide(q_pair)
            own_values = own_prob * d_wide
            for slot in range(2):
                rows = slice(slot * SLOT, (slot + 1) * SLOT)
                mine = block_rows(slot, core)
                d_keys[rows, columns] = part_keys[mine, :] + own_keys[rows, :]
                d_values[rows, columns] = part_values[mine, :] + own_values[rows, :]
                other = block_rows(slot, 1 - core)
                sent[pair, 0, rows, :] = low(part_keys[other, :])
                sent[pair, 1, rows, :] = low(part_values[other, :])
            grad_copy(layer, pair).start()
            return 0

        lax.fori_loop(first_pair, last_pair, pair_step, 0)

    def merge_grads(layer):
        def pair_step(pair, _):
            grad_copy(layer, pair).wait()
            columns = pl.ds(pl.multiple_of(pair * 128, 128), 128)
            k_columns = pl.ds(pl.multiple_of(512 + pair * 128, 128), 128)
            v_columns = pl.ds(pl.multiple_of(1024 + pair * 128, 128), 128)
            d_packed[:, k_columns] = low(d_keys[:, columns] + wide(received[layer, pair, 0]))
            d_packed[:, v_columns] = low(d_values[:, columns] + wide(received[layer, pair, 1]))
            return 0

        lax.fori_loop(0, PAIRS, pair_step, 0)

    def input_weights(layer, batch):
        for third in range(3):
            put_tiles(
                batch,
                4 * third,
                dot(x_round[layer], d_packed[:, third * 512 : (third + 1) * 512], TN),
            )
        add_vector(0, layer, column_sum(wide(d_packed[:, 0:512])))
        add_vector(1, layer, column_sum(wide(d_packed[:, 1024:1536])))

    def input_grad(layer, slot):
        rows = slot_rows(slot)
        stream[rows, :] = d_first[rows, :] + dot(d_packed[rows, :], win[layer], NT)

    def reduction(index, batch, result):
        from_core, s0, s1, s2, a, b, c, d = reduction_refs[index * 8 : index * 8 + 8]
        return Reduction(place, batch, result, from_core, (s0, s1, s2), (a, b, c, d))

    one_a = reduction(0, batch_a, reduced.at[0])
    one_b = reduction(1, batch_b, reduced.at[1])
    zero_a = reduction(2, batch_a, reduced.at[2])
    zero_b = reduction(3, batch_b, result_last)
    from_core, from_x, from_plane, a, b = reduction_refs[32:]
    more = ExtraReduction(place, extra, extra_result, from_core, from_x, from_plane, (a, b))

    loads[0].wait()
    gather_scale(here)
    loads[2].wait()
    project(0, here)
    swap_ids.wait()
    gather_scale(there)
    swap_hidden.wait()
    project(0, there)
    probs_out = pltpu.make_async_copy(probs, kept_probs, probs_sem.at[0])
    probs_back = pltpu.make_async_copy(kept_probs, probs, probs_sem.at[1])
    for layer in range(2):
        for slot in range(2):
            for copy in kv_copies(layer, slot):
                copy.wait()
        if layer == 1:
            probs_out.wait()
        attend(layer)
        if layer == 0:
            probs_out.start()
        for load in loads[3 + 4 * layer : 6 + 4 * layer]:
            load.wait()
        for slot in range(2):
            dense_forward(layer, slot)
        if layer == 0:
            loads[6].wait()
            for slot in range(2):
                project(1, slot)

    out_round[...] = low(stream[...])
    keep_out = pltpu.make_async_copy(
        out_round.at[slot_rows(here)], layer_out.at[here], out_sems.at[0]
    )
    send_out = remote(
        out_round.at[slot_rows(there)],
        layer_out.at[here],
        swap_send.at[3],
        swap_recv.at[3],
        partner,
    )
    keep_out.start()
    send_out.start()

    loads[1].wait()
    swap_cot.wait()
    stream[...] = wide(cot[...])
    for slot in range(2):
        dense_backward(1, slot)
    dense_weights(1, batch_a)
    one_a.core_start()
    attend_backward(1, 0, 2)
    one_a.core_finish()
    one_a.scatter_start(0)
    attend_backward(1, 2, 4)
    probs_back.start()
    one_a.scatter_finish(0)
    one_a.scatter_start(1)
    merge_grads(1)
    input_weights(1, batch_b)
    one_b.core_start()
    one_a.scatter_finish(1)
    one_a.scatter_start(2)
    for slot in range(2):
        input_grad(1, slot)
    one_a.scatter_finish(2)
    one_a.gather_start(2)
    one_b.core_finish()
    one_b.scatter_start(0)

    dense_backward(0, 0)
    one_a.gather_finish(2)
    one_a.gather_start(1)
    dense_backward(0, 1)
    one_b.scatter_finish(0)
    one_b.scatter_start(1)
    dense_weights(0, batch_a)
    zero_a.core_start()
    one_a.gather_finish(1)
    one_a.gather_start(0)
    one_b.scatter_finish(1)
    one_b.scatter_start(2)
    probs_back.wait()
    attend_backward(0, 0, 2)
    zero_a.core_finish()
    zero_a.scatter_start(0)
    one_b.scatter_finish(2)
    one_b.gather_start(2)
    one_a.gather_finish(0)
    one_a.share_start()
    attend_backward(0, 2, 4)
    zero_a.scatter_finish(0)
    zero_a.scatter_start(1)
    one_b.gather_finish(2)
    one_b.gather_start(1)
    merge_grads(0)
    input_weights(0, batch_b)
    zero_b.core_start()
    zero_a.scatter_finish(1)
    zero_a.scatter_start(2)
    for slot in range(2):
        input_grad(0, slot)
    zero_b.core_finish()
    zero_b.scatter_start(0)

    genes = jnp.zeros((GENE_ROWS, 128), jnp.float32)
    for slot in range(2):
        rows = slot_rows(slot)
        is_high, is_low = slot_ids(slot)
        per_token = jnp.sum(stream[rows, :] * wide(hidden[rows, :]), axis=1, keepdims=True)
        row = jnp.transpose(jnp.broadcast_to(per_token, (SLOT, 128)))
        for piece in split_three(jnp.where(is_low, row, 0.0)):
            genes = genes + dot(is_high, piece, NT)
    extra[0:GENE_ROWS, :] = genes
    for index in range(18):
        for tile in range(4):
            at = GENE_ROWS + 4 * index + tile
            extra[at : at + 1, :] = vectors[index : index + 1, tile * 128 : (tile + 1) * 128]
    more.core_start()

    for slot in range(2):
        rows = slot_rows(slot)
        d_mixed[rows, :] = low(stream[rows, :] * four(scale[rows, :]))
    keep_grad = pltpu.make_async_copy(
        d_mixed.at[slot_rows(here)], grad_hidden.at[here], out_sems.at[1]
    )
    send_grad = remote(
        d_mixed.at[slot_rows(there)],
        grad_hidden.at[here],
        swap_send.at[4],
        swap_recv.at[4],
        partner,
    )
    more.core_finish()
    more.x_start()
    keep_grad.start()

    zero_b.scatter_finish(0)
    zero_b.scatter_start(1)
    zero_a.scatter_finish(2)
    zero_a.gather_start(2)
    one_b.gather_finish(1)
    one_b.gather_start(0)
    more.x_finish()
    more.plane_start(1)
    send_grad.start()
    zero_b.scatter_finish(1)
    zero_b.scatter_start(2)
    zero_a.gather_finish(2)
    zero_a.gather_start(1)
    more.plane_finish(1)
    more.plane_start(2)
    zero_b.scatter_finish(2)
    zero_b.gather_start(2)
    more.plane_finish(2)
    more.x_back_start()
    one_b.gather_finish(0)
    one_b.share_start()
    zero_a.gather_finish(1)
    zero_a.gather_start(0)
    zero_b.gather_finish(2)
    zero_b.gather_start(1)
    more.x_back_finish()
    more.share_start()
    zero_b.gather_finish(1)
    zero_b.gather_start(0)
    zero_a.gather_finish(0)
    zero_a.share_start()
    more.share_finish()
    extra_copy = pltpu.make_async_copy(extra_result, extra_out, out_sems.at[2])
    extra_copy.start()
    zero_b.gather_finish(0)
    zero_b.share_start()
    one_a.share_finish()
    one_b.share_finish()
    zero_a.share_finish()
    zero_b.share_finish()
    last_copy = pltpu.make_async_copy(result_last, reduced.at[3], out_sems.at[3])
    last_copy.start()
    keep_out.wait()
    send_out.wait()
    keep_grad.wait()
    send_grad.wait()
    extra_copy.wait()
    last_copy.wait()


def reduction_scratch():
    return [
        pltpu.VMEM((HALF_ROWS, 128), jnp.bfloat16),
        pltpu.VMEM((3, 3, STEP_ROWS[0], 128), jnp.bfloat16),
        pltpu.VMEM((3, 3, STEP_ROWS[1], 128), jnp.bfloat16),
        pltpu.VMEM((3, 3, STEP_ROWS[2], 128), jnp.bfloat16),
        pltpu.SemaphoreType.DMA((2,)),
        pltpu.SemaphoreType.DMA((2,)),
        pltpu.SemaphoreType.DMA((57,)),
        pltpu.SemaphoreType.DMA((54,)),
    ]


def extra_scratch():
    return [
        pltpu.VMEM((EXTRA_HALF, 128), jnp.float32),
        pltpu.VMEM((3, EXTRA_PIECE, 128), jnp.float32),
        pltpu.VMEM((2, 4, EXTRA_PIECE, 128), jnp.float32),
        pltpu.SemaphoreType.DMA((14,)),
        pltpu.SemaphoreType.DMA((14,)),
    ]


def run_model(hidden_in, cotangent, gene_ids, unknown_count, table, weights, vector_args):
    f32, bf16 = jnp.float32, jnp.bfloat16
    vmem = pl.BlockSpec(memory_space=pltpu.VMEM)
    smem = pl.BlockSpec(memory_space=pltpu.SMEM)
    anywhere = pl.BlockSpec(memory_space=pl.ANY)
    scratch = [
        pltpu.VMEM((ROWS, 512), bf16),
        pltpu.VMEM((ROWS, 512), bf16),
        pltpu.VMEM((3, 8, SLOT), jnp.int32),
        pltpu.VMEM((ROWS, 128), f32),
        pltpu.VMEM((2, 512, 1536), bf16),
        pltpu.VMEM((2, 512, 512), bf16),
        pltpu.VMEM((2, 512, 512), bf16),
        pltpu.VMEM((2, 512, 512), bf16),
        pltpu.VMEM((ROWS, 512), f32),
        pltpu.VMEM((2, ROWS, 512), bf16),
        pltpu.VMEM((2, ROWS, 512), bf16),
        pltpu.VMEM((2, GENES, 512), bf16),
        pltpu.VMEM((2, GENES, 512), bf16),
        pltpu.VMEM((HEADS, ROWS, KEYS), bf16),
        pltpu.VMEM((2, ROWS, 128), f32),
        pltpu.VMEM((2, ROWS, 512), f32),
        pltpu.VMEM((2, ROWS, 512), f32),
        pltpu.VMEM((2, ROWS, 512), f32),
        pltpu.VMEM((2, ROWS, 512), f32),
        pltpu.VMEM((2, ROWS, 512), bf16),
        pltpu.VMEM((ROWS, 512), f32),
        pltpu.VMEM((ROWS, 512), bf16),
        pltpu.VMEM((ROWS, 1536), bf16),
        pltpu.VMEM((ROWS, 512), f32),
        pltpu.VMEM((ROWS, 512), f32),
        pltpu.VMEM((GENES, 128), f32),
        pltpu.VMEM((GENES, 128), f32),
        pltpu.VMEM((PAIRS, 2, ROWS, 128), bf16),
        pltpu.VMEM((2, PAIRS, 2, ROWS, 128), bf16),
        pltpu.VMEM((8, KEYS), f32),
        pltpu.VMEM((ROWS, 128), f32),
        pltpu.VMEM((24, 512), f32),
        pltpu.VMEM((ROWS, 512), bf16),
        pltpu.VMEM((EXTRA_ROWS, 128), f32),
        pltpu.VMEM((BATCH_ROWS, 128), bf16),
        pltpu.VMEM((BATCH_ROWS, 128), bf16),
        pltpu.VMEM((BATCH_ROWS, 128), bf16),
        pltpu.VMEM((EXTRA_ROWS, 128), f32),
        pltpu.SemaphoreType.DMA((10,)),
        pltpu.SemaphoreType.DMA((5,)),
        pltpu.SemaphoreType.DMA((5,)),
        pltpu.SemaphoreType.DMA((8,)),
        pltpu.SemaphoreType.DMA((8,)),
        pltpu.SemaphoreType.DMA((8,)),
        pltpu.SemaphoreType.DMA((8,)),
        pltpu.SemaphoreType.DMA((2,)),
        pltpu.SemaphoreType.DMA((4,)),
    ]
    for _ in range(4):
        scratch += reduction_scratch()
    scratch += extra_scratch()
    outs = (
        jax.ShapeDtypeStruct((2, SLOT, 512), bf16),
        jax.ShapeDtypeStruct((2, SLOT, 512), bf16),
        jax.ShapeDtypeStruct((4, BATCH_ROWS, 128), bf16),
        jax.ShapeDtypeStruct((EXTRA_ROWS, 128), f32),
        jax.ShapeDtypeStruct((HEADS, ROWS, KEYS), bf16),
    )
    return pl.pallas_call(
        model_kernel,
        out_shape=outs,
        in_specs=[anywhere, anywhere, vmem, smem, vmem] + [anywhere] * 4 + [vmem] * 9,
        out_specs=(anywhere,) * 5,
        scratch_shapes=scratch,
        compiler_params=pltpu.CompilerParams(
            collective_id=0, has_side_effects=True, vmem_limit_bytes=63 << 20
        ),
        name="model",
    )(hidden_in, cotangent, gene_ids, unknown_count, table, *weights, *vector_args)


def finish_kernel(layer_in, hidden_grad_in, reduced, extra, *refs):
    layer_out, hidden_out, g_inputs, g_output, g_up, g_down, genes = refs[:7]
    vector_outs = refs[7:16]
    rounded, narrow, rows_out, wide_in, wide_rest, in_sems, out_sems = refs[16:]
    sources = [layer_in, hidden_grad_in]
    loads = [
        pltpu.make_async_copy(sources[i], rounded.at[i], in_sems.at[i]) for i in range(2)
    ] + [pltpu.make_async_copy(reduced.at[i], narrow.at[i], in_sems.at[2 + i]) for i in range(4)]
    for load in loads:
        load.start()
    genes[...] = extra[0:GENE_ROWS, :]
    for member in range(9):
        for layer in range(2):
            for tile in range(4):
                at = GENE_ROWS + 4 * (2 * member + layer) + tile
                vector_outs[member][layer : layer + 1, tile * 128 : (tile + 1) * 128] = extra[
                    at : at + 1, :
                ]
    stores = []

    def send(source, target):
        store = pltpu.make_async_copy(source, target, out_sems.at[len(stores)])
        store.start()
        stores.append(store)

    for index, target in enumerate((layer_out, hidden_out)):
        loads[index].wait()
        rows_out[index] = wide(rounded[index])
        send(rows_out.at[index], target)
    for layer in (1, 0):
        base = 2 * (1 - layer)
        loads[2 + base].wait()
        for index, target in enumerate((g_down, g_up, g_output)):
            for tile in range(4):
                at = (4 * index + tile) * 512
                wide_rest[layer, index, :, tile * 128 : (tile + 1) * 128] = wide(
                    narrow[base, at : at + 512, :]
                )
            send(wide_rest.at[layer, index], target.at[layer])
        loads[3 + base].wait()
        for tile in range(12):
            at = tile * 512
            wide_in[layer, :, tile * 128 : (tile + 1) * 128] = wide(
                narrow[base + 1, at : at + 512, :]
            )
        send(wide_in.at[layer], g_inputs.at[layer])
    for store in stores:
        store.wait()


def finish(layer_out, grad_hidden, reduced, extra):
    f32, bf16 = jnp.float32, jnp.bfloat16
    vmem = pl.BlockSpec(memory_space=pltpu.VMEM)
    anywhere = pl.BlockSpec(memory_space=pl.ANY)
    outs = [
        jax.ShapeDtypeStruct((2, SLOT, 512), f32),
        jax.ShapeDtypeStruct((2, SLOT, 512), f32),
        jax.ShapeDtypeStruct((2, 512, 1536), f32),
        jax.ShapeDtypeStruct((2, 512, 512), f32),
        jax.ShapeDtypeStruct((2, 512, 512), f32),
        jax.ShapeDtypeStruct((2, 512, 512), f32),
        jax.ShapeDtypeStruct((GENE_ROWS, 128), f32),
    ] + [jax.ShapeDtypeStruct((2, 512), f32)] * 9
    return pl.pallas_call(
        finish_kernel,
        out_shape=outs,
        in_specs=[anywhere, anywhere, anywhere, vmem],
        out_specs=[anywhere] * 6 + [vmem] * 10,
        scratch_shapes=[
            pltpu.VMEM((2, 2, SLOT, 512), bf16),
            pltpu.VMEM((4, BATCH_ROWS, 128), bf16),
            pltpu.VMEM((2, 2, SLOT, 512), f32),
            pltpu.VMEM((2, 512, 1536), f32),
            pltpu.VMEM((2, 3, 512, 512), f32),
            pltpu.SemaphoreType.DMA((6,)),
            pltpu.SemaphoreType.DMA((10,)),
        ],
        compiler_params=pltpu.CompilerParams(vmem_limit_bytes=48 << 20),
        name="finish",
    )(layer_out, grad_hidden, reduced, extra)


def shards(
    hidden_in,
    gene_ids,
    unknown_count,
    gene_scale,
    w_inputs,
    b_query,
    b_value,
    w_output,
    b_output,
    gain_one,
    shift_one,
    w_up,
    b_up,
    w_down,
    b_down,
    gain_two,
    shift_two,
    cotangent,
):
    gene_count = gene_scale.shape[0]
    table = jnp.pad(gene_scale, (0, GENE_ROWS * 128 - gene_count)).reshape(GENE_ROWS, 128)
    layer_out, grad_hidden, reduced, extra, _ = run_model(
        hidden_in,
        cotangent,
        gene_ids,
        unknown_count,
        table,
        (w_inputs, w_output, w_up, w_down),
        (b_query, b_value, b_output, gain_one, shift_one, b_up, b_down, gain_two, shift_two),
    )
    (
        layer_out,
        grad_hidden,
        g_inputs,
        g_output,
        g_up,
        g_down,
        genes,
        g_b_query,
        g_b_value,
        g_b_output,
        g_gain_one,
        g_shift_one,
        g_b_up,
        g_b_down,
        g_gain_two,
        g_shift_two,
    ) = finish(layer_out, grad_hidden, reduced, extra)
    return (
        layer_out,
        grad_hidden,
        genes.reshape(-1)[:gene_count],
        g_inputs,
        g_b_query,
        g_b_value,
        g_output,
        g_b_output,
        g_gain_one,
        g_shift_one,
        g_up,
        g_b_up,
        g_down,
        g_b_down,
        g_gain_two,
        g_shift_two,
    )


def solution(mesh):
    placed = (
        P("dp", "blk", None),
        P("dp", "blk"),
        P("dp"),
        P(),
        P(),
        P(),
        P(),
        P(),
        P(),
        P(),
        P(),
        P(),
        P(),
        P(),
        P(),
        P(),
        P(),
        P("dp", "blk", None),
    )
    return jax.shard_map(
        shards,
        mesh=mesh,
        in_specs=placed,
        out_specs=(
            P("dp", "blk", None),
            P("dp", "blk", None),
            P(),
            P(),
            P(),
            P(),
            P(),
            P(),
            P(),
            P(),
            P(),
            P(),
            P(),
            P(),
            P(),
            P(),
        ),
        check_vma=False,
    )
```

```python
import jax
import jax.numpy as jnp
from jax import lax
from jax.experimental import pallas as pl
from jax.experimental.pallas import tpu as pltpu
from jax.sharding import PartitionSpec as P

HEADS = 8
MESH = pl.DeviceIdType.MESH
AXIS_ORDER = ((0, 1, 2), (1, 2, 0), (2, 0, 1))
PART_ROWS = 1024
HALF_ROWS = 3 * PART_ROWS
BATCH_ROWS = 2 * HALF_ROWS
STEP_ROWS = (256, 64)
EXTRA_ROWS = 576
EXTRA_HALF = EXTRA_ROWS // 2
EXTRA_PIECE = EXTRA_HALF // 4


class Place:
    def __init__(self):
        dp = lax.axis_index("dp")
        blk = lax.axis_index("blk")
        self.y = dp // 8
        self.z = (dp // 2) % 4
        self.x_lo = dp % 2
        self.x_hi = blk // 2
        self.core = blk % 2
        self.coord = (self.x_hi * 2 + self.x_lo, self.y, self.z)

    def device(self, coord, core):
        x, y, z = coord
        return ((y * 4 + z) * 2 + x % 2, (x // 2) * 2 + core)

    def sibling(self):
        return self.device(self.coord, 1 - self.core)

    def peer(self, axis, distance):
        coord = list(self.coord)
        coord[axis] = (coord[axis] + distance) % 4
        return self.device(coord, self.core)


def greet(place):
    barrier = pltpu.get_barrier_semaphore()
    others = [place.sibling()]
    for axis in range(3):
        for distance in (1, 2, 3):
            others.append(place.peer(axis, distance))
    for other in others:
        pl.semaphore_signal(barrier, inc=1, device_id=other, device_id_type=MESH)
    pl.semaphore_wait(barrier, len(others))


def remote(src, dst, send_sem, recv_sem, device):
    return pltpu.make_async_remote_copy(
        src_ref=src,
        dst_ref=dst,
        send_sem=send_sem,
        recv_sem=recv_sem,
        device_id=device,
        device_id_type=MESH,
    )


class Reduction:
    def __init__(self, place, batch, result, from_core, from_step, sems):
        self.place = place
        self.batch = batch
        self.result = result
        self.from_core = from_core
        self.from_step = from_step
        self.core_send, self.core_recv, self.step_send, self.step_recv = sems
        self.mine = place.core * HALF_ROWS
        self.other = (1 - place.core) * HALF_ROWS

    def offset(self, part, steps):
        rows = self.mine + part * PART_ROWS
        for step in range(steps):
            rows = rows + self.place.coord[AXIS_ORDER[part][step]] * STEP_ROWS[step]
        return pl.multiple_of(rows, 16)

    def core_copy(self):
        rows = pl.ds(pl.multiple_of(self.other, 16), HALF_ROWS)
        return remote(
            self.batch.at[rows],
            self.from_core,
            self.core_send.at[0],
            self.core_recv.at[0],
            self.place.sibling(),
        )

    def core_start(self):
        self.core_copy().start()

    def core_finish(self):
        self.core_copy().wait()
        size = STEP_ROWS[0]

        def add(i, _):
            here = pl.ds(pl.multiple_of(self.mine + i * size, 16), size)
            there = pl.ds(pl.multiple_of(i * size, 16), size)
            self.batch[here] = (
                self.batch[here].astype(jnp.float32) + self.from_core[there].astype(jnp.float32)
            ).astype(jnp.bfloat16)
            return 0

        lax.fori_loop(0, HALF_ROWS // size, add, 0)

    def slot(self, step, part, distance):
        return (step * 3 + part) * 3 + distance - 1

    def scatter_copies(self, step):
        size = STEP_ROWS[step]
        copies = []
        for part in range(3):
            axis = AXIS_ORDER[part][step]
            base = self.offset(part, step)
            for distance in (1, 2, 3):
                target = (self.place.coord[axis] + distance) % 4
                rows = pl.ds(pl.multiple_of(base + target * size, 16), size)
                slot = self.slot(step, part, distance)
                copies.append(
                    remote(
                        self.batch.at[rows],
                        self.from_step[step].at[part, distance - 1],
                        self.step_send.at[slot],
                        self.step_recv.at[slot],
                        self.place.peer(axis, distance),
                    )
                )
        return copies

    def scatter_start(self, step):
        for copy in self.scatter_copies(step):
            copy.start()

    def scatter_finish(self, step):
        for copy in self.scatter_copies(step):
            copy.wait()
        size = STEP_ROWS[step]
        for part in range(3):
            rows = pl.ds(self.offset(part, step + 1), size)
            total = self.batch[rows].astype(jnp.float32)
            for distance in (1, 2, 3):
                total = total + self.from_step[step][part, distance - 1].astype(jnp.float32)
            self.batch[rows] = total.astype(jnp.bfloat16)

    def exchange_copies(self):
        copies = []
        for part in range(3):
            axis = AXIS_ORDER[part][2]
            mine = self.place.coord[axis]
            rows = pl.ds(self.offset(part, 2), STEP_ROWS[1])
            for distance in (1, 2, 3):
                slot = self.slot(2, part, distance)
                copies.append(
                    remote(
                        self.batch.at[rows],
                        self.from_step[2].at[part, mine],
                        self.step_send.at[slot],
                        self.step_recv.at[slot],
                        self.place.peer(axis, distance),
                    )
                )
        return copies

    def exchange_start(self):
        for copy in self.exchange_copies():
            copy.start()

    def exchange_finish(self):
        for part in range(3):
            mine = self.place.coord[AXIS_ORDER[part][2]]
            rows = pl.ds(self.offset(part, 2), STEP_ROWS[1])
            self.from_step[2][part, mine] = self.batch[rows]
        for copy in self.exchange_copies():
            copy.wait()
        for part in range(3):
            rows = pl.ds(self.offset(part, 2), STEP_ROWS[1])
            terms = [self.from_step[2][part, place].astype(jnp.float32) for place in range(4)]
            self.batch[rows] = ((terms[0] + terms[1]) + (terms[2] + terms[3])).astype(jnp.bfloat16)

    def gather_copies(self, step):
        size = STEP_ROWS[step]
        copies = []
        for part in range(3):
            axis = AXIS_ORDER[part][step]
            rows = pl.ds(self.offset(part, step + 1), size)
            for distance in (1, 2, 3):
                slot = 27 + self.slot(step, part, distance)
                copies.append(
                    remote(
                        (self.batch if step == 1 else self.result).at[rows],
                        self.result.at[rows],
                        self.step_send.at[slot],
                        self.step_recv.at[slot],
                        self.place.peer(axis, distance),
                    )
                )
            if step == 1:
                copies.append(
                    pltpu.make_async_copy(
                        self.batch.at[rows], self.result.at[rows], self.step_send.at[45 + part]
                    )
                )
        return copies

    def gather_start(self, step):
        for copy in self.gather_copies(step):
            copy.start()

    def gather_finish(self, step):
        for copy in self.gather_copies(step):
            copy.wait()

    def share_copy(self):
        rows = pl.ds(pl.multiple_of(self.mine, 16), HALF_ROWS)
        return remote(
            self.result.at[rows],
            self.result.at[rows],
            self.core_send.at[1],
            self.core_recv.at[1],
            self.place.sibling(),
        )

    def share_start(self):
        self.share_copy().start()

    def share_finish(self):
        self.share_copy().wait()


class ExtraReduction:
    def __init__(self, place, rows_ref, result, from_core, from_x, from_plane, sems):
        self.place = place
        self.ref = rows_ref
        self.result = result
        self.from_core = from_core
        self.from_x = from_x
        self.from_plane = from_plane
        self.send, self.recv = sems
        self.mine = place.core * EXTRA_HALF
        self.other = (1 - place.core) * EXTRA_HALF

    def piece(self, quarter):
        return pl.ds(pl.multiple_of(self.mine + quarter * EXTRA_PIECE, 8), EXTRA_PIECE)

    def core_copy(self):
        rows = pl.ds(pl.multiple_of(self.other, 8), EXTRA_HALF)
        return remote(
            self.ref.at[rows], self.from_core, self.send.at[0], self.recv.at[0], self.place.sibling()
        )

    def core_start(self):
        self.core_copy().start()

    def core_finish(self):
        self.core_copy().wait()
        rows = pl.ds(pl.multiple_of(self.mine, 8), EXTRA_HALF)
        self.ref[rows] = self.ref[rows] + self.from_core[...]

    def x_copies(self):
        copies = []
        for distance in (1, 2, 3):
            target = (self.place.coord[0] + distance) % 4
            copies.append(
                remote(
                    self.ref.at[self.piece(target)],
                    self.from_x.at[distance - 1],
                    self.send.at[distance],
                    self.recv.at[distance],
                    self.place.peer(0, distance),
                )
            )
        return copies

    def x_start(self):
        for copy in self.x_copies():
            copy.start()

    def x_finish(self):
        for copy in self.x_copies():
            copy.wait()
        rows = self.piece(self.place.coord[0])
        self.ref[rows] = self.ref[rows] + self.from_x[0] + self.from_x[1] + self.from_x[2]

    def plane_copies(self, axis):
        copies = []
        mine = self.place.coord[axis]
        rows = self.piece(self.place.coord[0])
        for distance in (1, 2, 3):
            slot = axis * 3 + distance
            copies.append(
                remote(
                    self.ref.at[rows],
                    self.from_plane.at[axis - 1, mine],
                    self.send.at[slot],
                    self.recv.at[slot],
                    self.place.peer(axis, distance),
                )
            )
        return copies

    def plane_start(self, axis):
        for copy in self.plane_copies(axis):
            copy.start()

    def plane_finish(self, axis):
        rows = self.piece(self.place.coord[0])
        self.from_plane[axis - 1, self.place.coord[axis]] = self.ref[rows]
        for copy in self.plane_copies(axis):
            copy.wait()
        terms = [self.from_plane[axis - 1, place] for place in range(4)]
        target = self.ref if axis == 1 else self.result
        target[rows] = (terms[0] + terms[1]) + (terms[2] + terms[3])

    def x_back_copies(self):
        copies = []
        rows = self.piece(self.place.coord[0])
        for distance in (1, 2, 3):
            copies.append(
                remote(
                    self.result.at[rows],
                    self.result.at[rows],
                    self.send.at[9 + distance],
                    self.recv.at[9 + distance],
                    self.place.peer(0, distance),
                )
            )
        return copies

    def x_back_start(self):
        for copy in self.x_back_copies():
            copy.start()

    def x_back_finish(self):
        for copy in self.x_back_copies():
            copy.wait()

    def share_copy(self):
        rows = pl.ds(pl.multiple_of(self.mine, 8), EXTRA_HALF)
        return remote(
            self.result.at[rows], self.result.at[rows], self.send.at[13], self.recv.at[13], self.place.sibling()
        )

    def share_start(self):
        self.share_copy().start()

    def share_finish(self):
        self.share_copy().wait()


ROWS = 512
SLOT = 256
KEYS = 768
GENES = 1024
GENE_ROWS = 480
PAIRS = 4
NEG = -1e30
SCORE_SCALE = 0.125
NN = (((1,), (0,)), ((), ()))
NT = (((1,), (1,)), ((), ()))
TN = (((0,), (0,)), ((), ()))


def dot(left, right, dims):
    return lax.dot_general(left, right, dims, preferred_element_type=jnp.float32)


def low(values):
    return values.astype(jnp.bfloat16)


def wide(values):
    return values.astype(jnp.float32)


def lane(shape):
    return lax.broadcasted_iota(jnp.int32, shape, 1)


def normalize(values):
    center = values - jnp.mean(values, axis=1, keepdims=True)
    root = lax.rsqrt(jnp.mean(center * center, axis=1, keepdims=True) + 1e-05)
    return center * root, root


def norm_back(grad, gain, normal, root):
    u = grad * gain
    mean = jnp.mean(u, axis=1, keepdims=True)
    along = jnp.mean(u * normal, axis=1, keepdims=True)
    return (u - mean - normal * along) * root


def column_sum(values):
    return jnp.sum(values, axis=0, keepdims=True)


def split_three(values):
    first = low(values)
    rest = values - wide(first)
    second = low(rest)
    third = low(rest - wide(second))
    return first, second, third


def model_kernel(
    hidden_in,
    cotangent,
    ids_in,
    unknown,
    table,
    w_inputs,
    w_output,
    w_up,
    w_down,
    b_query,
    b_value,
    b_output,
    gain_one,
    shift_one,
    b_up,
    b_down,
    gain_two,
    shift_two,
    layer_out,
    grad_hidden,
    reduced,
    extra_out,
    kept_probs,
    hidden,
    cot,
    ids,
    scale,
    win,
    wout,
    wup,
    wdown,
    stream,
    x_round,
    queries,
    keys,
    values,
    probs,
    stats,
    inverses,
    self_parts,
    mixed,
    normal_one,
    normal_two,
    slope,
    active,
    d_first,
    d_mixed,
    d_packed,
    d_keys,
    d_values,
    part_keys,
    part_values,
    sent,
    received,
    bias,
    self_bias,
    vectors,
    out_round,
    extra,
    batch_a,
    batch_b,
    batch_c,
    result_last,
    extra_result,
    load_sems,
    swap_send,
    swap_recv,
    kv_send,
    kv_recv,
    grad_send,
    grad_recv,
    probs_sem,
    out_sems,
    *reduction_refs,
):
    place = Place()
    core, here = place.core, place.x_hi
    there = 1 - here
    partner = place.peer(0, 2)
    sibling = place.sibling()

    def slot_rows(slot):
        return pl.ds(pl.multiple_of(slot * SLOT, SLOT), SLOT)

    def block_rows(slot, which):
        return pl.ds(pl.multiple_of((2 * slot + which) * SLOT, SLOT), SLOT)

    loads = [
        pltpu.make_async_copy(hidden_in.at[here], hidden.at[slot_rows(here)], load_sems.at[0]),
        pltpu.make_async_copy(cotangent.at[here], cot.at[slot_rows(here)], load_sems.at[1]),
    ]
    for layer in range(2):
        for index, (source, target) in enumerate(
            ((w_inputs, win), (w_output, wout), (w_up, wup), (w_down, wdown))
        ):
            loads.append(
                pltpu.make_async_copy(
                    source.at[layer], target.at[layer], load_sems.at[2 + 4 * layer + index]
                )
            )
    for load in loads[:1] + loads[2:6]:
        load.start()
    for cell in range(2):
        ids[cell] = jnp.broadcast_to(ids_in[cell : cell + 1, :], (8, SLOT))
    known = GENES - unknown[here]

    greet(place)

    swap_hidden = remote(
        hidden_in.at[there],
        hidden.at[slot_rows(here)],
        swap_send.at[0],
        swap_recv.at[0],
        partner,
    )
    swap_ids = remote(ids.at[there], ids.at[2], swap_send.at[1], swap_recv.at[1], partner)
    swap_cot = remote(
        cotangent.at[there],
        cot.at[slot_rows(here)],
        swap_send.at[2],
        swap_recv.at[2],
        partner,
    )
    swap_ids.start()
    swap_hidden.start()

    bias[...] = jnp.where(lane((8, KEYS)) < known, 0.0, NEG)
    for slot in range(2):
        position = (2 * slot + core) * SLOT + lax.broadcasted_iota(jnp.int32, (SLOT, 128), 0)
        self_bias[slot * SLOT : (slot + 1) * SLOT, :] = jnp.where(position >= known, 0.0, NEG)
    part_keys[KEYS:GENES, :] = jnp.zeros((GENES - KEYS, 128), jnp.float32)
    part_values[KEYS:GENES, :] = jnp.zeros((GENES - KEYS, 128), jnp.float32)
    vectors[...] = jnp.zeros_like(vectors)
    extra[...] = jnp.zeros_like(extra)

    def slot_ids(slot):
        row = jnp.where(slot == here, ids[here, 0:1, :], ids[2, 0:1, :])
        high = lax.shift_right_logical(row, 7)
        lowest = lax.bitwise_and(row, 127)
        is_high = lax.broadcasted_iota(jnp.int32, (GENE_ROWS, SLOT), 0) == high
        is_low = lax.broadcasted_iota(jnp.int32, (128, SLOT), 0) == lowest
        return low(jnp.where(is_high, 1.0, 0.0)), is_low

    def gather_scale(slot):
        is_high, is_low = slot_ids(slot)
        total = jnp.zeros((128, SLOT), jnp.float32)
        for piece in split_three(table[...]):
            total = total + dot(piece, is_high, TN)
        row = column_sum(jnp.where(is_low, total, 0.0))
        scale[slot_rows(slot), :] = jnp.transpose(jnp.broadcast_to(row, (128, SLOT)))

    def four(part):
        return jnp.concatenate([part] * 4, axis=1)

    def vector(ref, layer):
        return ref[layer : layer + 1, :]

    def kv_copies(layer, slot):
        rows = block_rows(slot, core)
        return [
            remote(
                ref.at[layer, rows],
                ref.at[layer, rows],
                kv_send.at[layer * 4 + slot * 2 + index],
                kv_recv.at[layer * 4 + slot * 2 + index],
                sibling,
            )
            for index, ref in enumerate((keys, values))
        ]

    def project_keys(layer, slot):
        rows = slot_rows(slot)
        if layer == 0:
            stream[rows, :] = wide(hidden[rows, :]) * four(scale[rows, :])
        x_b = low(stream[rows, :])
        x_round[layer, rows, :] = x_b
        weights = win.at[layer]
        mine = block_rows(slot, core)
        keys[layer, mine, :] = low(dot(x_b, weights[:, 512:1024], NN))
        values[layer, mine, :] = low(
            dot(x_b, weights[:, 1024:1536], NN) + vector(b_value, layer)
        )
        for copy in kv_copies(layer, slot):
            copy.start()

    def project_queries(layer):
        query = dot(x_round[layer], win[layer, :, 0:512], NN) + vector(b_query, layer)
        queries[layer] = low(wide(low(query)) * SCORE_SCALE)

    def own(ref, layer, columns):
        return jnp.concatenate(
            [ref[layer, block_rows(slot, core), columns] for slot in range(2)], axis=0
        )

    def attend(layer):
        first_half = lane((ROWS, 128)) < 64
        first_keys = lane((KEYS, 128)) < 64

        for pair in range(PAIRS):
            columns = slice(pair * 128, (pair + 1) * 128)
            q_pair = queries[layer, :, columns]
            k_pair = keys[layer, 0:KEYS, columns]
            v_pair = values[layer, 0:KEYS, columns]
            product = wide(q_pair) * wide(own(keys, layer, columns))
            found, self_terms = [], []
            for half in range(2):
                inside = first_half if half == 0 else jnp.logical_not(first_half)
                self_score = (
                    jnp.sum(jnp.where(inside, product, 0.0), axis=1, keepdims=True)
                    + self_bias[:, 0:1]
                )
                scores = dot(jnp.where(inside, q_pair, jnp.zeros_like(q_pair)), k_pair, NT)
                scores = scores + bias[0:1, :]
                top = jnp.maximum(jnp.max(scores, axis=1, keepdims=True), self_score)
                exponent = low(jnp.exp(scores - top))
                probs[2 * pair + half] = exponent
                with_ones = jnp.where(
                    first_keys if half == 0 else jnp.logical_not(first_keys),
                    v_pair,
                    jnp.ones_like(v_pair),
                )
                found.append(dot(exponent, with_ones, NN))
                self_terms.append(jnp.exp(self_score - top))
            self_low = low(jnp.where(first_half, self_terms[0], self_terms[1]))
            self_term = wide(self_low)
            sums = pltpu.roll(jnp.where(first_half, found[1], found[0]), 64, 1)
            inverse = 1.0 / (sums + self_term)
            total = jnp.where(first_half, found[0], found[1])
            total = total + self_term * wide(own(values, layer, columns))
            mixed[layer, :, columns] = total * inverse
            inverses[layer, :, columns] = inverse
            self_parts[layer, :, columns] = self_low

    def put_stat(layer, rows, index, column):
        stats[layer, rows, :] = jnp.where(lane((SLOT, 128)) == index, column, stats[layer, rows, :])

    def dense_forward(layer, slot):
        rows = slot_rows(slot)
        mixed_b = low(mixed[layer, rows, :])
        first = stream[rows, :] + (dot(mixed_b, wout[layer], NN) + vector(b_output, layer))
        normal, root = normalize(first)
        normal_one[layer, rows, :] = normal
        put_stat(layer, rows, 8, root)
        normed = normal * vector(gain_one, layer) + vector(shift_one, layer)
        inner = dot(low(normed), wup[layer], NN) + vector(b_up, layer)
        share = 0.5 * (1.0 + lax.erf(inner * 0.7071067811865476))
        slope[layer, rows, :] = share + inner * (
            0.3989422804014327 * jnp.exp(inner * inner * -0.5)
        )
        active_b = low(inner * share)
        active[layer, rows, :] = active_b
        second = normed + (dot(active_b, wdown[layer], NN) + vector(b_down, layer))
        normal, root = normalize(second)
        normal_two[layer, rows, :] = normal
        put_stat(layer, rows, 9, root)
        stream[rows, :] = normal * vector(gain_two, layer) + vector(shift_two, layer)

    def add_vector(member, layer, row):
        at = 2 * member + layer
        vectors[at : at + 1, :] = vectors[at : at + 1, :] + row

    def dense_backward(layer, slot):
        rows = slot_rows(slot)
        grad = stream[rows, :]
        normal = normal_two[layer, rows, :]
        add_vector(7, layer, column_sum(grad * normal))
        add_vector(8, layer, column_sum(grad))
        root = stats[layer, rows, :][:, 9:10]
        d_second = norm_back(grad, vector(gain_two, layer), normal, root)
        d_branch = low(d_second)
        d_packed[rows, 0:512] = d_branch
        add_vector(6, layer, column_sum(wide(d_branch)))
        d_inner = low(dot(d_branch, wdown[layer], NT) * slope[layer, rows, :])
        d_packed[rows, 512:1024] = d_inner
        add_vector(5, layer, column_sum(wide(d_inner)))
        d_normed = d_second + dot(d_inner, wup[layer], NT)
        normal = normal_one[layer, rows, :]
        add_vector(3, layer, column_sum(d_normed * normal))
        add_vector(4, layer, column_sum(d_normed))
        root = stats[layer, rows, :][:, 8:9]
        first = norm_back(d_normed, vector(gain_one, layer), normal, root)
        d_first[rows, :] = first
        d_attn = low(first)
        d_packed[rows, 1024:1536] = d_attn
        add_vector(2, layer, column_sum(wide(d_attn)))
        d_mixed[rows, :] = low(dot(d_attn, wout[layer], NT))

    def put_tiles(batch, first_tile, matrix):
        for tile in range(4):
            at = (first_tile + tile) * 512
            batch[at : at + 512, :] = low(matrix[:, tile * 128 : (tile + 1) * 128])

    def dense_weights(layer, batch):
        put_tiles(batch, 0, dot(active[layer], d_packed[:, 0:512], TN))
        normed = normal_one[layer] * vector(gain_one, layer) + vector(shift_one, layer)
        put_tiles(batch, 4, dot(low(normed), d_packed[:, 512:1024], TN))
        put_tiles(batch, 8, dot(low(mixed[layer]), d_packed[:, 1024:1536], TN))

    def grad_copy(layer, pair):
        return remote(
            sent.at[pair],
            received.at[pair],
            grad_send.at[layer * PAIRS + pair],
            grad_recv.at[layer * PAIRS + pair],
            sibling,
        )

    def attend_backward(layer, first_pair, last_pair):
        first_half = lane((ROWS, 128)) < 64

        for pair in range(first_pair, last_pair):
            columns = slice(pair * 128, (pair + 1) * 128)
            q_pair = queries[layer, :, columns]
            k_pair = keys[layer, 0:KEYS, columns]
            v_pair = values[layer, 0:KEYS, columns]
            d_out = low(wide(d_mixed[:, columns]) * inverses[layer, :, columns])
            d_wide = wide(d_out)
            d_turned = jnp.transpose(d_out)
            q_turned = jnp.transpose(q_pair)
            with_out = mixed[layer, :, columns] * d_wide
            with_own = wide(own(values, layer, columns)) * d_wide - with_out
            d_q, d_k, d_v, self_score, delta, d_probs = [], [], [], [], [], []
            for half in range(2):
                inside = first_half if half == 0 else jnp.logical_not(first_half)
                delta.append(jnp.sum(jnp.where(inside, with_out, 0.0), axis=1, keepdims=True))
                self_score.append(jnp.sum(jnp.where(inside, with_own, 0.0), axis=1, keepdims=True))
                d_probs.append(
                    dot(jnp.where(inside, d_out, jnp.zeros_like(d_out)), v_pair, NT)
                )
            for half in range(2):
                exponent = probs[2 * pair + half]
                d_scores = low(wide(exponent) * (d_probs[half] - delta[half]))
                d_q.append(dot(d_scores, k_pair, NN))
                d_k.append(dot(q_turned, d_scores, NN))
                d_v.append(dot(d_turned, exponent, NN))
            self_term = wide(self_parts[layer, :, columns])
            own_score = self_term * jnp.where(first_half, self_score[0], self_score[1])
            d_query = jnp.where(first_half, d_q[0], d_q[1]) + own_score * wide(
                own(keys, layer, columns)
            )
            d_packed[:, columns] = low(d_query * SCORE_SCALE)
            part_keys[0:KEYS, :] = jnp.transpose(
                jnp.concatenate([d_k[0][0:64], d_k[1][64:128]], axis=0)
            )
            part_values[0:KEYS, :] = jnp.transpose(
                jnp.concatenate([d_v[0][0:64], d_v[1][64:128]], axis=0)
            )
            own_keys = own_score * wide(q_pair)
            own_values = self_term * d_wide
            for slot in range(2):
                rows = slice(slot * SLOT, (slot + 1) * SLOT)
                mine = block_rows(slot, core)
                d_keys[rows, columns] = part_keys[mine, :] + own_keys[rows, :]
                d_values[rows, columns] = part_values[mine, :] + own_values[rows, :]
                other = block_rows(slot, 1 - core)
                sent[pair, 0, rows, :] = low(part_keys[other, :])
                sent[pair, 1, rows, :] = low(part_values[other, :])
            grad_copy(layer, pair).start()

    def merge_grads(layer):
        def pair_step(pair, _):
            grad_copy(layer, pair).wait()
            columns = pl.ds(pl.multiple_of(pair * 128, 128), 128)
            k_columns = pl.ds(pl.multiple_of(512 + pair * 128, 128), 128)
            v_columns = pl.ds(pl.multiple_of(1024 + pair * 128, 128), 128)
            d_packed[:, k_columns] = low(d_keys[:, columns] + wide(received[pair, 0]))
            d_packed[:, v_columns] = low(d_values[:, columns] + wide(received[pair, 1]))
            return 0

        lax.fori_loop(0, PAIRS, pair_step, 0)

    def input_weights(layer, batch, third):
        columns = slice(third * 512, (third + 1) * 512)
        put_tiles(batch, 4 * third, dot(x_round[layer], d_packed[:, columns], TN))
        if third == 0:
            add_vector(0, layer, column_sum(wide(d_packed[:, columns])))
        if third == 2:
            add_vector(1, layer, column_sum(wide(d_packed[:, columns])))

    def input_grad(layer, slot):
        rows = slot_rows(slot)
        stream[rows, :] = d_first[rows, :] + dot(d_packed[rows, :], win[layer], NT)

    def reduction(index, batch, result):
        from_core, s0, s1, s2, a, b, c, d = reduction_refs[index * 8 : index * 8 + 8]
        return Reduction(place, batch, result, from_core, (s0, s1, s2), (a, b, c, d))

    one_a = reduction(0, batch_a, reduced.at[0])
    one_b = reduction(1, batch_b, reduced.at[1])
    zero_a = reduction(2, batch_c, reduced.at[2])
    zero_b = reduction(3, batch_a, result_last)
    from_core, from_x, from_plane, a, b = reduction_refs[32:]
    more = ExtraReduction(place, extra, extra_result, from_core, from_x, from_plane, (a, b))

    loads[0].wait()
    gather_scale(here)
    loads[2].wait()
    project_keys(0, here)
    swap_ids.wait()
    gather_scale(there)
    swap_hidden.wait()
    project_keys(0, there)
    project_queries(0)
    swap_cot.start()
    for load in loads[1:2] + loads[6:]:
        load.start()
    probs_out = pltpu.make_async_copy(probs, kept_probs, probs_sem.at[0])
    probs_back = pltpu.make_async_copy(kept_probs, probs, probs_sem.at[1])
    for layer in range(2):
        for slot in range(2):
            for copy in kv_copies(layer, slot):
                copy.wait()
        if layer == 1:
            probs_out.wait()
        attend(layer)
        if layer == 0:
            probs_out.start()
        for load in loads[3 + 4 * layer : 6 + 4 * layer]:
            load.wait()
        if layer == 0:
            loads[6].wait()
        for slot in range(2):
            dense_forward(layer, slot)
            if layer == 0:
                project_keys(1, slot)
        if layer == 0:
            project_queries(1)

    out_round[...] = low(stream[...])
    keep_out = pltpu.make_async_copy(
        out_round.at[slot_rows(here)], layer_out.at[here], out_sems.at[0]
    )
    send_out = remote(
        out_round.at[slot_rows(there)],
        layer_out.at[here],
        swap_send.at[3],
        swap_recv.at[3],
        partner,
    )
    keep_out.start()
    send_out.start()

    loads[1].wait()
    swap_cot.wait()
    stream[...] = wide(cot[...])
    for slot in range(2):
        dense_backward(1, slot)
    dense_weights(1, batch_a)
    one_a.core_start()
    attend_backward(1, 0, 2)
    one_a.core_finish()
    one_a.scatter_start(0)
    attend_backward(1, 2, 4)
    probs_back.start()
    input_weights(1, batch_b, 0)
    merge_grads(1)
    input_weights(1, batch_b, 1)
    input_weights(1, batch_b, 2)
    one_b.core_start()
    one_a.scatter_finish(0)
    one_a.scatter_start(1)
    for slot in range(2):
        input_grad(1, slot)
    dense_backward(0, 0)
    one_b.core_finish()
    one_b.scatter_start(0)
    dense_backward(0, 1)
    one_a.scatter_finish(1)
    one_a.exchange_start()
    dense_weights(0, batch_c)
    zero_a.core_start()
    probs_back.wait()
    attend_backward(0, 0, 1)
    one_a.exchange_finish()
    one_a.gather_start(1)
    one_b.scatter_finish(0)
    one_b.scatter_start(1)
    attend_backward(0, 1, 2)
    zero_a.core_finish()
    zero_a.scatter_start(0)
    attend_backward(0, 2, 3)
    one_a.gather_finish(1)
    one_a.gather_start(0)
    one_b.scatter_finish(1)
    one_b.exchange_start()
    attend_backward(0, 3, 4)
    input_weights(0, batch_a, 0)
    merge_grads(0)
    input_weights(0, batch_a, 1)
    input_weights(0, batch_a, 2)
    zero_b.core_start()
    zero_a.scatter_finish(0)
    zero_a.scatter_start(1)
    one_b.exchange_finish()
    one_b.gather_start(1)
    for slot in range(2):
        input_grad(0, slot)
    zero_b.core_finish()
    zero_b.scatter_start(0)

    genes = jnp.zeros((GENE_ROWS, 128), jnp.float32)
    for slot in range(2):
        rows = slot_rows(slot)
        is_high, is_low = slot_ids(slot)
        per_token = jnp.sum(stream[rows, :] * wide(hidden[rows, :]), axis=1, keepdims=True)
        row = jnp.transpose(jnp.broadcast_to(per_token, (SLOT, 128)))
        for piece in split_three(jnp.where(is_low, row, 0.0)):
            genes = genes + dot(is_high, piece, NT)
    extra[0:GENE_ROWS, :] = genes
    for index in range(18):
        for tile in range(4):
            at = GENE_ROWS + 4 * index + tile
            extra[at : at + 1, :] = vectors[index : index + 1, tile * 128 : (tile + 1) * 128]
    more.core_start()

    for slot in range(2):
        rows = slot_rows(slot)
        d_mixed[rows, :] = low(stream[rows, :] * four(scale[rows, :]))
    keep_grad = pltpu.make_async_copy(
        d_mixed.at[slot_rows(here)], grad_hidden.at[here], out_sems.at[1]
    )
    send_grad = remote(
        d_mixed.at[slot_rows(there)],
        grad_hidden.at[here],
        swap_send.at[4],
        swap_recv.at[4],
        partner,
    )
    more.core_finish()
    more.x_start()
    keep_grad.start()

    send_grad.start()
    one_a.gather_finish(0)
    one_a.share_start()
    zero_a.scatter_finish(1)
    zero_a.exchange_start()
    zero_b.scatter_finish(0)
    zero_b.scatter_start(1)
    more.x_finish()
    more.plane_start(1)
    one_b.gather_finish(1)
    one_b.gather_start(0)
    zero_b.scatter_finish(1)
    zero_b.exchange_start()
    zero_a.exchange_finish()
    zero_a.gather_start(1)
    more.plane_finish(1)
    more.plane_start(2)
    zero_b.exchange_finish()
    zero_b.gather_start(1)
    more.plane_finish(2)
    more.x_back_start()
    zero_a.gather_finish(1)
    zero_a.gather_start(0)
    one_b.gather_finish(0)
    one_b.share_start()
    zero_b.gather_finish(1)
    zero_b.gather_start(0)
    more.x_back_finish()
    more.share_start()
    zero_a.gather_finish(0)
    zero_a.share_start()
    more.share_finish()
    extra_copy = pltpu.make_async_copy(extra_result, extra_out, out_sems.at[2])
    extra_copy.start()
    zero_b.gather_finish(0)
    zero_b.share_start()
    one_a.share_finish()
    one_b.share_finish()
    zero_a.share_finish()
    zero_b.share_finish()
    last_copy = pltpu.make_async_copy(result_last, reduced.at[3], out_sems.at[3])
    last_copy.start()
    keep_out.wait()
    send_out.wait()
    keep_grad.wait()
    send_grad.wait()
    extra_copy.wait()
    last_copy.wait()


def reduction_scratch():
    return [
        pltpu.VMEM((HALF_ROWS, 128), jnp.bfloat16),
        pltpu.VMEM((3, 3, STEP_ROWS[0], 128), jnp.bfloat16),
        pltpu.VMEM((3, 3, STEP_ROWS[1], 128), jnp.bfloat16),
        pltpu.VMEM((3, 4, STEP_ROWS[1], 128), jnp.bfloat16),
        pltpu.SemaphoreType.DMA((2,)),
        pltpu.SemaphoreType.DMA((2,)),
        pltpu.SemaphoreType.DMA((48,)),
        pltpu.SemaphoreType.DMA((45,)),
    ]


def extra_scratch():
    return [
        pltpu.VMEM((EXTRA_HALF, 128), jnp.float32),
        pltpu.VMEM((3, EXTRA_PIECE, 128), jnp.float32),
        pltpu.VMEM((2, 4, EXTRA_PIECE, 128), jnp.float32),
        pltpu.SemaphoreType.DMA((14,)),
        pltpu.SemaphoreType.DMA((14,)),
    ]


def run_model(hidden_in, cotangent, gene_ids, unknown_count, table, weights, vector_args):
    f32, bf16 = jnp.float32, jnp.bfloat16
    vmem = pl.BlockSpec(memory_space=pltpu.VMEM)
    smem = pl.BlockSpec(memory_space=pltpu.SMEM)
    anywhere = pl.BlockSpec(memory_space=pl.ANY)
    scratch = [
        pltpu.VMEM((ROWS, 512), bf16),
        pltpu.VMEM((ROWS, 512), bf16),
        pltpu.VMEM((3, 8, SLOT), jnp.int32),
        pltpu.VMEM((ROWS, 128), f32),
        pltpu.VMEM((2, 512, 1536), bf16),
        pltpu.VMEM((2, 512, 512), bf16),
        pltpu.VMEM((2, 512, 512), bf16),
        pltpu.VMEM((2, 512, 512), bf16),
        pltpu.VMEM((ROWS, 512), f32),
        pltpu.VMEM((2, ROWS, 512), bf16),
        pltpu.VMEM((2, ROWS, 512), bf16),
        pltpu.VMEM((2, GENES, 512), bf16),
        pltpu.VMEM((2, GENES, 512), bf16),
        pltpu.VMEM((HEADS, ROWS, KEYS), bf16),
        pltpu.VMEM((2, ROWS, 128), f32),
        pltpu.VMEM((2, ROWS, 512), f32),
        pltpu.VMEM((2, ROWS, 512), bf16),
        pltpu.VMEM((2, ROWS, 512), f32),
        pltpu.VMEM((2, ROWS, 512), f32),
        pltpu.VMEM((2, ROWS, 512), f32),
        pltpu.VMEM((2, ROWS, 512), f32),
        pltpu.VMEM((2, ROWS, 512), bf16),
        pltpu.VMEM((ROWS, 512), f32),
        pltpu.VMEM((ROWS, 512), bf16),
        pltpu.VMEM((ROWS, 1536), bf16),
        pltpu.VMEM((ROWS, 512), f32),
        pltpu.VMEM((ROWS, 512), f32),
        pltpu.VMEM((GENES, 128), f32),
        pltpu.VMEM((GENES, 128), f32),
        pltpu.VMEM((PAIRS, 2, ROWS, 128), bf16),
        pltpu.VMEM((PAIRS, 2, ROWS, 128), bf16),
        pltpu.VMEM((8, KEYS), f32),
        pltpu.VMEM((ROWS, 128), f32),
        pltpu.VMEM((24, 512), f32),
        pltpu.VMEM((ROWS, 512), bf16),
        pltpu.VMEM((EXTRA_ROWS, 128), f32),
        pltpu.VMEM((BATCH_ROWS, 128), bf16),
        pltpu.VMEM((BATCH_ROWS, 128), bf16),
        pltpu.VMEM((BATCH_ROWS, 128), bf16),
        pltpu.VMEM((BATCH_ROWS, 128), bf16),
        pltpu.VMEM((EXTRA_ROWS, 128), f32),
        pltpu.SemaphoreType.DMA((10,)),
        pltpu.SemaphoreType.DMA((5,)),
        pltpu.SemaphoreType.DMA((5,)),
        pltpu.SemaphoreType.DMA((8,)),
        pltpu.SemaphoreType.DMA((8,)),
        pltpu.SemaphoreType.DMA((8,)),
        pltpu.SemaphoreType.DMA((8,)),
        pltpu.SemaphoreType.DMA((2,)),
        pltpu.SemaphoreType.DMA((4,)),
    ]
    for _ in range(4):
        scratch += reduction_scratch()
    scratch += extra_scratch()
    outs = (
        jax.ShapeDtypeStruct((2, SLOT, 512), bf16),
        jax.ShapeDtypeStruct((2, SLOT, 512), bf16),
        jax.ShapeDtypeStruct((4, BATCH_ROWS, 128), bf16),
        jax.ShapeDtypeStruct((EXTRA_ROWS, 128), f32),
        jax.ShapeDtypeStruct((HEADS, ROWS, KEYS), bf16),
    )
    return pl.pallas_call(
        model_kernel,
        out_shape=outs,
        in_specs=[anywhere, anywhere, vmem, smem, vmem] + [anywhere] * 4 + [vmem] * 9,
        out_specs=(anywhere,) * 5,
        scratch_shapes=scratch,
        compiler_params=pltpu.CompilerParams(
            collective_id=0, has_side_effects=True, vmem_limit_bytes=63 << 20
        ),
        name="model",
    )(hidden_in, cotangent, gene_ids, unknown_count, table, *weights, *vector_args)


def finish_kernel(layer_in, hidden_grad_in, reduced, extra, *refs):
    layer_out, hidden_out, g_inputs, g_output, g_up, g_down, genes = refs[:7]
    vector_outs = refs[7:16]
    rounded, narrow, rows_out, wide_in, wide_rest, extra_rows, in_sems, out_sems = refs[16:]
    sources = [layer_in, hidden_grad_in]
    loads = [
        pltpu.make_async_copy(sources[i], rounded.at[i], in_sems.at[i]) for i in range(2)
    ] + [pltpu.make_async_copy(reduced.at[i], narrow.at[i], in_sems.at[2 + i]) for i in range(4)]
    loads.append(pltpu.make_async_copy(extra, extra_rows, in_sems.at[6]))
    for load in loads[:1] + loads[6:] + loads[1:6]:
        load.start()
    stores = []

    def send(source, target):
        store = pltpu.make_async_copy(source, target, out_sems.at[len(stores)])
        store.start()
        stores.append(store)

    for index, target in enumerate((layer_out, hidden_out)):
        loads[index].wait()
        rows_out[index] = wide(rounded[index])
        send(rows_out.at[index], target)
    for layer in (1, 0):
        base = 2 * (1 - layer)
        loads[2 + base].wait()
        for index, target in enumerate((g_down, g_up, g_output)):
            for tile in range(4):
                at = (4 * index + tile) * 512
                wide_rest[layer, index, :, tile * 128 : (tile + 1) * 128] = wide(
                    narrow[base, at : at + 512, :]
                )
            send(wide_rest.at[layer, index], target.at[layer])
        loads[3 + base].wait()
        for tile in range(12):
            at = tile * 512
            wide_in[layer, :, tile * 128 : (tile + 1) * 128] = wide(
                narrow[base + 1, at : at + 512, :]
            )
        send(wide_in.at[layer], g_inputs.at[layer])
    loads[6].wait()
    genes[...] = extra_rows[0:GENE_ROWS, :]
    for member in range(9):
        for layer in range(2):
            for tile in range(4):
                at = GENE_ROWS + 4 * (2 * member + layer) + tile
                vector_outs[member][layer : layer + 1, tile * 128 : (tile + 1) * 128] = extra_rows[
                    at : at + 1, :
                ]
    for store in stores:
        store.wait()


def finish(layer_out, grad_hidden, reduced, extra):
    f32, bf16 = jnp.float32, jnp.bfloat16
    vmem = pl.BlockSpec(memory_space=pltpu.VMEM)
    anywhere = pl.BlockSpec(memory_space=pl.ANY)
    outs = [
        jax.ShapeDtypeStruct((2, SLOT, 512), f32),
        jax.ShapeDtypeStruct((2, SLOT, 512), f32),
        jax.ShapeDtypeStruct((2, 512, 1536), f32),
        jax.ShapeDtypeStruct((2, 512, 512), f32),
        jax.ShapeDtypeStruct((2, 512, 512), f32),
        jax.ShapeDtypeStruct((2, 512, 512), f32),
        jax.ShapeDtypeStruct((GENE_ROWS, 128), f32),
    ] + [jax.ShapeDtypeStruct((2, 512), f32)] * 9
    return pl.pallas_call(
        finish_kernel,
        out_shape=outs,
        in_specs=[anywhere] * 4,
        out_specs=[anywhere] * 6 + [vmem] * 10,
        scratch_shapes=[
            pltpu.VMEM((2, 2, SLOT, 512), bf16),
            pltpu.VMEM((4, BATCH_ROWS, 128), bf16),
            pltpu.VMEM((2, 2, SLOT, 512), f32),
            pltpu.VMEM((2, 512, 1536), f32),
            pltpu.VMEM((2, 3, 512, 512), f32),
            pltpu.VMEM((EXTRA_ROWS, 128), f32),
            pltpu.SemaphoreType.DMA((7,)),
            pltpu.SemaphoreType.DMA((10,)),
        ],
        compiler_params=pltpu.CompilerParams(vmem_limit_bytes=48 << 20),
        name="finish",
    )(layer_out, grad_hidden, reduced, extra)


def shards(
    hidden_in,
    gene_ids,
    unknown_count,
    gene_scale,
    w_inputs,
    b_query,
    b_value,
    w_output,
    b_output,
    gain_one,
    shift_one,
    w_up,
    b_up,
    w_down,
    b_down,
    gain_two,
    shift_two,
    cotangent,
):
    gene_count = gene_scale.shape[0]
    table = jnp.pad(gene_scale, (0, GENE_ROWS * 128 - gene_count)).reshape(GENE_ROWS, 128)
    layer_out, grad_hidden, reduced, extra, _ = run_model(
        hidden_in,
        cotangent,
        gene_ids,
        unknown_count,
        table,
        (w_inputs, w_output, w_up, w_down),
        (b_query, b_value, b_output, gain_one, shift_one, b_up, b_down, gain_two, shift_two),
    )
    (
        layer_out,
        grad_hidden,
        g_inputs,
        g_output,
        g_up,
        g_down,
        genes,
        g_b_query,
        g_b_value,
        g_b_output,
        g_gain_one,
        g_shift_one,
        g_b_up,
        g_b_down,
        g_gain_two,
        g_shift_two,
    ) = finish(layer_out, grad_hidden, reduced, extra)
    return (
        layer_out,
        grad_hidden,
        genes.reshape(-1)[:gene_count],
        g_inputs,
        g_b_query,
        g_b_value,
        g_output,
        g_b_output,
        g_gain_one,
        g_shift_one,
        g_up,
        g_b_up,
        g_down,
        g_b_down,
        g_gain_two,
        g_shift_two,
    )


def solution(mesh):
    placed = (
        P("dp", "blk", None),
        P("dp", "blk"),
        P("dp"),
        P(),
        P(),
        P(),
        P(),
        P(),
        P(),
        P(),
        P(),
        P(),
        P(),
        P(),
        P(),
        P(),
        P(),
        P("dp", "blk", None),
    )
    return jax.shard_map(
        shards,
        mesh=mesh,
        in_specs=placed,
        out_specs=(
            P("dp", "blk", None),
            P("dp", "blk", None),
            P(),
            P(),
            P(),
            P(),
            P(),
            P(),
            P(),
            P(),
            P(),
            P(),
            P(),
            P(),
            P(),
            P(),
        ),
        check_vma=False,
    )
```

```python
import jax
import jax.numpy as jnp
from jax import lax
from jax.experimental import pallas as pl
from jax.experimental.pallas import tpu as pltpu
from jax.sharding import PartitionSpec as P

HEADS = 8
MESH = pl.DeviceIdType.MESH
AXIS_ORDER = ((0, 1, 2), (1, 2, 0), (2, 0, 1))
BATCH_ROWS = 6144
EXTRA_ROWS = 576
EXTRA_HALF = EXTRA_ROWS // 2
EXTRA_PIECE = EXTRA_HALF // 4


class Place:
    def __init__(self):
        dp = lax.axis_index("dp")
        blk = lax.axis_index("blk")
        self.core = blk & 1
        self.x_hi = blk >> 1
        self.coord = (self.x_hi * 2 + (dp & 1), dp >> 3, (dp >> 1) & 3)
        self.next = [
            [(coord + distance) & 3 for distance in range(4)] for coord in self.coord
        ]
        self.peers = [
            [self.device(axis, self.next[axis][distance]) for distance in range(4)]
            for axis in range(3)
        ]
        self.other_core = (dp, blk ^ 1)

    def device(self, axis, place):
        x, y, z = (place if axis == index else self.coord[index] for index in range(3))
        return (y * 8 + z * 2 + (x & 1), (x & 2) + self.core)

    def sibling(self):
        return self.other_core

    def peer(self, axis, distance):
        return self.peers[axis][distance]


def greet(place):
    barrier = pltpu.get_barrier_semaphore()
    others = [place.sibling()]
    for axis in range(3):
        for distance in (1, 2, 3):
            others.append(place.peer(axis, distance))
    for other in others:
        pl.semaphore_signal(barrier, inc=1, device_id=other, device_id_type=MESH)
    pl.semaphore_wait(barrier, len(others))


def remote(src, dst, send_sem, recv_sem, device):
    return pltpu.make_async_remote_copy(
        src_ref=src,
        dst_ref=dst,
        send_sem=send_sem,
        recv_sem=recv_sem,
        device_id=device,
        device_id_type=MESH,
    )


class Reduction:
    def __init__(self, place, batch, result, rows, deep, refs):
        self.place = place
        self.batch = batch
        self.result = result
        self.half = rows // 2
        self.part = rows // 6
        self.first = self.part // 4
        self.piece = self.first // 4 if deep else self.first
        self.from_core, self.from_first, self.from_second, self.from_third = refs[:4]
        self.send, self.recv, self.local = refs[4:]
        self.mine = place.core * self.half
        self.other = (1 - place.core) * self.half
        if deep:
            self.steps = ["core", "scatter0", "scatter1", "exchange2", "gather1", "gather0", "share"]
        else:
            self.steps = ["core", "scatter0", "exchange1", "exchange2", "gather0", "share"]
        self.deep = deep
        self.at = 0
        self.last = len(self.steps)

    def scratch(rows, deep):
        first = rows // 24
        piece = first // 4 if deep else first
        second = (3, 3, piece, 128) if deep else (3, 4, piece, 128)
        return [
            pltpu.VMEM((rows // 2, 128), jnp.bfloat16),
            pltpu.VMEM((3, 3, first, 128), jnp.bfloat16),
            pltpu.VMEM(second, jnp.bfloat16),
            pltpu.VMEM((3, 4, piece, 128), jnp.bfloat16),
            pltpu.SemaphoreType.DMA,
            pltpu.SemaphoreType.DMA((7,)),
            pltpu.SemaphoreType.DMA((3,)),
        ]

    def advance(self):
        if self.at > 0:
            name = self.steps[self.at - 1]
            self.run(name, "finish", self.at - 1)
        if self.at < len(self.steps):
            self.run(self.steps[self.at], "start", self.at)
        self.at += 1

    def run(self, name, action, index):
        if name[-1] in "012":
            getattr(self, name[:-1] + "_" + action)(int(name[-1]), index)
        else:
            getattr(self, name + "_" + action)(index)

    def wait_bytes(self, like, index):
        remote(like, like, self.send, self.recv.at[index], self.place.sibling()).wait()

    def base(self, part, steps):
        rows = self.mine + part * self.part
        if steps > 0:
            rows = rows + self.place.coord[AXIS_ORDER[part][0]] * self.first
        if steps > 1 and self.deep:
            rows = rows + self.place.coord[AXIS_ORDER[part][1]] * self.piece
        return pl.multiple_of(rows, 16)

    def block(self, part):
        return pl.ds(self.base(part, 2), self.piece)

    def core_copy(self, index):
        rows = pl.ds(pl.multiple_of(self.other, 16), self.half)
        return remote(
            self.batch.at[rows], self.from_core, self.send, self.recv.at[index], self.place.sibling()
        )

    def core_start(self, index):
        self.core_copy(index).start()

    def core_finish(self, index):
        self.core_copy(index).wait()
        size = self.half // 12

        def add(i, _):
            here = pl.ds(pl.multiple_of(self.mine + i * size, 16), size)
            there = pl.ds(pl.multiple_of(i * size, 16), size)
            self.batch[here] = (
                self.batch[here].astype(jnp.float32) + self.from_core[there].astype(jnp.float32)
            ).astype(jnp.bfloat16)
            return 0

        lax.fori_loop(0, 12, add, 0)

    def scatter_start(self, step, index):
        size = self.first if step == 0 else self.piece
        landing = self.from_first if step == 0 else self.from_second
        for part in range(3):
            axis = AXIS_ORDER[part][step]
            for distance in (1, 2, 3):
                target = self.place.next[axis][distance]
                rows = pl.multiple_of(self.base(part, step) + target * size, 16)
                remote(
                    self.batch.at[pl.ds(rows, size)],
                    landing.at[part, distance - 1],
                    self.send,
                    self.recv.at[index],
                    self.place.peer(axis, distance),
                ).start()

    def scatter_finish(self, step, index):
        size = self.first if step == 0 else self.piece
        landing = self.from_first if step == 0 else self.from_second
        self.wait_bytes(landing, index)
        for part in range(3):
            rows = pl.ds(self.base(part, step + 1), size)
            total = self.batch[rows].astype(jnp.float32)
            for distance in (1, 2, 3):
                total = total + landing[part, distance - 1].astype(jnp.float32)
            self.batch[rows] = total.astype(jnp.bfloat16)

    def exchange_start(self, step, index):
        landing = self.from_second if step == 1 else self.from_third
        for part in range(3):
            axis = AXIS_ORDER[part][step]
            for distance in (1, 2, 3):
                remote(
                    self.batch.at[self.block(part)],
                    landing.at[part, self.place.coord[axis]],
                    self.send,
                    self.recv.at[index],
                    self.place.peer(axis, distance),
                ).start()

    def exchange_finish(self, step, index):
        landing = self.from_second if step == 1 else self.from_third
        for part in range(3):
            landing[part, self.place.coord[AXIS_ORDER[part][step]]] = self.batch[self.block(part)]
        self.wait_bytes(self.from_second if self.deep else self.from_first, index)
        for part in range(3):
            terms = [landing[part, place].astype(jnp.float32) for place in range(4)]
            total = (terms[0] + terms[1]) + (terms[2] + terms[3])
            self.batch[self.block(part)] = total.astype(jnp.bfloat16)

    def local_copies(self):
        return [
            pltpu.make_async_copy(
                self.batch.at[self.block(part)],
                self.result.at[self.block(part)],
                self.local.at[part],
            )
            for part in range(3)
        ]

    def gather_start(self, step, index):
        from_batch = step == 1 or not self.deep
        size = self.first if step == 0 else self.piece
        if from_batch:
            for copy in self.local_copies():
                copy.start()
        source = self.batch if from_batch else self.result
        for part in range(3):
            axis = AXIS_ORDER[part][step]
            rows = pl.ds(self.base(part, step + 1), size)
            for distance in (1, 2, 3):
                remote(
                    source.at[rows],
                    self.result.at[rows],
                    self.send,
                    self.recv.at[index],
                    self.place.peer(axis, distance),
                ).start()

    def gather_finish(self, step, index):
        if step == 1 or not self.deep:
            for copy in self.local_copies():
                copy.wait()
        self.wait_bytes(self.from_first if step == 0 else self.from_second, index)

    def share_copy(self, index):
        rows = pl.ds(pl.multiple_of(self.mine, 16), self.half)
        return remote(
            self.result.at[rows],
            self.result.at[rows],
            self.send,
            self.recv.at[index],
            self.place.sibling(),
        )

    def share_start(self, index):
        self.share_copy(index).start()

    def share_finish(self, index):
        self.share_copy(index).wait()


class ExtraReduction:
    def __init__(self, place, rows_ref, result, refs):
        self.place = place
        self.ref = rows_ref
        self.result = result
        self.from_core, self.from_x, self.from_plane, self.send, self.recv = refs
        self.mine = place.core * EXTRA_HALF
        self.other = (1 - place.core) * EXTRA_HALF
        self.at = 0
        self.last = 6

    def scratch():
        return [
            pltpu.VMEM((EXTRA_HALF, 128), jnp.float32),
            pltpu.VMEM((3, EXTRA_PIECE, 128), jnp.float32),
            pltpu.VMEM((2, 4, EXTRA_PIECE, 128), jnp.float32),
            pltpu.SemaphoreType.DMA,
            pltpu.SemaphoreType.DMA((6,)),
        ]

    def advance(self):
        if self.at > 0:
            self.finish(self.at - 1)
        if self.at < 6:
            self.start(self.at)
        self.at += 1

    def piece(self, quarter):
        return pl.ds(pl.multiple_of(self.mine + quarter * EXTRA_PIECE, 8), EXTRA_PIECE)

    def copy(self, index, source, target, device):
        return remote(source, target, self.send, self.recv.at[index], device)

    def core_copy(self):
        rows = pl.ds(pl.multiple_of(self.other, 8), EXTRA_HALF)
        return self.copy(0, self.ref.at[rows], self.from_core, self.place.sibling())

    def share_copy(self):
        rows = pl.ds(pl.multiple_of(self.mine, 8), EXTRA_HALF)
        return self.copy(5, self.result.at[rows], self.result.at[rows], self.place.sibling())

    def start(self, index):
        rows = self.piece(self.place.coord[0])
        if index == 0:
            self.core_copy().start()
            return
        if index == 5:
            self.share_copy().start()
            return
        for distance in (1, 2, 3):
            if index == 1:
                target = self.place.next[0][distance]
                source, target, axis = self.ref.at[self.piece(target)], self.from_x.at[distance - 1], 0
            elif index == 4:
                source, target, axis = self.result.at[rows], self.result.at[rows], 0
            else:
                axis = index - 1
                source = self.ref.at[rows]
                target = self.from_plane.at[axis - 1, self.place.coord[axis]]
            self.copy(index, source, target, self.place.peer(axis, distance)).start()

    def finish(self, index):
        rows = self.piece(self.place.coord[0])
        if index == 0:
            self.core_copy().wait()
            half = pl.ds(pl.multiple_of(self.mine, 8), EXTRA_HALF)
            self.ref[half] = self.ref[half] + self.from_core[...]
            return
        if index == 5:
            self.share_copy().wait()
            return
        if index in (2, 3):
            self.from_plane[index - 2, self.place.coord[index - 1]] = self.ref[rows]
        self.copy(index, self.from_x, self.from_x, self.place.sibling()).wait()
        if index == 1:
            self.ref[rows] = self.ref[rows] + self.from_x[0] + self.from_x[1] + self.from_x[2]
        elif index in (2, 3):
            terms = [self.from_plane[index - 2, place] for place in range(4)]
            target = self.ref if index == 2 else self.result
            target[rows] = (terms[0] + terms[1]) + (terms[2] + terms[3])


ROWS = 512
SLOT = 256
KEYS = 768
GENES = 1024
GENE_ROWS = 480
PAIRS = 4
GROUPS = ((0, 2), (2, 4))
PLAN = {
    "one pair 1": ("one_a",),
    "one keys": ("one_a",),
    "zero dense 0": ("one_b",),
    "zero dense 1": ("one_a",),
    "zero pair 1": ("zero_a",),
    "zero pair 2": ("one_b", "one_a"),
    "zero queries": ("first",),
    "zero merge": ("zero_a",),
    "zero values": ("one_b", "one_a"),
    "genes": ("last", "first"),
    "hidden": ("zero_a",),
}
ENDING = (
    "more", "one_b", "one_a", "first", "more", "zero_a",
    "one_a", "last", "one_b", "first", "more", "last",
    "zero_a", "first", "more", "one_b", "last", "one_b",
    "more", "first", "last", "zero_a", "more", "first",
    "zero_a", "last", "last",
)
NEG = -1e30
SCORE_SCALE = 0.125
NN = (((1,), (0,)), ((), ()))
NT = (((1,), (1,)), ((), ()))
TN = (((0,), (0,)), ((), ()))


def dot(left, right, dims):
    return lax.dot_general(left, right, dims, preferred_element_type=jnp.float32)


def low(values):
    return values.astype(jnp.bfloat16)


def wide(values):
    return values.astype(jnp.float32)


def lane(shape):
    return lax.broadcasted_iota(jnp.int32, shape, 1)


def normalize(values):
    center = values - jnp.mean(values, axis=1, keepdims=True)
    root = lax.rsqrt(jnp.mean(center * center, axis=1, keepdims=True) + 1e-05)
    return center * root, root


def norm_back(grad, gain, normal, root):
    u = grad * gain
    mean = jnp.mean(u, axis=1, keepdims=True)
    along = jnp.mean(u * normal, axis=1, keepdims=True)
    return (u - mean - normal * along) * root


def column_sum(values):
    return jnp.sum(values, axis=0, keepdims=True)


def split_three(values):
    first = low(values)
    rest = values - wide(first)
    second = low(rest)
    third = low(rest - wide(second))
    return first, second, third


def model_kernel(
    hidden_in,
    cotangent,
    ids_in,
    unknown,
    table,
    w_inputs,
    w_output,
    w_up,
    w_down,
    b_query,
    b_value,
    b_output,
    gain_one,
    shift_one,
    b_up,
    b_down,
    gain_two,
    shift_two,
    layer_out,
    grad_hidden,
    reduced,
    extra_out,
    kept_probs,
    hidden,
    ids,
    scale,
    win,
    wout,
    wup,
    wdown,
    stream,
    x_round,
    queries,
    keys,
    values,
    probs,
    stats,
    inverses,
    self_parts,
    mixed,
    normal_one,
    normal_two,
    slope,
    active,
    d_first,
    d_mixed,
    d_packed,
    d_keys,
    d_values,
    part_keys,
    part_values,
    sent,
    received,
    bias,
    self_bias,
    vectors,
    out_round,
    extra,
    batch_a,
    batch_b,
    batch_c,
    batch_d,
    extra_result,
    load_sems,
    swap_send,
    swap_recv,
    kv_send,
    kv_recv,
    grad_send,
    grad_recv,
    probs_sem,
    out_sems,
    *reduction_refs,
):
    place = Place()
    cot = d_mixed
    core, here = place.core, place.x_hi
    there = 1 - here
    partner = place.peer(0, 2)
    sibling = place.sibling()

    def slot_rows(slot):
        return pl.ds(pl.multiple_of(slot * SLOT, SLOT), SLOT)

    def block_rows(slot, which):
        return pl.ds(pl.multiple_of((2 * slot + which) * SLOT, SLOT), SLOT)

    load_hidden = pltpu.make_async_copy(
        hidden_in.at[here], hidden.at[slot_rows(here)], load_sems.at[0]
    )
    load_cot = pltpu.make_async_copy(cotangent.at[here], cot.at[slot_rows(here)], load_sems.at[1])
    loads = []
    for layer in range(2):
        for index, (source, target) in enumerate(
            ((w_inputs, win), (w_output, wout), (w_up, wup), (w_down, wdown))
        ):
            loads.append(
                pltpu.make_async_copy(
                    source.at[layer],
                    target.at[layer],
                    load_sems.at[4 if layer == 1 else 2 if index == 0 else 3],
                )
            )
    load_hidden.start()
    for load in loads[0:4]:
        load.start()
    wait_rest = pltpu.make_async_copy(w_inputs.at[0], win.at[0], load_sems.at[3])
    wait_next = pltpu.make_async_copy(w_inputs, win, load_sems.at[4])
    for cell in range(2):
        ids[cell] = jnp.broadcast_to(ids_in[cell : cell + 1, :], (8, SLOT))
    known = GENES - unknown[here]

    greet(place)

    swap_hidden = remote(
        hidden_in.at[there],
        hidden.at[slot_rows(here)],
        swap_send.at[0],
        swap_recv.at[0],
        partner,
    )
    swap_ids = remote(ids.at[there], ids.at[2], swap_send.at[1], swap_recv.at[1], partner)
    swap_cot = remote(
        cotangent.at[there],
        cot.at[slot_rows(here)],
        swap_send.at[2],
        swap_recv.at[2],
        partner,
    )
    swap_ids.start()
    swap_hidden.start()

    bias[...] = jnp.where(lane((8, KEYS)) < known, 0.0, NEG)
    for slot in range(2):
        position = (2 * slot + core) * SLOT + lax.broadcasted_iota(jnp.int32, (SLOT, 128), 0)
        self_bias[slot * SLOT : (slot + 1) * SLOT, :] = jnp.where(position >= known, 0.0, NEG)
    part_keys[KEYS:GENES, :] = jnp.zeros((GENES - KEYS, 128), jnp.float32)
    part_values[KEYS:GENES, :] = jnp.zeros((GENES - KEYS, 128), jnp.float32)
    vectors[...] = jnp.zeros_like(vectors)
    extra[...] = jnp.zeros_like(extra)

    def slot_ids(slot):
        row = jnp.where(slot == here, ids[here, 0:1, :], ids[2, 0:1, :])
        high = lax.shift_right_logical(row, 7)
        lowest = lax.bitwise_and(row, 127)
        is_high = lax.broadcasted_iota(jnp.int32, (GENE_ROWS, SLOT), 0) == high
        is_low = lax.broadcasted_iota(jnp.int32, (128, SLOT), 0) == lowest
        return low(jnp.where(is_high, 1.0, 0.0)), is_low

    def gather_scale(slot):
        is_high, is_low = slot_ids(slot)
        total = jnp.zeros((128, SLOT), jnp.float32)
        for piece in split_three(table[...]):
            total = total + dot(piece, is_high, TN)
        row = column_sum(jnp.where(is_low, total, 0.0))
        scale[slot_rows(slot), :] = jnp.transpose(jnp.broadcast_to(row, (128, SLOT)))

    def four(part):
        return jnp.concatenate([part] * 4, axis=1)

    def vector(ref, layer):
        return ref[layer : layer + 1, :]

    def kv_copies(layer, slot):
        rows = block_rows(slot, core)
        return [
            remote(
                ref.at[layer, rows],
                ref.at[layer, rows],
                kv_send,
                kv_recv.at[layer],
                sibling,
            )
            for ref in (keys, values)
        ]

    def project_keys(layer, slot):
        rows = slot_rows(slot)
        if layer == 0:
            stream[rows, :] = wide(hidden[rows, :]) * four(scale[rows, :])
        x_b = low(stream[rows, :])
        x_round[layer, rows, :] = x_b
        weights = win.at[layer]
        mine = block_rows(slot, core)
        keys[layer, mine, :] = low(dot(x_b, weights[:, 512:1024], NN))
        values[layer, mine, :] = low(
            dot(x_b, weights[:, 1024:1536], NN) + vector(b_value, layer)
        )
        for copy in kv_copies(layer, slot):
            copy.start()

    def project_queries(layer):
        query = dot(x_round[layer], win[layer, :, 0:512], NN) + vector(b_query, layer)
        queries[layer] = low(wide(low(query)) * SCORE_SCALE)

    def own(ref, layer, columns):
        return jnp.concatenate(
            [ref[layer, block_rows(slot, core), columns] for slot in range(2)], axis=0
        )

    def attend(layer):
        first_half = lane((ROWS, 128)) < 64
        first_keys = lane((KEYS, 128)) < 64

        for pair in range(PAIRS):
            columns = slice(pair * 128, (pair + 1) * 128)
            q_pair = queries[layer, :, columns]
            k_pair = keys[layer, 0:KEYS, columns]
            v_pair = values[layer, 0:KEYS, columns]
            product = wide(q_pair) * wide(own(keys, layer, columns))
            found, self_terms = [], []
            for half in range(2):
                inside = first_half if half == 0 else jnp.logical_not(first_half)
                self_score = (
                    jnp.sum(jnp.where(inside, product, 0.0), axis=1, keepdims=True)
                    + self_bias[:, 0:1]
                )
                scores = dot(jnp.where(inside, q_pair, jnp.zeros_like(q_pair)), k_pair, NT)
                scores = scores + bias[0:1, :]
                top = jnp.maximum(jnp.max(scores, axis=1, keepdims=True), self_score)
                exponent = low(jnp.exp(scores - top))
                probs[2 * pair + half] = exponent
                with_ones = jnp.where(
                    first_keys if half == 0 else jnp.logical_not(first_keys),
                    v_pair,
                    jnp.ones_like(v_pair),
                )
                found.append(dot(exponent, with_ones, NN))
                self_terms.append(jnp.exp(self_score - top))
            self_low = low(jnp.where(first_half, self_terms[0], self_terms[1]))
            self_term = wide(self_low)
            sums = pltpu.roll(jnp.where(first_half, found[1], found[0]), 64, 1)
            inverse = 1.0 / (sums + self_term)
            total = jnp.where(first_half, found[0], found[1])
            total = total + self_term * wide(own(values, layer, columns))
            mixed[layer, :, columns] = total * inverse
            inverses[layer, :, columns] = inverse
            self_parts[layer, :, columns] = self_low

    def put_stat(layer, rows, index, column):
        stats[layer, rows, :] = jnp.where(lane((SLOT, 128)) == index, column, stats[layer, rows, :])

    def dense_forward(layer, slot):
        rows = slot_rows(slot)
        mixed_b = low(mixed[layer, rows, :])
        first = stream[rows, :] + (dot(mixed_b, wout[layer], NN) + vector(b_output, layer))
        normal, root = normalize(first)
        normal_one[layer, rows, :] = normal
        put_stat(layer, rows, 8, root)
        normed = normal * vector(gain_one, layer) + vector(shift_one, layer)
        inner = dot(low(normed), wup[layer], NN) + vector(b_up, layer)
        share = 0.5 * (1.0 + lax.erf(inner * 0.7071067811865476))
        slope[layer, rows, :] = share + inner * (
            0.3989422804014327 * jnp.exp(inner * inner * -0.5)
        )
        active_b = low(inner * share)
        active[layer, rows, :] = active_b
        second = normed + (dot(active_b, wdown[layer], NN) + vector(b_down, layer))
        normal, root = normalize(second)
        normal_two[layer, rows, :] = normal
        put_stat(layer, rows, 9, root)
        stream[rows, :] = normal * vector(gain_two, layer) + vector(shift_two, layer)

    def add_vector(member, layer, row):
        at = 2 * member + layer
        vectors[at : at + 1, :] = vectors[at : at + 1, :] + row

    def dense_backward(layer, slot):
        rows = slot_rows(slot)
        grad = stream[rows, :]
        normal = normal_two[layer, rows, :]
        add_vector(7, layer, column_sum(grad * normal))
        add_vector(8, layer, column_sum(grad))
        root = stats[layer, rows, :][:, 9:10]
        d_second = norm_back(grad, vector(gain_two, layer), normal, root)
        d_branch = low(d_second)
        d_packed[rows, 0:512] = d_branch
        add_vector(6, layer, column_sum(wide(d_branch)))
        d_inner = low(dot(d_branch, wdown[layer], NT) * slope[layer, rows, :])
        d_packed[rows, 512:1024] = d_inner
        add_vector(5, layer, column_sum(wide(d_inner)))
        d_normed = d_second + dot(d_inner, wup[layer], NT)
        normal = normal_one[layer, rows, :]
        add_vector(3, layer, column_sum(d_normed * normal))
        add_vector(4, layer, column_sum(d_normed))
        root = stats[layer, rows, :][:, 8:9]
        first = norm_back(d_normed, vector(gain_one, layer), normal, root)
        d_first[rows, :] = first
        d_attn = low(first)
        d_packed[rows, 1024:1536] = d_attn
        add_vector(2, layer, column_sum(wide(d_attn)))
        d_mixed[rows, :] = low(dot(d_attn, wout[layer], NT))

    def put_tiles(batch, first_tile, matrix):
        for tile in range(4):
            at = (first_tile + tile) * 512
            batch[at : at + 512, :] = low(matrix[:, tile * 128 : (tile + 1) * 128])

    def dense_weights(layer, batch):
        put_tiles(batch, 0, dot(active[layer], d_packed[:, 0:512], TN))
        normed = normal_one[layer] * vector(gain_one, layer) + vector(shift_one, layer)
        put_tiles(batch, 4, dot(low(normed), d_packed[:, 512:1024], TN))
        put_tiles(batch, 8, dot(low(mixed[layer]), d_packed[:, 1024:1536], TN))

    def grad_copy(pair):
        return remote(
            sent.at[pair], received.at[pair], grad_send, grad_recv.at[pair], sibling
        )

    def attend_backward(layer, first_pair, last_pair):
        first_half = lane((ROWS, 128)) < 64

        for pair in range(first_pair, last_pair):
            columns = slice(pair * 128, (pair + 1) * 128)
            q_pair = queries[layer, :, columns]
            k_pair = keys[layer, 0:KEYS, columns]
            v_pair = values[layer, 0:KEYS, columns]
            d_out = low(wide(d_mixed[:, columns]) * inverses[layer, :, columns])
            d_wide = wide(d_out)
            d_turned = jnp.transpose(d_out)
            q_turned = jnp.transpose(q_pair)
            with_out = mixed[layer, :, columns] * d_wide
            with_own = wide(own(values, layer, columns)) * d_wide - with_out
            d_q, d_k, d_v, self_score, delta, d_probs = [], [], [], [], [], []
            for half in range(2):
                inside = first_half if half == 0 else jnp.logical_not(first_half)
                delta.append(jnp.sum(jnp.where(inside, with_out, 0.0), axis=1, keepdims=True))
                self_score.append(jnp.sum(jnp.where(inside, with_own, 0.0), axis=1, keepdims=True))
                d_probs.append(
                    dot(jnp.where(inside, d_out, jnp.zeros_like(d_out)), v_pair, NT)
                )
            for half in range(2):
                exponent = probs[2 * pair + half]
                d_scores = low(wide(exponent) * (d_probs[half] - delta[half]))
                d_q.append(dot(d_scores, k_pair, NN))
                d_k.append(dot(q_turned, d_scores, NN))
                d_v.append(dot(d_turned, exponent, NN))
            self_term = wide(self_parts[layer, :, columns])
            own_score = self_term * jnp.where(first_half, self_score[0], self_score[1])
            d_query = jnp.where(first_half, d_q[0], d_q[1]) + own_score * wide(
                own(keys, layer, columns)
            )
            d_packed[:, columns] = low(d_query * SCORE_SCALE)
            part_keys[0:KEYS, :] = jnp.transpose(
                jnp.concatenate([d_k[0][0:64], d_k[1][64:128]], axis=0)
            )
            part_values[0:KEYS, :] = jnp.transpose(
                jnp.concatenate([d_v[0][0:64], d_v[1][64:128]], axis=0)
            )
            own_keys = own_score * wide(q_pair)
            own_values = self_term * d_wide
            for slot in range(2):
                rows = slice(slot * SLOT, (slot + 1) * SLOT)
                mine = block_rows(slot, core)
                d_keys[rows, columns] = part_keys[mine, :] + own_keys[rows, :]
                d_values[rows, columns] = part_values[mine, :] + own_values[rows, :]
                other = block_rows(slot, 1 - core)
                sent[pair, 0, rows, :] = low(part_keys[other, :])
                sent[pair, 1, rows, :] = low(part_values[other, :])
            grad_copy(pair).start()

    def merge_grads(pairs):
        for pair in range(*pairs):
            grad_copy(pair).wait_recv()
            at = pair * 128
            columns = slice(at, at + 128)
            d_packed[:, 512 + at : 640 + at] = low(d_keys[:, columns] + wide(received[pair, 0]))
            d_packed[:, 1024 + at : 1152 + at] = low(d_values[:, columns] + wide(received[pair, 1]))

    def wait_sent():
        remote(sent, sent, grad_send, grad_recv.at[0], sibling).wait_send()

    def input_weights(layer, batch, first_row, third, pairs):
        first, last = pairs
        count = last - first
        columns = slice(third * 512 + first * 128, third * 512 + last * 128)
        product = dot(x_round[layer], d_packed[:, columns], TN)
        for tile in range(count):
            at = first_row + (third * count + tile) * 512
            batch[at : at + 512, :] = low(product[:, tile * 128 : (tile + 1) * 128])
        if third != 1:
            at = 2 * (third // 2) + layer
            inside = slice(first * 128, last * 128)
            vectors[at : at + 1, inside] = column_sum(wide(d_packed[:, columns]))

    def input_grad(layer, slot):
        rows = slot_rows(slot)
        stream[rows, :] = d_first[rows, :] + dot(d_packed[rows, :], win[layer], NT)

    def reduction(index, batch, result, rows, deep):
        return Reduction(
            place, batch, result, rows, deep, reduction_refs[7 * index : 7 * index + 7]
        )

    group_rows = [1536 * (last - first) for first, last in GROUPS]
    group_at = [sum(group_rows[:index]) for index in range(len(GROUPS))]
    one_a = reduction(0, batch_a, reduced.at[0], BATCH_ROWS, True)
    one_b = reduction(1, batch_b, reduced.at[1], BATCH_ROWS, True)
    zero_a = reduction(2, batch_c, reduced.at[2], BATCH_ROWS, True)
    groups = [
        reduction(
            3 + index,
            batch_d.at[pl.ds(at, rows)],
            reduced.at[3, pl.ds(at, rows)],
            rows,
            True,
        )
        for index, (at, rows) in enumerate(zip(group_at, group_rows))
    ]
    more = ExtraReduction(place, extra, extra_result, reduction_refs[7 * (3 + len(GROUPS)) :])
    running = {
        "one_a": one_a,
        "one_b": one_b,
        "zero_a": zero_a,
        "first": groups[0],
        "last": groups[1],
        "more": more,
    }

    def after(piece):
        for name in PLAN.get(piece, ()):
            running[name].advance()

    load_hidden.wait()
    gather_scale(here)
    loads[0].wait()
    project_keys(0, here)
    swap_ids.wait()
    gather_scale(there)
    swap_hidden.wait()
    project_keys(0, there)
    project_queries(0)
    swap_cot.start()
    load_cot.start()
    for load in loads[4:]:
        load.start()
    probs_out = pltpu.make_async_copy(probs, kept_probs, probs_sem.at[0])
    probs_back = pltpu.make_async_copy(kept_probs, probs, probs_sem.at[1])
    for layer in range(2):
        whole = keys.at[layer]
        remote(whole, whole, kv_send, kv_recv.at[layer], sibling).wait()
        if layer == 1:
            probs_out.wait()
        attend(layer)
        if layer == 0:
            probs_out.start()
            wait_rest.wait()
            wait_next.wait()
        for slot in range(2):
            dense_forward(layer, slot)
            if layer == 0:
                project_keys(1, slot)
        if layer == 0:
            project_queries(1)

    out_round[...] = low(stream[...])
    keep_out = pltpu.make_async_copy(
        out_round.at[slot_rows(here)], layer_out.at[here], out_sems.at[0]
    )
    send_out = remote(
        out_round.at[slot_rows(there)],
        layer_out.at[here],
        swap_send.at[3],
        swap_recv.at[3],
        partner,
    )
    keep_out.start()
    send_out.start()

    load_cot.wait()
    swap_cot.wait()
    stream[...] = wide(cot[...])
    every = (0, PAIRS)
    for slot in range(2):
        dense_backward(1, slot)
    dense_weights(1, batch_a)
    one_a.advance()
    for pair in range(PAIRS):
        attend_backward(1, pair, pair + 1)
        after(f"one pair {pair}")
    probs_back.start()
    input_weights(1, batch_b, 0, 0, every)
    after("one queries")
    merge_grads(every)
    after("one merge")
    input_weights(1, batch_b, 0, 1, every)
    after("one keys")
    input_weights(1, batch_b, 0, 2, every)
    one_b.advance()
    for slot in range(2):
        input_grad(1, slot)
        after(f"one input {slot}")
    for slot in range(2):
        dense_backward(0, slot)
        after(f"zero dense {slot}")
    dense_weights(0, batch_c)
    zero_a.advance()
    wait_sent()
    probs_back.wait()
    for pair in range(PAIRS):
        attend_backward(0, pair, pair + 1)
        after(f"zero pair {pair}")
        if pair == GROUPS[0][1]:
            merge_grads(GROUPS[0])
            for third in range(3):
                input_weights(0, batch_d, group_at[0], third, GROUPS[0])
            groups[0].advance()
    input_weights(0, batch_d, group_at[1], 0, GROUPS[1])
    after("zero queries")
    merge_grads(GROUPS[1])
    after("zero merge")
    for third in (1, 2):
        input_weights(0, batch_d, group_at[1], third, GROUPS[1])
    groups[1].advance()
    after("zero values")
    for slot in range(2):
        input_grad(0, slot)
        after(f"zero input {slot}")

    genes = jnp.zeros((GENE_ROWS, 128), jnp.float32)
    for slot in range(2):
        rows = slot_rows(slot)
        is_high, is_low = slot_ids(slot)
        per_token = jnp.sum(stream[rows, :] * wide(hidden[rows, :]), axis=1, keepdims=True)
        row = jnp.transpose(jnp.broadcast_to(per_token, (SLOT, 128)))
        for piece in split_three(jnp.where(is_low, row, 0.0)):
            genes = genes + dot(is_high, piece, NT)
    extra[0:GENE_ROWS, :] = genes
    for index in range(18):
        for tile in range(4):
            at = GENE_ROWS + 4 * index + tile
            extra[at : at + 1, :] = vectors[index : index + 1, tile * 128 : (tile + 1) * 128]
    after("genes")
    more.advance()
    for slot in range(2):
        rows = slot_rows(slot)
        d_mixed[rows, :] = low(stream[rows, :] * four(scale[rows, :]))
    keep_grad = pltpu.make_async_copy(
        d_mixed.at[slot_rows(here)], grad_hidden.at[here], out_sems.at[1]
    )
    send_grad = remote(
        d_mixed.at[slot_rows(there)],
        grad_hidden.at[here],
        swap_send.at[4],
        swap_recv.at[4],
        partner,
    )
    keep_grad.start()
    send_grad.start()
    after("hidden")
    for name in ENDING:
        running[name].advance()
        if name == "more" and more.at == 7:
            extra_copy = pltpu.make_async_copy(extra_result, extra_out, out_sems.at[2])
            extra_copy.start()
    for one in running.values():
        assert one.at == one.last + 1
    wait_sent()
    keep_out.wait()
    send_out.wait()
    keep_grad.wait()
    send_grad.wait()
    extra_copy.wait()


def run_model(hidden_in, cotangent, gene_ids, unknown_count, table, weights, vector_args):
    f32, bf16 = jnp.float32, jnp.bfloat16
    vmem = pl.BlockSpec(memory_space=pltpu.VMEM)
    smem = pl.BlockSpec(memory_space=pltpu.SMEM)
    anywhere = pl.BlockSpec(memory_space=pl.ANY)
    scratch = [
        pltpu.VMEM((ROWS, 512), bf16),
        pltpu.VMEM((3, 8, SLOT), jnp.int32),
        pltpu.VMEM((ROWS, 128), f32),
        pltpu.VMEM((2, 512, 1536), bf16),
        pltpu.VMEM((2, 512, 512), bf16),
        pltpu.VMEM((2, 512, 512), bf16),
        pltpu.VMEM((2, 512, 512), bf16),
        pltpu.VMEM((ROWS, 512), f32),
        pltpu.VMEM((2, ROWS, 512), bf16),
        pltpu.VMEM((2, ROWS, 512), bf16),
        pltpu.VMEM((2, GENES, 512), bf16),
        pltpu.VMEM((2, GENES, 512), bf16),
        pltpu.VMEM((HEADS, ROWS, KEYS), bf16),
        pltpu.VMEM((2, ROWS, 128), f32),
        pltpu.VMEM((2, ROWS, 512), f32),
        pltpu.VMEM((2, ROWS, 512), bf16),
        pltpu.VMEM((2, ROWS, 512), f32),
        pltpu.VMEM((2, ROWS, 512), f32),
        pltpu.VMEM((2, ROWS, 512), f32),
        pltpu.VMEM((2, ROWS, 512), f32),
        pltpu.VMEM((2, ROWS, 512), bf16),
        pltpu.VMEM((ROWS, 512), f32),
        pltpu.VMEM((ROWS, 512), bf16),
        pltpu.VMEM((ROWS, 1536), bf16),
        pltpu.VMEM((ROWS, 512), f32),
        pltpu.VMEM((ROWS, 512), f32),
        pltpu.VMEM((GENES, 128), f32),
        pltpu.VMEM((GENES, 128), f32),
        pltpu.VMEM((PAIRS, 2, ROWS, 128), bf16),
        pltpu.VMEM((PAIRS, 2, ROWS, 128), bf16),
        pltpu.VMEM((8, KEYS), f32),
        pltpu.VMEM((ROWS, 128), f32),
        pltpu.VMEM((24, 512), f32),
        pltpu.VMEM((ROWS, 512), bf16),
        pltpu.VMEM((EXTRA_ROWS, 128), f32),
        pltpu.VMEM((BATCH_ROWS, 128), bf16),
        pltpu.VMEM((BATCH_ROWS, 128), bf16),
        pltpu.VMEM((BATCH_ROWS, 128), bf16),
        pltpu.VMEM((BATCH_ROWS, 128), bf16),
        pltpu.VMEM((EXTRA_ROWS, 128), f32),
        pltpu.SemaphoreType.DMA((5,)),
        pltpu.SemaphoreType.DMA((5,)),
        pltpu.SemaphoreType.DMA((5,)),
        pltpu.SemaphoreType.DMA,
        pltpu.SemaphoreType.DMA((2,)),
        pltpu.SemaphoreType.DMA,
        pltpu.SemaphoreType.DMA((PAIRS,)),
        pltpu.SemaphoreType.DMA((2,)),
        pltpu.SemaphoreType.DMA((3,)),
    ]
    for _ in range(3):
        scratch += Reduction.scratch(BATCH_ROWS, True)
    for first, last in GROUPS:
        scratch += Reduction.scratch(1536 * (last - first), True)
    scratch += ExtraReduction.scratch()
    outs = (
        jax.ShapeDtypeStruct((2, SLOT, 512), bf16),
        jax.ShapeDtypeStruct((2, SLOT, 512), bf16),
        jax.ShapeDtypeStruct((4, BATCH_ROWS, 128), bf16),
        jax.ShapeDtypeStruct((EXTRA_ROWS, 128), f32),
        jax.ShapeDtypeStruct((HEADS, ROWS, KEYS), bf16),
    )
    return pl.pallas_call(
        model_kernel,
        out_shape=outs,
        in_specs=[anywhere, anywhere, vmem, smem, vmem] + [anywhere] * 4 + [vmem] * 9,
        out_specs=(anywhere,) * 5,
        scratch_shapes=scratch,
        compiler_params=pltpu.CompilerParams(
            collective_id=0, has_side_effects=True, vmem_limit_bytes=63 << 20
        ),
        name="model",
    )(hidden_in, cotangent, gene_ids, unknown_count, table, *weights, *vector_args)


def finish_kernel(layer_in, hidden_grad_in, reduced, extra, *refs):
    layer_out, hidden_out, g_inputs, g_output, g_up, g_down, genes = refs[:7]
    vector_outs = refs[7:16]
    rounded, narrow, rows_out, wide_in, wide_rest, extra_rows, in_sems, out_sems = refs[16:]
    sources = [layer_in, hidden_grad_in]
    loads = [
        pltpu.make_async_copy(sources[i], rounded.at[i], in_sems.at[i]) for i in range(2)
    ] + [pltpu.make_async_copy(reduced.at[i], narrow.at[i], in_sems.at[2 + i]) for i in range(4)]
    loads.append(pltpu.make_async_copy(extra, extra_rows, in_sems.at[6]))
    for load in loads[:1] + loads[6:] + loads[1:6]:
        load.start()
    stores = []

    def send(source, target):
        store = pltpu.make_async_copy(source, target, out_sems.at[len(stores)])
        store.start()
        stores.append(store)

    for index, target in enumerate((layer_out, hidden_out)):
        loads[index].wait()
        rows_out[index] = wide(rounded[index])
        send(rows_out.at[index], target)
    for layer in (1, 0):
        base = 2 * (1 - layer)
        loads[2 + base].wait()
        for index, target in enumerate((g_down, g_up, g_output)):
            for tile in range(4):
                at = (4 * index + tile) * 512
                wide_rest[layer, index, :, tile * 128 : (tile + 1) * 128] = wide(
                    narrow[base, at : at + 512, :]
                )
            send(wide_rest.at[layer, index], target.at[layer])
        loads[3 + base].wait()
        at = 0
        for first, last in GROUPS if layer == 0 else ((0, PAIRS),):
            for third in range(3):
                for pair in range(first, last):
                    column = third * 512 + pair * 128
                    wide_in[layer, :, column : column + 128] = wide(
                        narrow[base + 1, at : at + 512, :]
                    )
                    at += 512
        send(wide_in.at[layer], g_inputs.at[layer])
    loads[6].wait()
    genes[...] = extra_rows[0:GENE_ROWS, :]
    for member in range(9):
        for layer in range(2):
            for tile in range(4):
                at = GENE_ROWS + 4 * (2 * member + layer) + tile
                vector_outs[member][layer : layer + 1, tile * 128 : (tile + 1) * 128] = extra_rows[
                    at : at + 1, :
                ]
    for store in stores:
        store.wait()


def finish(layer_out, grad_hidden, reduced, extra):
    f32, bf16 = jnp.float32, jnp.bfloat16
    vmem = pl.BlockSpec(memory_space=pltpu.VMEM)
    anywhere = pl.BlockSpec(memory_space=pl.ANY)
    outs = [
        jax.ShapeDtypeStruct((2, SLOT, 512), f32),
        jax.ShapeDtypeStruct((2, SLOT, 512), f32),
        jax.ShapeDtypeStruct((2, 512, 1536), f32),
        jax.ShapeDtypeStruct((2, 512, 512), f32),
        jax.ShapeDtypeStruct((2, 512, 512), f32),
        jax.ShapeDtypeStruct((2, 512, 512), f32),
        jax.ShapeDtypeStruct((GENE_ROWS, 128), f32),
    ] + [jax.ShapeDtypeStruct((2, 512), f32)] * 9
    return pl.pallas_call(
        finish_kernel,
        out_shape=outs,
        in_specs=[anywhere] * 4,
        out_specs=[anywhere] * 6 + [vmem] * 10,
        scratch_shapes=[
            pltpu.VMEM((2, 2, SLOT, 512), bf16),
            pltpu.VMEM((4, BATCH_ROWS, 128), bf16),
            pltpu.VMEM((2, 2, SLOT, 512), f32),
            pltpu.VMEM((2, 512, 1536), f32),
            pltpu.VMEM((2, 3, 512, 512), f32),
            pltpu.VMEM((EXTRA_ROWS, 128), f32),
            pltpu.SemaphoreType.DMA((7,)),
            pltpu.SemaphoreType.DMA((10,)),
        ],
        compiler_params=pltpu.CompilerParams(vmem_limit_bytes=63 << 20),
        name="finish",
    )(layer_out, grad_hidden, reduced, extra)


def shards(
    hidden_in,
    gene_ids,
    unknown_count,
    gene_scale,
    w_inputs,
    b_query,
    b_value,
    w_output,
    b_output,
    gain_one,
    shift_one,
    w_up,
    b_up,
    w_down,
    b_down,
    gain_two,
    shift_two,
    cotangent,
):
    gene_count = gene_scale.shape[0]
    table = jnp.pad(gene_scale, (0, GENE_ROWS * 128 - gene_count)).reshape(GENE_ROWS, 128)
    layer_out, grad_hidden, reduced, extra, _ = run_model(
        hidden_in,
        cotangent,
        gene_ids,
        unknown_count,
        table,
        (w_inputs, w_output, w_up, w_down),
        (b_query, b_value, b_output, gain_one, shift_one, b_up, b_down, gain_two, shift_two),
    )
    (
        layer_out,
        grad_hidden,
        g_inputs,
        g_output,
        g_up,
        g_down,
        genes,
        g_b_query,
        g_b_value,
        g_b_output,
        g_gain_one,
        g_shift_one,
        g_b_up,
        g_b_down,
        g_gain_two,
        g_shift_two,
    ) = finish(layer_out, grad_hidden, reduced, extra)
    return (
        layer_out,
        grad_hidden,
        genes.reshape(-1)[:gene_count],
        g_inputs,
        g_b_query,
        g_b_value,
        g_output,
        g_b_output,
        g_gain_one,
        g_shift_one,
        g_up,
        g_b_up,
        g_down,
        g_b_down,
        g_gain_two,
        g_shift_two,
    )


def solution(mesh):
    placed = (
        P("dp", "blk", None),
        P("dp", "blk"),
        P("dp"),
        P(),
        P(),
        P(),
        P(),
        P(),
        P(),
        P(),
        P(),
        P(),
        P(),
        P(),
        P(),
        P(),
        P(),
        P("dp", "blk", None),
    )
    return jax.shard_map(
        shards,
        mesh=mesh,
        in_specs=placed,
        out_specs=(
            P("dp", "blk", None),
            P("dp", "blk", None),
            P(),
            P(),
            P(),
            P(),
            P(),
            P(),
            P(),
            P(),
            P(),
            P(),
            P(),
            P(),
            P(),
            P(),
        ),
        check_vma=False,
    )
```

```python
import jax
import jax.numpy as jnp
from jax import lax
from jax.experimental import pallas as pl
from jax.experimental.pallas import tpu as pltpu
from jax.sharding import PartitionSpec as P

HEADS = 8
MESH = pl.DeviceIdType.MESH
AXIS_ORDER = ((0, 1, 2), (1, 2, 0), (2, 0, 1))
BATCH_ROWS = 6144
EXTRA_ROWS = 576
EXTRA_HALF = EXTRA_ROWS // 2
EXTRA_PIECE = EXTRA_HALF // 4


class Place:
    def __init__(self):
        dp = lax.axis_index("dp")
        blk = lax.axis_index("blk")
        self.core = blk & 1
        self.x_hi = blk >> 1
        self.coord = (self.x_hi * 2 + (dp & 1), dp >> 3, (dp >> 1) & 3)
        self.next = [
            [(coord + distance) & 3 for distance in range(4)] for coord in self.coord
        ]
        self.peers = [
            [self.device(axis, self.next[axis][distance]) for distance in range(4)]
            for axis in range(3)
        ]
        self.other_core = (dp, blk ^ 1)

    def device(self, axis, place):
        x, y, z = (place if axis == index else self.coord[index] for index in range(3))
        return (y * 8 + z * 2 + (x & 1), (x & 2) + self.core)

    def sibling(self):
        return self.other_core

    def peer(self, axis, distance):
        return self.peers[axis][distance]


def greet(place):
    barrier = pltpu.get_barrier_semaphore()
    others = [place.sibling()]
    for axis in range(3):
        for distance in (1, 2, 3):
            others.append(place.peer(axis, distance))
    for other in others:
        pl.semaphore_signal(barrier, inc=1, device_id=other, device_id_type=MESH)
    pl.semaphore_wait(barrier, len(others))


def remote(src, dst, send_sem, recv_sem, device):
    return pltpu.make_async_remote_copy(
        src_ref=src,
        dst_ref=dst,
        send_sem=send_sem,
        recv_sem=recv_sem,
        device_id=device,
        device_id_type=MESH,
    )


class Reduction:
    def __init__(self, place, batch, result, rows, deep, refs):
        self.place = place
        self.batch = batch
        self.result = result
        self.half = rows // 2
        self.part = rows // 6
        self.first = self.part // 4
        self.piece = self.first // 4 if deep else self.first
        self.from_core, self.from_first, self.from_second, self.from_third = refs[:4]
        self.send, self.recv, self.local = refs[4:]
        self.mine = place.core * self.half
        self.other = (1 - place.core) * self.half
        if deep:
            self.steps = ["core", "scatter0", "scatter1", "exchange2", "gather1", "gather0", "share"]
        else:
            self.steps = ["core", "scatter0", "exchange1", "exchange2", "gather0", "share"]
        self.deep = deep
        self.at = 0
        self.last = len(self.steps)

    def scratch(rows, deep):
        first = rows // 24
        piece = first // 4 if deep else first
        second = (3, 3, piece, 128) if deep else (3, 4, piece, 128)
        return [
            pltpu.VMEM((rows // 2, 128), jnp.bfloat16),
            pltpu.VMEM((3, 3, first, 128), jnp.bfloat16),
            pltpu.VMEM(second, jnp.bfloat16),
            pltpu.VMEM((3, 4, piece, 128), jnp.bfloat16),
            pltpu.SemaphoreType.DMA,
            pltpu.SemaphoreType.DMA((7,)),
            pltpu.SemaphoreType.DMA((3,)),
        ]

    def advance(self):
        if self.at > 0:
            name = self.steps[self.at - 1]
            self.run(name, "finish", self.at - 1)
        if self.at < len(self.steps):
            self.run(self.steps[self.at], "start", self.at)
        self.at += 1

    def run(self, name, action, index):
        if name[-1] in "012":
            getattr(self, name[:-1] + "_" + action)(int(name[-1]), index)
        else:
            getattr(self, name + "_" + action)(index)

    def wait_bytes(self, like, index):
        remote(like, like, self.send, self.recv.at[index], self.place.sibling()).wait()

    def base(self, part, steps):
        rows = self.mine + part * self.part
        if steps > 0:
            rows = rows + self.place.coord[AXIS_ORDER[part][0]] * self.first
        if steps > 1 and self.deep:
            rows = rows + self.place.coord[AXIS_ORDER[part][1]] * self.piece
        return pl.multiple_of(rows, 16)

    def block(self, part):
        return pl.ds(self.base(part, 2), self.piece)

    def core_copy(self, index):
        rows = pl.ds(pl.multiple_of(self.other, 16), self.half)
        return remote(
            self.batch.at[rows], self.from_core, self.send, self.recv.at[index], self.place.sibling()
        )

    def core_start(self, index):
        self.core_copy(index).start()

    def core_finish(self, index):
        self.core_copy(index).wait()
        size = self.half // 12

        def add(i, _):
            here = pl.ds(pl.multiple_of(self.mine + i * size, 16), size)
            there = pl.ds(pl.multiple_of(i * size, 16), size)
            self.batch[here] = (
                self.batch[here].astype(jnp.float32) + self.from_core[there].astype(jnp.float32)
            ).astype(jnp.bfloat16)
            return 0

        lax.fori_loop(0, 12, add, 0)

    def scatter_start(self, step, index):
        size = self.first if step == 0 else self.piece
        landing = self.from_first if step == 0 else self.from_second
        for part in range(3):
            axis = AXIS_ORDER[part][step]
            for distance in (1, 2, 3):
                target = self.place.next[axis][distance]
                rows = pl.multiple_of(self.base(part, step) + target * size, 16)
                remote(
                    self.batch.at[pl.ds(rows, size)],
                    landing.at[part, distance - 1],
                    self.send,
                    self.recv.at[index],
                    self.place.peer(axis, distance),
                ).start()

    def scatter_finish(self, step, index):
        size = self.first if step == 0 else self.piece
        landing = self.from_first if step == 0 else self.from_second
        self.wait_bytes(landing, index)
        for part in range(3):
            rows = pl.ds(self.base(part, step + 1), size)
            total = self.batch[rows].astype(jnp.float32)
            for distance in (1, 2, 3):
                total = total + landing[part, distance - 1].astype(jnp.float32)
            self.batch[rows] = total.astype(jnp.bfloat16)

    def exchange_start(self, step, index):
        landing = self.from_second if step == 1 else self.from_third
        for part in range(3):
            axis = AXIS_ORDER[part][step]
            for distance in (1, 2, 3):
                remote(
                    self.batch.at[self.block(part)],
                    landing.at[part, self.place.coord[axis]],
                    self.send,
                    self.recv.at[index],
                    self.place.peer(axis, distance),
                ).start()

    def exchange_finish(self, step, index):
        landing = self.from_second if step == 1 else self.from_third
        for part in range(3):
            landing[part, self.place.coord[AXIS_ORDER[part][step]]] = self.batch[self.block(part)]
        self.wait_bytes(self.from_second if self.deep else self.from_first, index)
        for part in range(3):
            terms = [landing[part, place].astype(jnp.float32) for place in range(4)]
            total = (terms[0] + terms[1]) + (terms[2] + terms[3])
            self.batch[self.block(part)] = total.astype(jnp.bfloat16)

    def local_copies(self):
        return [
            pltpu.make_async_copy(
                self.batch.at[self.block(part)],
                self.result.at[self.block(part)],
                self.local.at[part],
            )
            for part in range(3)
        ]

    def gather_start(self, step, index):
        from_batch = step == 1 or not self.deep
        size = self.first if step == 0 else self.piece
        if from_batch:
            for copy in self.local_copies():
                copy.start()
        source = self.batch if from_batch else self.result
        for part in range(3):
            axis = AXIS_ORDER[part][step]
            rows = pl.ds(self.base(part, step + 1), size)
            for distance in (1, 2, 3):
                remote(
                    source.at[rows],
                    self.result.at[rows],
                    self.send,
                    self.recv.at[index],
                    self.place.peer(axis, distance),
                ).start()

    def gather_finish(self, step, index):
        if step == 1 or not self.deep:
            for copy in self.local_copies():
                copy.wait()
        self.wait_bytes(self.from_first if step == 0 else self.from_second, index)

    def share_copy(self, index):
        rows = pl.ds(pl.multiple_of(self.mine, 16), self.half)
        return remote(
            self.result.at[rows],
            self.result.at[rows],
            self.send,
            self.recv.at[index],
            self.place.sibling(),
        )

    def share_start(self, index):
        self.share_copy(index).start()

    def share_finish(self, index):
        self.share_copy(index).wait()


class ExtraReduction:
    def __init__(self, place, rows_ref, result, refs):
        self.place = place
        self.ref = rows_ref
        self.result = result
        self.from_core, self.from_x, self.from_plane, self.send, self.recv = refs
        self.mine = place.core * EXTRA_HALF
        self.other = (1 - place.core) * EXTRA_HALF
        self.at = 0
        self.last = 6

    def scratch():
        return [
            pltpu.VMEM((EXTRA_HALF, 128), jnp.float32),
            pltpu.VMEM((3, EXTRA_PIECE, 128), jnp.float32),
            pltpu.VMEM((2, 4, EXTRA_PIECE, 128), jnp.float32),
            pltpu.SemaphoreType.DMA,
            pltpu.SemaphoreType.DMA((6,)),
        ]

    def advance(self):
        if self.at > 0:
            self.finish(self.at - 1)
        if self.at < 6:
            self.start(self.at)
        self.at += 1

    def piece(self, quarter):
        return pl.ds(pl.multiple_of(self.mine + quarter * EXTRA_PIECE, 8), EXTRA_PIECE)

    def copy(self, index, source, target, device):
        return remote(source, target, self.send, self.recv.at[index], device)

    def core_copy(self):
        rows = pl.ds(pl.multiple_of(self.other, 8), EXTRA_HALF)
        return self.copy(0, self.ref.at[rows], self.from_core, self.place.sibling())

    def share_copy(self):
        rows = pl.ds(pl.multiple_of(self.mine, 8), EXTRA_HALF)
        return self.copy(5, self.result.at[rows], self.result.at[rows], self.place.sibling())

    def start(self, index):
        rows = self.piece(self.place.coord[0])
        if index == 0:
            self.core_copy().start()
            return
        if index == 5:
            self.share_copy().start()
            return
        for distance in (1, 2, 3):
            if index == 1:
                target = self.place.next[0][distance]
                source, target, axis = self.ref.at[self.piece(target)], self.from_x.at[distance - 1], 0
            elif index == 4:
                source, target, axis = self.result.at[rows], self.result.at[rows], 0
            else:
                axis = index - 1
                source = self.ref.at[rows]
                target = self.from_plane.at[axis - 1, self.place.coord[axis]]
            self.copy(index, source, target, self.place.peer(axis, distance)).start()

    def finish(self, index):
        rows = self.piece(self.place.coord[0])
        if index == 0:
            self.core_copy().wait()
            half = pl.ds(pl.multiple_of(self.mine, 8), EXTRA_HALF)
            self.ref[half] = self.ref[half] + self.from_core[...]
            return
        if index == 5:
            self.share_copy().wait()
            return
        if index in (2, 3):
            self.from_plane[index - 2, self.place.coord[index - 1]] = self.ref[rows]
        self.copy(index, self.from_x, self.from_x, self.place.sibling()).wait()
        if index == 1:
            self.ref[rows] = self.ref[rows] + self.from_x[0] + self.from_x[1] + self.from_x[2]
        elif index in (2, 3):
            terms = [self.from_plane[index - 2, place] for place in range(4)]
            target = self.ref if index == 2 else self.result
            target[rows] = (terms[0] + terms[1]) + (terms[2] + terms[3])


ROWS = 512
SLOT = 256
KEYS = 768
GENES = 1024
GENE_ROWS = 480
PAIRS = 4
GROUPS = ((0, 2), (2, 4))
PLAN = {
    "one pair 1": ("one_a",),
    "one keys": ("one_a",),
    "zero dense": ("one_b", "one_a"),
    "zero pair 1": ("zero_a",),
    "zero pair 2": ("one_b", "one_a"),
    "zero queries": ("first",),
    "zero merge": ("zero_a",),
    "zero values": ("one_b", "one_a"),
    "genes": ("last", "first"),
    "hidden": ("zero_a",),
}
ENDING = (
    "more", "one_b", "one_a", "first", "more", "zero_a",
    "one_a", "last", "one_b", "first", "more", "last",
    "zero_a", "first", "more", "one_b", "last", "one_b",
    "more", "first", "last", "zero_a", "more", "first",
    "zero_a", "last", "last",
)
NEG = -1e30
SCORE_SCALE = 0.125
NN = (((1,), (0,)), ((), ()))
NT = (((1,), (1,)), ((), ()))
TN = (((0,), (0,)), ((), ()))


def dot(left, right, dims):
    return lax.dot_general(left, right, dims, preferred_element_type=jnp.float32)


def low(values):
    return values.astype(jnp.bfloat16)


def wide(values):
    return values.astype(jnp.float32)


def lane(shape):
    return lax.broadcasted_iota(jnp.int32, shape, 1)


def normalize(values):
    center = values - jnp.mean(values, axis=1, keepdims=True)
    root = lax.rsqrt(jnp.mean(center * center, axis=1, keepdims=True) + 1e-05)
    return center * root, root


def norm_back(grad, gain, normal, root):
    u = grad * gain
    mean = jnp.mean(u, axis=1, keepdims=True)
    along = jnp.mean(u * normal, axis=1, keepdims=True)
    return (u - mean - normal * along) * root


def column_sum(values):
    return jnp.sum(values, axis=0, keepdims=True)


def split_three(values):
    first = low(values)
    rest = values - wide(first)
    second = low(rest)
    third = low(rest - wide(second))
    return first, second, third


def model_kernel(
    hidden_in,
    cotangent,
    ids_in,
    unknown,
    table,
    w_inputs,
    w_output,
    w_up,
    w_down,
    b_query,
    b_value,
    b_output,
    gain_one,
    shift_one,
    b_up,
    b_down,
    gain_two,
    shift_two,
    layer_out,
    grad_hidden,
    reduced,
    extra_out,
    kept_probs,
    hidden,
    ids,
    win,
    wout,
    wup,
    wdown,
    stream,
    x_round,
    queries,
    keys,
    values,
    probs,
    stats,
    inverses,
    self_parts,
    mixed,
    normal_one,
    normal_two,
    slope,
    active,
    d_mixed,
    d_packed,
    d_keys,
    d_values,
    part_keys,
    part_values,
    sent,
    received,
    bias,
    vectors,
    out_round,
    extra,
    batch_a,
    batch_b,
    batch_c,
    batch_d,
    extra_result,
    load_sems,
    swap_send,
    swap_recv,
    kv_send,
    kv_recv,
    grad_send,
    grad_recv,
    probs_sem,
    out_sems,
    *reduction_refs,
):
    place = Place()
    cot = d_mixed
    core, here = place.core, place.x_hi
    there = 1 - here
    partner = place.peer(0, 2)
    sibling = place.sibling()

    def slot_rows(slot):
        return pl.ds(pl.multiple_of(slot * SLOT, SLOT), SLOT)

    def block_rows(slot, which):
        return pl.ds(pl.multiple_of((2 * slot + which) * SLOT, SLOT), SLOT)

    load_hidden = pltpu.make_async_copy(
        hidden_in.at[here], hidden.at[slot_rows(here)], load_sems.at[0]
    )
    load_cot = pltpu.make_async_copy(cotangent.at[here], cot.at[slot_rows(here)], load_sems.at[1])
    loads = []
    for layer in range(2):
        for index, (source, target) in enumerate(
            ((w_inputs, win), (w_output, wout), (w_up, wup), (w_down, wdown))
        ):
            loads.append(
                pltpu.make_async_copy(
                    source.at[layer],
                    target.at[layer],
                    load_sems.at[4 if layer == 1 else 2 if index == 0 else 3],
                )
            )
    load_hidden.start()
    for load in loads[0:4]:
        load.start()
    wait_rest = pltpu.make_async_copy(w_inputs.at[0], win.at[0], load_sems.at[3])
    wait_next = pltpu.make_async_copy(w_inputs, win, load_sems.at[4])
    for cell in range(2):
        ids[cell] = jnp.broadcast_to(ids_in[cell : cell + 1, :], (8, SLOT))
    known = GENES - unknown[here]

    greet(place)

    swap_hidden = remote(
        hidden_in.at[there],
        hidden.at[slot_rows(here)],
        swap_send.at[0],
        swap_recv.at[0],
        partner,
    )
    swap_ids = remote(ids.at[there], ids.at[2], swap_send.at[1], swap_recv.at[1], partner)
    swap_cot = remote(
        cotangent.at[there],
        cot.at[slot_rows(here)],
        swap_send.at[2],
        swap_recv.at[2],
        partner,
    )
    swap_ids.start()
    swap_hidden.start()

    bias[...] = jnp.where(lane((8, KEYS)) < known, 0.0, NEG)
    for slot in range(2):
        position = (2 * slot + core) * SLOT + lax.broadcasted_iota(jnp.int32, (SLOT, 128), 0)
        stats[slot * SLOT : (slot + 1) * SLOT, :] = jnp.where(position >= known, 0.0, NEG)
    part_keys[KEYS:GENES, :] = jnp.zeros((GENES - KEYS, 128), jnp.float32)
    part_values[KEYS:GENES, :] = jnp.zeros((GENES - KEYS, 128), jnp.float32)
    vectors[...] = jnp.zeros_like(vectors)
    extra[...] = jnp.zeros_like(extra)

    def slot_ids(slot):
        row = jnp.where(slot == here, ids[here, 0:1, :], ids[2, 0:1, :])
        high = lax.shift_right_logical(row, 7)
        lowest = lax.bitwise_and(row, 127)
        is_high = lax.broadcasted_iota(jnp.int32, (GENE_ROWS, SLOT), 0) == high
        is_low = lax.broadcasted_iota(jnp.int32, (128, SLOT), 0) == lowest
        return low(jnp.where(is_high, 1.0, 0.0)), is_low

    def gather_scale(slot):
        is_high, is_low = slot_ids(slot)
        total = jnp.zeros((128, SLOT), jnp.float32)
        for piece in split_three(table[...]):
            total = total + dot(piece, is_high, TN)
        row = column_sum(jnp.where(is_low, total, 0.0))
        put_column(slot_rows(slot), 5, jnp.transpose(jnp.broadcast_to(row, (128, SLOT))))

    def put_column(rows, at, column):
        stats[rows, :] = jnp.where(lane((SLOT, 128)) == at, column, stats[rows, :])

    def get_column(rows, at):
        return stats[rows, :][:, at : at + 1]

    def vector(ref, layer):
        return ref[pl.ds(layer, 1), :]

    def kv_copies(layer, slot):
        rows = block_rows(slot, core)
        return [
            remote(
                ref.at[layer, rows],
                ref.at[layer, rows],
                kv_send,
                kv_recv.at[layer],
                sibling,
            )
            for ref in (keys, values)
        ]

    def project_keys(layer, slot):
        rows = slot_rows(slot)
        if layer == 0:
            stream[rows, :] = wide(hidden[rows, :]) * get_column(rows, 5)
        x_b = low(stream[rows, :])
        x_round[layer, rows, :] = x_b
        weights = win.at[layer]
        mine = block_rows(slot, core)
        keys[layer, mine, :] = low(dot(x_b, weights[:, 512:1024], NN))
        values[layer, mine, :] = low(
            dot(x_b, weights[:, 1024:1536], NN) + vector(b_value, layer)
        )
        for copy in kv_copies(layer, slot):
            copy.start()

    def project_queries(layer):
        query = dot(x_round[layer], win[layer, :, 0:512], NN) + vector(b_query, layer)
        queries[layer] = low(wide(low(query)) * SCORE_SCALE)

    def own(ref, layer, columns):
        return jnp.concatenate(
            [ref[layer, block_rows(slot, core), columns] for slot in range(2)], axis=0
        )

    def attend(layer):
        first_half = lane((ROWS, 128)) < 64
        first_keys = lane((KEYS, 128)) < 64

        for pair in range(PAIRS):
            columns = slice(pair * 128, (pair + 1) * 128)
            q_pair = queries[layer, :, columns]
            k_pair = keys[layer, 0:KEYS, columns]
            v_pair = values[layer, 0:KEYS, columns]
            product = wide(q_pair) * wide(own(keys, layer, columns))
            found, self_terms = [], []
            for half in range(2):
                inside = first_half if half == 0 else jnp.logical_not(first_half)
                self_score = (
                    jnp.sum(jnp.where(inside, product, 0.0), axis=1, keepdims=True)
                    + stats[:, 0:1]
                )
                scores = dot(jnp.where(inside, q_pair, jnp.zeros_like(q_pair)), k_pair, NT)
                scores = scores + bias[0:1, :]
                top = jnp.maximum(jnp.max(scores, axis=1, keepdims=True), self_score)
                exponent = low(jnp.exp(scores - top))
                probs[2 * pair + half] = exponent
                with_ones = jnp.where(
                    first_keys if half == 0 else jnp.logical_not(first_keys),
                    v_pair,
                    jnp.ones_like(v_pair),
                )
                found.append(dot(exponent, with_ones, NN))
                self_terms.append(jnp.exp(self_score - top))
            self_low = low(jnp.where(first_half, self_terms[0], self_terms[1]))
            self_term = wide(self_low)
            sums = pltpu.roll(jnp.where(first_half, found[1], found[0]), 64, 1)
            inverse = 1.0 / (sums + self_term)
            total = jnp.where(first_half, found[0], found[1])
            total = total + self_term * wide(own(values, layer, columns))
            mixed[layer, :, columns] = total * inverse
            inverses[layer, :, columns] = inverse
            self_parts[layer, :, columns] = self_low

    def dense_forward(layer, slot):
        rows = slot_rows(slot)
        mixed_b = low(mixed[layer, rows, :])
        first = stream[rows, :] + (dot(mixed_b, wout[layer], NN) + vector(b_output, layer))
        normal, root = normalize(first)
        normal_one[layer, rows, :] = normal
        put_column(rows, 1 + 2 * layer, root)
        normed = normal * vector(gain_one, layer) + vector(shift_one, layer)
        inner = dot(low(normed), wup[layer], NN) + vector(b_up, layer)
        share = 0.5 * (1.0 + lax.erf(inner * 0.7071067811865476))
        slope[layer, rows, :] = share + inner * (
            0.3989422804014327 * jnp.exp(inner * inner * -0.5)
        )
        active_b = low(inner * share)
        active[layer, rows, :] = active_b
        second = normed + (dot(active_b, wdown[layer], NN) + vector(b_down, layer))
        normal, root = normalize(second)
        normal_two[layer, rows, :] = normal
        put_column(rows, 2 + 2 * layer, root)
        stream[rows, :] = normal * vector(gain_two, layer) + vector(shift_two, layer)

    def add_vector(member, layer, row):
        at = 2 * member + layer
        vectors[at : at + 1, :] = vectors[at : at + 1, :] + row

    def dense_backward(layer, slot):
        rows = slot_rows(slot)
        grad = stream[rows, :]
        normal = normal_two[layer, rows, :]
        add_vector(7, layer, column_sum(grad * normal))
        add_vector(8, layer, column_sum(grad))
        root = get_column(rows, 2 + 2 * layer)
        d_second = norm_back(grad, vector(gain_two, layer), normal, root)
        d_branch = low(d_second)
        d_packed[rows, 0:512] = d_branch
        add_vector(6, layer, column_sum(wide(d_branch)))
        d_inner = low(dot(d_branch, wdown[layer], NT) * slope[layer, rows, :])
        d_packed[rows, 512:1024] = d_inner
        add_vector(5, layer, column_sum(wide(d_inner)))
        d_normed = d_second + dot(d_inner, wup[layer], NT)
        normal = normal_one[layer, rows, :]
        add_vector(3, layer, column_sum(d_normed * normal))
        add_vector(4, layer, column_sum(d_normed))
        root = get_column(rows, 1 + 2 * layer)
        first = norm_back(d_normed, vector(gain_one, layer), normal, root)
        stream[rows, :] = first
        d_attn = low(first)
        d_packed[rows, 1024:1536] = d_attn
        add_vector(2, layer, column_sum(wide(d_attn)))
        d_mixed[rows, :] = low(dot(d_attn, wout[layer], NT))

    def put_tiles(batch, first_tile, matrix):
        for tile in range(4):
            at = (first_tile + tile) * 512
            batch[at : at + 512, :] = low(matrix[:, tile * 128 : (tile + 1) * 128])

    def dense_weights(layer, batch):
        put_tiles(batch, 0, dot(active[layer], d_packed[:, 0:512], TN))
        normed = normal_one[layer] * vector(gain_one, layer) + vector(shift_one, layer)
        put_tiles(batch, 4, dot(low(normed), d_packed[:, 512:1024], TN))
        put_tiles(batch, 8, dot(low(mixed[layer]), d_packed[:, 1024:1536], TN))

    def grad_copy(pair):
        return remote(
            sent.at[pair], received.at[pair], grad_send, grad_recv.at[pair], sibling
        )

    def attend_backward(layer, first_pair, last_pair):
        first_half = lane((ROWS, 128)) < 64

        for pair in range(first_pair, last_pair):
            columns = slice(pair * 128, (pair + 1) * 128)
            q_pair = queries[layer, :, columns]
            k_pair = keys[layer, 0:KEYS, columns]
            v_pair = values[layer, 0:KEYS, columns]
            d_out = low(wide(d_mixed[:, columns]) * inverses[layer, :, columns])
            d_wide = wide(d_out)
            d_turned = jnp.transpose(d_out)
            q_turned = jnp.transpose(q_pair)
            with_out = mixed[layer, :, columns] * d_wide
            with_own = wide(own(values, layer, columns)) * d_wide - with_out
            d_q, d_k, d_v, self_score, delta, d_probs = [], [], [], [], [], []
            for half in range(2):
                inside = first_half if half == 0 else jnp.logical_not(first_half)
                delta.append(jnp.sum(jnp.where(inside, with_out, 0.0), axis=1, keepdims=True))
                self_score.append(jnp.sum(jnp.where(inside, with_own, 0.0), axis=1, keepdims=True))
                d_probs.append(
                    dot(jnp.where(inside, d_out, jnp.zeros_like(d_out)), v_pair, NT)
                )
            for half in range(2):
                exponent = probs[2 * pair + half]
                d_scores = low(wide(exponent) * (d_probs[half] - delta[half]))
                d_q.append(dot(d_scores, k_pair, NN))
                d_k.append(dot(q_turned, d_scores, NN))
                d_v.append(dot(d_turned, exponent, NN))
            self_term = wide(self_parts[layer, :, columns])
            own_score = self_term * jnp.where(first_half, self_score[0], self_score[1])
            d_query = jnp.where(first_half, d_q[0], d_q[1]) + own_score * wide(
                own(keys, layer, columns)
            )
            d_packed[:, columns] = low(d_query * SCORE_SCALE)
            part_keys[0:KEYS, :] = jnp.transpose(
                jnp.concatenate([d_k[0][0:64], d_k[1][64:128]], axis=0)
            )
            part_values[0:KEYS, :] = jnp.transpose(
                jnp.concatenate([d_v[0][0:64], d_v[1][64:128]], axis=0)
            )
            own_keys = own_score * wide(q_pair)
            own_values = self_term * d_wide
            for slot in range(2):
                rows = slice(slot * SLOT, (slot + 1) * SLOT)
                mine = block_rows(slot, core)
                d_keys[rows, columns] = part_keys[mine, :] + own_keys[rows, :]
                d_values[rows, columns] = part_values[mine, :] + own_values[rows, :]
                other = block_rows(slot, 1 - core)
                sent[pair, 0, rows, :] = low(part_keys[other, :])
                sent[pair, 1, rows, :] = low(part_values[other, :])
            grad_copy(pair).start()

    def merge_grads(pairs):
        for pair in range(*pairs):
            grad_copy(pair).wait_recv()
            at = pair * 128
            columns = slice(at, at + 128)
            d_packed[:, 512 + at : 640 + at] = low(d_keys[:, columns] + wide(received[pair, 0]))
            d_packed[:, 1024 + at : 1152 + at] = low(d_values[:, columns] + wide(received[pair, 1]))

    def wait_sent():
        remote(sent, sent, grad_send, grad_recv.at[0], sibling).wait_send()

    def input_weights(layer, batch, first_row, third, pairs):
        first, last = pairs
        count = last - first
        columns = slice(third * 512 + first * 128, third * 512 + last * 128)
        product = dot(x_round[layer], d_packed[:, columns], TN)
        for tile in range(count):
            at = first_row + (third * count + tile) * 512
            batch[at : at + 512, :] = low(product[:, tile * 128 : (tile + 1) * 128])
        if third != 1:
            at = 2 * (third // 2) + layer
            inside = slice(first * 128, last * 128)
            vectors[at : at + 1, inside] = column_sum(wide(d_packed[:, columns]))

    def input_grad(layer, slot):
        rows = slot_rows(slot)
        stream[rows, :] = stream[rows, :] + dot(d_packed[rows, :], win[layer], NT)

    def reduction(index, batch, result, rows, deep):
        return Reduction(
            place, batch, result, rows, deep, reduction_refs[7 * index : 7 * index + 7]
        )

    group_rows = [1536 * (last - first) for first, last in GROUPS]
    group_at = [sum(group_rows[:index]) for index in range(len(GROUPS))]
    one_a = reduction(0, batch_a, reduced.at[0], BATCH_ROWS, True)
    one_b = reduction(1, batch_b, reduced.at[1], BATCH_ROWS, True)
    zero_a = reduction(2, batch_c, reduced.at[2], BATCH_ROWS, True)
    groups = [
        reduction(
            3 + index,
            batch_d.at[pl.ds(at, rows)],
            reduced.at[3, pl.ds(at, rows)],
            rows,
            True,
        )
        for index, (at, rows) in enumerate(zip(group_at, group_rows))
    ]
    more = ExtraReduction(place, extra, extra_result, reduction_refs[7 * (3 + len(GROUPS)) :])
    running = {
        "one_a": one_a,
        "one_b": one_b,
        "zero_a": zero_a,
        "first": groups[0],
        "last": groups[1],
        "more": more,
    }

    def both_slots(work):
        def step(slot, _):
            work(slot)
            return 0

        lax.fori_loop(0, 2, step, 0)

    def after(piece):
        for name in PLAN.get(piece, ()):
            running[name].advance()

    load_hidden.wait()
    gather_scale(here)
    loads[0].wait()
    project_keys(0, here)
    swap_ids.wait()
    gather_scale(there)
    swap_hidden.wait()
    project_keys(0, there)
    project_queries(0)
    swap_cot.start()
    load_cot.start()
    for load in loads[4:]:
        load.start()
    probs_out = pltpu.make_async_copy(probs, kept_probs, probs_sem.at[0])
    probs_back = pltpu.make_async_copy(kept_probs, probs, probs_sem.at[1])

    def forward(layer, _):
        whole = keys.at[layer]
        remote(whole, whole, kv_send, kv_recv.at[layer], sibling).wait()

        @pl.when(layer == 1)
        def _():
            probs_out.wait()

        attend(layer)

        @pl.when(layer == 0)
        def _():
            probs_out.start()
            wait_rest.wait()
            wait_next.wait()

        def forward_slot(slot, _):
            dense_forward(layer, slot)

            @pl.when(layer == 0)
            def _():
                project_keys(1, slot)

            return 0

        lax.fori_loop(0, 2, forward_slot, 0)

        @pl.when(layer == 0)
        def _():
            project_queries(1)

        return 0

    lax.fori_loop(0, 2, forward, 0)

    out_round[...] = low(stream[...])
    keep_out = pltpu.make_async_copy(
        out_round.at[slot_rows(here)], layer_out.at[here], out_sems.at[0]
    )
    send_out = remote(
        out_round.at[slot_rows(there)],
        layer_out.at[here],
        swap_send.at[3],
        swap_recv.at[3],
        partner,
    )
    keep_out.start()
    send_out.start()

    load_cot.wait()
    swap_cot.wait()
    stream[...] = wide(cot[...])
    every = (0, PAIRS)
    both_slots(lambda slot: dense_backward(1, slot))
    dense_weights(1, batch_a)
    one_a.advance()
    for pair in range(PAIRS):
        attend_backward(1, pair, pair + 1)
        after(f"one pair {pair}")
    probs_back.start()
    input_weights(1, batch_b, 0, 0, every)
    after("one queries")
    merge_grads(every)
    after("one merge")
    input_weights(1, batch_b, 0, 1, every)
    after("one keys")
    input_weights(1, batch_b, 0, 2, every)
    one_b.advance()
    both_slots(lambda slot: input_grad(1, slot))
    after("one input")
    both_slots(lambda slot: dense_backward(0, slot))
    after("zero dense")
    dense_weights(0, batch_c)
    zero_a.advance()
    wait_sent()
    probs_back.wait()
    for pair in range(PAIRS):
        attend_backward(0, pair, pair + 1)
        after(f"zero pair {pair}")
        if pair == GROUPS[0][1]:
            merge_grads(GROUPS[0])
            for third in range(3):
                input_weights(0, batch_d, group_at[0], third, GROUPS[0])
            groups[0].advance()
    input_weights(0, batch_d, group_at[1], 0, GROUPS[1])
    after("zero queries")
    merge_grads(GROUPS[1])
    after("zero merge")
    for third in (1, 2):
        input_weights(0, batch_d, group_at[1], third, GROUPS[1])
    groups[1].advance()
    after("zero values")
    both_slots(lambda slot: input_grad(0, slot))
    after("zero input")

    genes = jnp.zeros((GENE_ROWS, 128), jnp.float32)
    for slot in range(2):
        rows = slot_rows(slot)
        is_high, is_low = slot_ids(slot)
        per_token = jnp.sum(stream[rows, :] * wide(hidden[rows, :]), axis=1, keepdims=True)
        row = jnp.transpose(jnp.broadcast_to(per_token, (SLOT, 128)))
        for piece in split_three(jnp.where(is_low, row, 0.0)):
            genes = genes + dot(is_high, piece, NT)
    extra[0:GENE_ROWS, :] = genes
    for index in range(18):
        for tile in range(4):
            at = GENE_ROWS + 4 * index + tile
            extra[at : at + 1, :] = vectors[index : index + 1, tile * 128 : (tile + 1) * 128]
    after("genes")
    more.advance()
    for slot in range(2):
        rows = slot_rows(slot)
        d_mixed[rows, :] = low(stream[rows, :] * get_column(rows, 5))
    keep_grad = pltpu.make_async_copy(
        d_mixed.at[slot_rows(here)], grad_hidden.at[here], out_sems.at[1]
    )
    send_grad = remote(
        d_mixed.at[slot_rows(there)],
        grad_hidden.at[here],
        swap_send.at[4],
        swap_recv.at[4],
        partner,
    )
    keep_grad.start()
    send_grad.start()
    after("hidden")
    for name in ENDING:
        running[name].advance()
        if name == "more" and more.at == 7:
            extra_copy = pltpu.make_async_copy(extra_result, extra_out, out_sems.at[2])
            extra_copy.start()
    for one in running.values():
        assert one.at == one.last + 1
    wait_sent()
    keep_out.wait()
    send_out.wait()
    keep_grad.wait()
    send_grad.wait()
    extra_copy.wait()


def run_model(hidden_in, cotangent, gene_ids, unknown_count, table, weights, vector_args):
    f32, bf16 = jnp.float32, jnp.bfloat16
    vmem = pl.BlockSpec(memory_space=pltpu.VMEM)
    smem = pl.BlockSpec(memory_space=pltpu.SMEM)
    anywhere = pl.BlockSpec(memory_space=pl.ANY)
    scratch = [
        pltpu.VMEM((ROWS, 512), bf16),
        pltpu.VMEM((3, 8, SLOT), jnp.int32),
        pltpu.VMEM((2, 512, 1536), bf16),
        pltpu.VMEM((2, 512, 512), bf16),
        pltpu.VMEM((2, 512, 512), bf16),
        pltpu.VMEM((2, 512, 512), bf16),
        pltpu.VMEM((ROWS, 512), f32),
        pltpu.VMEM((2, ROWS, 512), bf16),
        pltpu.VMEM((2, ROWS, 512), bf16),
        pltpu.VMEM((2, GENES, 512), bf16),
        pltpu.VMEM((2, GENES, 512), bf16),
        pltpu.VMEM((HEADS, ROWS, KEYS), bf16),
        pltpu.VMEM((ROWS, 128), f32),
        pltpu.VMEM((2, ROWS, 512), f32),
        pltpu.VMEM((2, ROWS, 512), bf16),
        pltpu.VMEM((2, ROWS, 512), f32),
        pltpu.VMEM((2, ROWS, 512), f32),
        pltpu.VMEM((2, ROWS, 512), f32),
        pltpu.VMEM((2, ROWS, 512), f32),
        pltpu.VMEM((2, ROWS, 512), bf16),
        pltpu.VMEM((ROWS, 512), bf16),
        pltpu.VMEM((ROWS, 1536), bf16),
        pltpu.VMEM((ROWS, 512), f32),
        pltpu.VMEM((ROWS, 512), f32),
        pltpu.VMEM((GENES, 128), f32),
        pltpu.VMEM((GENES, 128), f32),
        pltpu.VMEM((PAIRS, 2, ROWS, 128), bf16),
        pltpu.VMEM((PAIRS, 2, ROWS, 128), bf16),
        pltpu.VMEM((8, KEYS), f32),
        pltpu.VMEM((24, 512), f32),
        pltpu.VMEM((ROWS, 512), bf16),
        pltpu.VMEM((EXTRA_ROWS, 128), f32),
        pltpu.VMEM((BATCH_ROWS, 128), bf16),
        pltpu.VMEM((BATCH_ROWS, 128), bf16),
        pltpu.VMEM((BATCH_ROWS, 128), bf16),
        pltpu.VMEM((BATCH_ROWS, 128), bf16),
        pltpu.VMEM((EXTRA_ROWS, 128), f32),
        pltpu.SemaphoreType.DMA((5,)),
        pltpu.SemaphoreType.DMA((5,)),
        pltpu.SemaphoreType.DMA((5,)),
        pltpu.SemaphoreType.DMA,
        pltpu.SemaphoreType.DMA((2,)),
        pltpu.SemaphoreType.DMA,
        pltpu.SemaphoreType.DMA((PAIRS,)),
        pltpu.SemaphoreType.DMA((2,)),
        pltpu.SemaphoreType.DMA((3,)),
    ]
    for _ in range(3):
        scratch += Reduction.scratch(BATCH_ROWS, True)
    for first, last in GROUPS:
        scratch += Reduction.scratch(1536 * (last - first), True)
    scratch += ExtraReduction.scratch()
    outs = (
        jax.ShapeDtypeStruct((2, SLOT, 512), bf16),
        jax.ShapeDtypeStruct((2, SLOT, 512), bf16),
        jax.ShapeDtypeStruct((4, BATCH_ROWS, 128), bf16),
        jax.ShapeDtypeStruct((EXTRA_ROWS, 128), f32),
        jax.ShapeDtypeStruct((HEADS, ROWS, KEYS), bf16),
    )
    return pl.pallas_call(
        model_kernel,
        out_shape=outs,
        in_specs=[anywhere, anywhere, vmem, smem, vmem] + [anywhere] * 4 + [vmem] * 9,
        out_specs=(anywhere,) * 5,
        scratch_shapes=scratch,
        compiler_params=pltpu.CompilerParams(
            collective_id=0, has_side_effects=True, vmem_limit_bytes=63 << 20
        ),
        name="model",
    )(hidden_in, cotangent, gene_ids, unknown_count, table, *weights, *vector_args)


def finish_kernel(layer_in, hidden_grad_in, reduced, extra, *refs):
    layer_out, hidden_out, g_inputs, g_output, g_up, g_down, genes = refs[:7]
    vector_outs = refs[7:16]
    rounded, narrow, rows_out, wide_in, wide_rest, extra_rows, in_sems, out_sems = refs[16:]
    sources = [layer_in, hidden_grad_in]
    loads = [
        pltpu.make_async_copy(sources[i], rounded.at[i], in_sems.at[i]) for i in range(2)
    ] + [pltpu.make_async_copy(reduced.at[i], narrow.at[i], in_sems.at[2 + i]) for i in range(4)]
    loads.append(pltpu.make_async_copy(extra, extra_rows, in_sems.at[6]))
    for load in loads[:1] + loads[6:] + loads[1:6]:
        load.start()
    stores = []

    def send(source, target):
        store = pltpu.make_async_copy(source, target, out_sems.at[len(stores)])
        store.start()
        stores.append(store)

    for index, target in enumerate((layer_out, hidden_out)):
        loads[index].wait()
        rows_out[index] = wide(rounded[index])
        send(rows_out.at[index], target)
    for layer in (1, 0):
        base = 2 * (1 - layer)
        loads[2 + base].wait()
        for index, target in enumerate((g_down, g_up, g_output)):
            for tile in range(4):
                at = (4 * index + tile) * 512
                wide_rest[layer, index, :, tile * 128 : (tile + 1) * 128] = wide(
                    narrow[base, at : at + 512, :]
                )
            send(wide_rest.at[layer, index], target.at[layer])
        loads[3 + base].wait()
        at = 0
        for first, last in GROUPS if layer == 0 else ((0, PAIRS),):
            for third in range(3):
                for pair in range(first, last):
                    column = third * 512 + pair * 128
                    wide_in[layer, :, column : column + 128] = wide(
                        narrow[base + 1, at : at + 512, :]
                    )
                    at += 512
        send(wide_in.at[layer], g_inputs.at[layer])
    loads[6].wait()
    genes[...] = extra_rows[0:GENE_ROWS, :]
    for member in range(9):
        for layer in range(2):
            for tile in range(4):
                at = GENE_ROWS + 4 * (2 * member + layer) + tile
                vector_outs[member][layer : layer + 1, tile * 128 : (tile + 1) * 128] = extra_rows[
                    at : at + 1, :
                ]
    for store in stores:
        store.wait()


def finish(layer_out, grad_hidden, reduced, extra):
    f32, bf16 = jnp.float32, jnp.bfloat16
    vmem = pl.BlockSpec(memory_space=pltpu.VMEM)
    anywhere = pl.BlockSpec(memory_space=pl.ANY)
    outs = [
        jax.ShapeDtypeStruct((2, SLOT, 512), f32),
        jax.ShapeDtypeStruct((2, SLOT, 512), f32),
        jax.ShapeDtypeStruct((2, 512, 1536), f32),
        jax.ShapeDtypeStruct((2, 512, 512), f32),
        jax.ShapeDtypeStruct((2, 512, 512), f32),
        jax.ShapeDtypeStruct((2, 512, 512), f32),
        jax.ShapeDtypeStruct((GENE_ROWS, 128), f32),
    ] + [jax.ShapeDtypeStruct((2, 512), f32)] * 9
    return pl.pallas_call(
        finish_kernel,
        out_shape=outs,
        in_specs=[anywhere] * 4,
        out_specs=[anywhere] * 6 + [vmem] * 10,
        scratch_shapes=[
            pltpu.VMEM((2, 2, SLOT, 512), bf16),
            pltpu.VMEM((4, BATCH_ROWS, 128), bf16),
            pltpu.VMEM((2, 2, SLOT, 512), f32),
            pltpu.VMEM((2, 512, 1536), f32),
            pltpu.VMEM((2, 3, 512, 512), f32),
            pltpu.VMEM((EXTRA_ROWS, 128), f32),
            pltpu.SemaphoreType.DMA((7,)),
            pltpu.SemaphoreType.DMA((10,)),
        ],
        compiler_params=pltpu.CompilerParams(vmem_limit_bytes=63 << 20),
        name="finish",
    )(layer_out, grad_hidden, reduced, extra)


def shards(
    hidden_in,
    gene_ids,
    unknown_count,
    gene_scale,
    w_inputs,
    b_query,
    b_value,
    w_output,
    b_output,
    gain_one,
    shift_one,
    w_up,
    b_up,
    w_down,
    b_down,
    gain_two,
    shift_two,
    cotangent,
):
    gene_count = gene_scale.shape[0]
    table = jnp.pad(gene_scale, (0, GENE_ROWS * 128 - gene_count)).reshape(GENE_ROWS, 128)
    layer_out, grad_hidden, reduced, extra, _ = run_model(
        hidden_in,
        cotangent,
        gene_ids,
        unknown_count,
        table,
        (w_inputs, w_output, w_up, w_down),
        (b_query, b_value, b_output, gain_one, shift_one, b_up, b_down, gain_two, shift_two),
    )
    (
        layer_out,
        grad_hidden,
        g_inputs,
        g_output,
        g_up,
        g_down,
        genes,
        g_b_query,
        g_b_value,
        g_b_output,
        g_gain_one,
        g_shift_one,
        g_b_up,
        g_b_down,
        g_gain_two,
        g_shift_two,
    ) = finish(layer_out, grad_hidden, reduced, extra)
    return (
        layer_out,
        grad_hidden,
        genes.reshape(-1)[:gene_count],
        g_inputs,
        g_b_query,
        g_b_value,
        g_output,
        g_b_output,
        g_gain_one,
        g_shift_one,
        g_up,
        g_b_up,
        g_down,
        g_b_down,
        g_gain_two,
        g_shift_two,
    )


def solution(mesh):
    placed = (
        P("dp", "blk", None),
        P("dp", "blk"),
        P("dp"),
        P(),
        P(),
        P(),
        P(),
        P(),
        P(),
        P(),
        P(),
        P(),
        P(),
        P(),
        P(),
        P(),
        P(),
        P("dp", "blk", None),
    )
    return jax.shard_map(
        shards,
        mesh=mesh,
        in_specs=placed,
        out_specs=(
            P("dp", "blk", None),
            P("dp", "blk", None),
            P(),
            P(),
            P(),
            P(),
            P(),
            P(),
            P(),
            P(),
            P(),
            P(),
            P(),
            P(),
            P(),
            P(),
        ),
        check_vma=False,
    )
```

```python
import jax
import jax.numpy as jnp
from jax import lax
from jax.experimental import pallas as pl
from jax.experimental.pallas import tpu as pltpu
from jax.sharding import PartitionSpec as P

HEADS = 8
MESH = pl.DeviceIdType.MESH
AXIS_ORDER = ((0, 1, 2), (1, 2, 0), (2, 0, 1))
BATCH_ROWS = 6144
EXTRA_ROWS = 576
EXTRA_HALF = EXTRA_ROWS // 2
EXTRA_PIECE = EXTRA_HALF // 4


class Place:
    def __init__(self):
        dp = lax.axis_index("dp")
        blk = lax.axis_index("blk")
        self.core = blk & 1
        self.x_hi = blk >> 1
        self.coord = (self.x_hi * 2 + (dp & 1), dp >> 3, (dp >> 1) & 3)
        self.next = [
            [(coord + distance) & 3 for distance in range(4)] for coord in self.coord
        ]
        self.peers = [
            [self.device(axis, self.next[axis][distance]) for distance in range(4)]
            for axis in range(3)
        ]
        self.other_core = (dp, blk ^ 1)

    def device(self, axis, place):
        x, y, z = (place if axis == index else self.coord[index] for index in range(3))
        return (y * 8 + z * 2 + (x & 1), (x & 2) + self.core)

    def sibling(self):
        return self.other_core

    def peer(self, axis, distance):
        return self.peers[axis][distance]


def greet(place):
    barrier = pltpu.get_barrier_semaphore()
    others = [place.sibling()]
    for axis in range(3):
        for distance in (1, 2, 3):
            others.append(place.peer(axis, distance))
    for other in others:
        pl.semaphore_signal(barrier, inc=1, device_id=other, device_id_type=MESH)
    pl.semaphore_wait(barrier, len(others))


def remote(src, dst, send_sem, recv_sem, device):
    return pltpu.make_async_remote_copy(
        src_ref=src,
        dst_ref=dst,
        send_sem=send_sem,
        recv_sem=recv_sem,
        device_id=device,
        device_id_type=MESH,
    )


class Reduction:
    def __init__(self, place, batch, result, rows, deep, refs):
        self.place = place
        self.batch = batch
        self.result = result
        self.half = rows // 2
        self.part = rows // 6
        self.first = self.part // 4
        self.piece = self.first // 4 if deep else self.first
        self.from_core, self.from_first, self.from_second, self.from_third = refs[:4]
        self.send, self.recv, self.local = refs[4:]
        self.mine = place.core * self.half
        self.other = (1 - place.core) * self.half
        if deep:
            self.steps = ["core", "scatter0", "scatter1", "exchange2", "gather1", "gather0", "share"]
        else:
            self.steps = ["core", "scatter0", "exchange1", "exchange2", "gather0", "share"]
        self.deep = deep
        self.at = 0
        self.last = len(self.steps)

    def scratch(rows, deep):
        first = rows // 24
        piece = first // 4 if deep else first
        second = (3, 3, piece, 128) if deep else (3, 4, piece, 128)
        return [
            pltpu.VMEM((rows // 2, 128), jnp.bfloat16),
            pltpu.VMEM((3, 3, first, 128), jnp.bfloat16),
            pltpu.VMEM(second, jnp.bfloat16),
            pltpu.VMEM((3, 4, piece, 128), jnp.bfloat16),
            pltpu.SemaphoreType.DMA,
            pltpu.SemaphoreType.DMA((7,)),
            pltpu.SemaphoreType.DMA((3,)),
        ]

    def advance(self):
        if self.at > 0:
            name = self.steps[self.at - 1]
            self.run(name, "finish", self.at - 1)
        if self.at < len(self.steps):
            self.run(self.steps[self.at], "start", self.at)
        self.at += 1

    def run(self, name, action, index):
        if name[-1] in "012":
            getattr(self, name[:-1] + "_" + action)(int(name[-1]), index)
        else:
            getattr(self, name + "_" + action)(index)

    def wait_bytes(self, like, index):
        remote(like, like, self.send, self.recv.at[index], self.place.sibling()).wait()

    def base(self, part, steps):
        rows = self.mine + part * self.part
        if steps > 0:
            rows = rows + self.place.coord[AXIS_ORDER[part][0]] * self.first
        if steps > 1 and self.deep:
            rows = rows + self.place.coord[AXIS_ORDER[part][1]] * self.piece
        return pl.multiple_of(rows, 16)

    def block(self, part):
        return pl.ds(self.base(part, 2), self.piece)

    def core_copy(self, index):
        rows = pl.ds(pl.multiple_of(self.other, 16), self.half)
        return remote(
            self.batch.at[rows], self.from_core, self.send, self.recv.at[index], self.place.sibling()
        )

    def core_start(self, index):
        self.core_copy(index).start()

    def core_finish(self, index):
        self.core_copy(index).wait()
        size = self.half // 12

        def add(i, _):
            here = pl.ds(pl.multiple_of(self.mine + i * size, 16), size)
            there = pl.ds(pl.multiple_of(i * size, 16), size)
            self.batch[here] = (
                self.batch[here].astype(jnp.float32) + self.from_core[there].astype(jnp.float32)
            ).astype(jnp.bfloat16)
            return 0

        lax.fori_loop(0, 12, add, 0)

    def scatter_start(self, step, index):
        size = self.first if step == 0 else self.piece
        landing = self.from_first if step == 0 else self.from_second
        for part in range(3):
            axis = AXIS_ORDER[part][step]
            for distance in (1, 2, 3):
                target = self.place.next[axis][distance]
                rows = pl.multiple_of(self.base(part, step) + target * size, 16)
                remote(
                    self.batch.at[pl.ds(rows, size)],
                    landing.at[part, distance - 1],
                    self.send,
                    self.recv.at[index],
                    self.place.peer(axis, distance),
                ).start()

    def scatter_finish(self, step, index):
        size = self.first if step == 0 else self.piece
        landing = self.from_first if step == 0 else self.from_second
        self.wait_bytes(landing, index)
        for part in range(3):
            rows = pl.ds(self.base(part, step + 1), size)
            total = self.batch[rows].astype(jnp.float32)
            for distance in (1, 2, 3):
                total = total + landing[part, distance - 1].astype(jnp.float32)
            self.batch[rows] = total.astype(jnp.bfloat16)

    def exchange_start(self, step, index):
        landing = self.from_second if step == 1 else self.from_third
        for part in range(3):
            axis = AXIS_ORDER[part][step]
            for distance in (1, 2, 3):
                remote(
                    self.batch.at[self.block(part)],
                    landing.at[part, self.place.coord[axis]],
                    self.send,
                    self.recv.at[index],
                    self.place.peer(axis, distance),
                ).start()

    def exchange_finish(self, step, index):
        landing = self.from_second if step == 1 else self.from_third
        for part in range(3):
            landing[part, self.place.coord[AXIS_ORDER[part][step]]] = self.batch[self.block(part)]
        self.wait_bytes(self.from_second if self.deep else self.from_first, index)
        for part in range(3):
            terms = [landing[part, place].astype(jnp.float32) for place in range(4)]
            total = (terms[0] + terms[1]) + (terms[2] + terms[3])
            self.batch[self.block(part)] = total.astype(jnp.bfloat16)

    def local_copies(self):
        return [
            pltpu.make_async_copy(
                self.batch.at[self.block(part)],
                self.result.at[self.block(part)],
                self.local.at[part],
            )
            for part in range(3)
        ]

    def gather_start(self, step, index):
        from_batch = step == 1 or not self.deep
        size = self.first if step == 0 else self.piece
        if from_batch:
            for copy in self.local_copies():
                copy.start()
        source = self.batch if from_batch else self.result
        for part in range(3):
            axis = AXIS_ORDER[part][step]
            rows = pl.ds(self.base(part, step + 1), size)
            for distance in (1, 2, 3):
                remote(
                    source.at[rows],
                    self.result.at[rows],
                    self.send,
                    self.recv.at[index],
                    self.place.peer(axis, distance),
                ).start()

    def gather_finish(self, step, index):
        if step == 1 or not self.deep:
            for copy in self.local_copies():
                copy.wait()
        self.wait_bytes(self.from_first if step == 0 else self.from_second, index)

    def share_copy(self, index):
        rows = pl.ds(pl.multiple_of(self.mine, 16), self.half)
        return remote(
            self.result.at[rows],
            self.result.at[rows],
            self.send,
            self.recv.at[index],
            self.place.sibling(),
        )

    def share_start(self, index):
        self.share_copy(index).start()

    def share_finish(self, index):
        self.share_copy(index).wait()


class ExtraReduction:
    def __init__(self, place, rows_ref, result, refs):
        self.place = place
        self.ref = rows_ref
        self.result = result
        self.from_core, self.from_x, self.from_plane, self.send, self.recv = refs
        self.mine = place.core * EXTRA_HALF
        self.other = (1 - place.core) * EXTRA_HALF
        self.at = 0
        self.last = 6

    def scratch():
        return [
            pltpu.VMEM((EXTRA_HALF, 128), jnp.float32),
            pltpu.VMEM((3, EXTRA_PIECE, 128), jnp.float32),
            pltpu.VMEM((2, 4, EXTRA_PIECE, 128), jnp.float32),
            pltpu.SemaphoreType.DMA,
            pltpu.SemaphoreType.DMA((6,)),
        ]

    def advance(self):
        if self.at > 0:
            self.finish(self.at - 1)
        if self.at < 6:
            self.start(self.at)
        self.at += 1

    def piece(self, quarter):
        return pl.ds(pl.multiple_of(self.mine + quarter * EXTRA_PIECE, 8), EXTRA_PIECE)

    def copy(self, index, source, target, device):
        return remote(source, target, self.send, self.recv.at[index], device)

    def core_copy(self):
        rows = pl.ds(pl.multiple_of(self.other, 8), EXTRA_HALF)
        return self.copy(0, self.ref.at[rows], self.from_core, self.place.sibling())

    def share_copy(self):
        rows = pl.ds(pl.multiple_of(self.mine, 8), EXTRA_HALF)
        return self.copy(5, self.result.at[rows], self.result.at[rows], self.place.sibling())

    def start(self, index):
        rows = self.piece(self.place.coord[0])
        if index == 0:
            self.core_copy().start()
            return
        if index == 5:
            self.share_copy().start()
            return
        for distance in (1, 2, 3):
            if index == 1:
                target = self.place.next[0][distance]
                source, target, axis = self.ref.at[self.piece(target)], self.from_x.at[distance - 1], 0
            elif index == 4:
                source, target, axis = self.result.at[rows], self.result.at[rows], 0
            else:
                axis = index - 1
                source = self.ref.at[rows]
                target = self.from_plane.at[axis - 1, self.place.coord[axis]]
            self.copy(index, source, target, self.place.peer(axis, distance)).start()

    def finish(self, index):
        rows = self.piece(self.place.coord[0])
        if index == 0:
            self.core_copy().wait()
            half = pl.ds(pl.multiple_of(self.mine, 8), EXTRA_HALF)
            self.ref[half] = self.ref[half] + self.from_core[...]
            return
        if index == 5:
            self.share_copy().wait()
            return
        if index in (2, 3):
            self.from_plane[index - 2, self.place.coord[index - 1]] = self.ref[rows]
        self.copy(index, self.from_x, self.from_x, self.place.sibling()).wait()
        if index == 1:
            self.ref[rows] = self.ref[rows] + self.from_x[0] + self.from_x[1] + self.from_x[2]
        elif index in (2, 3):
            terms = [self.from_plane[index - 2, place] for place in range(4)]
            target = self.ref if index == 2 else self.result
            target[rows] = (terms[0] + terms[1]) + (terms[2] + terms[3])


ROWS = 512
SLOT = 256
KEYS = 768
GENES = 1024
GENE_ROWS = 480
PAIRS = 4
GROUPS = ((0, 2), (2, 4))
PLAN = {
    "one pair 1": ("one_a",),
    "one keys": ("one_a",),
    "zero dense": ("one_b", "one_a"),
    "zero pair 1": ("zero_a",),
    "zero pair 2": ("one_b", "one_a"),
    "zero queries": ("first",),
    "zero merge": ("zero_a",),
    "zero values": ("one_b", "one_a"),
    "zero here": ("last", "first"),
    "genes": ("zero_a",),
}
ENDING = (
    "more", "last", "first", "one_b", "one_a",
    "zero_a", "last", "more", "first", "one_b",
    "last", "more", "zero_a", "first", "one_a",
    "last", "more", "one_b", "zero_a", "first",
    "more", "one_b", "zero_a", "first", "last", "more",
)
NEG = -1e30
SCORE_SCALE = 0.125
NN = (((1,), (0,)), ((), ()))
NT = (((1,), (1,)), ((), ()))
TN = (((0,), (0,)), ((), ()))


def dot(left, right, dims):
    return lax.dot_general(left, right, dims, preferred_element_type=jnp.float32)


def low(values):
    return values.astype(jnp.bfloat16)


def wide(values):
    return values.astype(jnp.float32)


def lane(shape):
    return lax.broadcasted_iota(jnp.int32, shape, 1)


def normalize(values):
    center = values - jnp.mean(values, axis=1, keepdims=True)
    root = lax.rsqrt(jnp.mean(center * center, axis=1, keepdims=True) + 1e-05)
    return center * root, root


def norm_back(grad, gain, normal, root):
    u = grad * gain
    mean = jnp.mean(u, axis=1, keepdims=True)
    along = jnp.mean(u * normal, axis=1, keepdims=True)
    return (u - mean - normal * along) * root


def column_sum(values):
    return jnp.sum(values, axis=0, keepdims=True)


def split_three(values):
    first = low(values)
    rest = values - wide(first)
    second = low(rest)
    third = low(rest - wide(second))
    return first, second, third


def model_kernel(
    hidden_in,
    cotangent,
    ids_in,
    unknown,
    table,
    w_inputs,
    w_output,
    w_up,
    w_down,
    b_query,
    b_value,
    b_output,
    gain_one,
    shift_one,
    b_up,
    b_down,
    gain_two,
    shift_two,
    layer_out,
    grad_hidden,
    reduced,
    extra_out,
    kept_probs,
    hidden,
    ids,
    win,
    wout,
    wup,
    wdown,
    stream,
    x_round,
    queries,
    keys,
    values,
    probs,
    stats,
    inverses,
    self_parts,
    mixed,
    normal_one,
    normal_two,
    slope,
    active,
    d_mixed,
    d_packed,
    d_keys,
    d_values,
    part_keys,
    part_values,
    sent,
    received,
    bias,
    vectors,
    out_round,
    extra,
    batch_a,
    batch_b,
    batch_c,
    batch_d,
    extra_result,
    load_sems,
    swap_send,
    swap_recv,
    kv_send,
    kv_recv,
    grad_send,
    grad_recv,
    probs_sem,
    out_sems,
    *reduction_refs,
):
    place = Place()
    cot = d_mixed
    core, here = place.core, place.x_hi
    there = 1 - here
    partner = place.peer(0, 2)
    sibling = place.sibling()

    def slot_rows(slot):
        return pl.ds(pl.multiple_of(slot * SLOT, SLOT), SLOT)

    def block_rows(slot, which):
        return pl.ds(pl.multiple_of((2 * slot + which) * SLOT, SLOT), SLOT)

    load_hidden = pltpu.make_async_copy(
        hidden_in.at[here], hidden.at[slot_rows(here)], load_sems.at[0]
    )
    load_cot = pltpu.make_async_copy(cotangent.at[here], cot.at[slot_rows(here)], load_sems.at[1])
    loads = []
    for layer in range(2):
        for index, (source, target) in enumerate(
            ((w_inputs, win), (w_output, wout), (w_up, wup), (w_down, wdown))
        ):
            loads.append(
                pltpu.make_async_copy(
                    source.at[layer],
                    target.at[layer],
                    load_sems.at[4 if layer == 1 else 2 if index == 0 else 3],
                )
            )
    load_hidden.start()
    for load in loads[0:4]:
        load.start()
    wait_rest = pltpu.make_async_copy(w_inputs.at[0], win.at[0], load_sems.at[3])
    wait_next = pltpu.make_async_copy(w_inputs, win, load_sems.at[4])
    for cell in range(2):
        ids[cell] = jnp.broadcast_to(ids_in[cell : cell + 1, :], (8, SLOT))
    known = GENES - unknown[here]

    greet(place)

    swap_hidden = remote(
        hidden_in.at[there],
        hidden.at[slot_rows(here)],
        swap_send.at[0],
        swap_recv.at[0],
        partner,
    )
    swap_ids = remote(ids.at[there], ids.at[2], swap_send.at[1], swap_recv.at[1], partner)
    swap_cot = remote(
        cotangent.at[there],
        cot.at[slot_rows(here)],
        swap_send.at[2],
        swap_recv.at[2],
        partner,
    )
    swap_ids.start()
    swap_hidden.start()

    bias[...] = jnp.where(lane((8, KEYS)) < known, 0.0, NEG)
    for slot in range(2):
        position = (2 * slot + core) * SLOT + lax.broadcasted_iota(jnp.int32, (SLOT, 128), 0)
        stats[slot * SLOT : (slot + 1) * SLOT, :] = jnp.where(position >= known, 0.0, NEG)
    part_keys[KEYS:GENES, :] = jnp.zeros((GENES - KEYS, 128), jnp.float32)
    part_values[KEYS:GENES, :] = jnp.zeros((GENES - KEYS, 128), jnp.float32)
    vectors[...] = jnp.zeros_like(vectors)
    extra[...] = jnp.zeros_like(extra)

    def slot_ids(slot):
        row = jnp.where(slot == here, ids[here, 0:1, :], ids[2, 0:1, :])
        high = lax.shift_right_logical(row, 7)
        lowest = lax.bitwise_and(row, 127)
        is_high = lax.broadcasted_iota(jnp.int32, (GENE_ROWS, SLOT), 0) == high
        is_low = lax.broadcasted_iota(jnp.int32, (128, SLOT), 0) == lowest
        return low(jnp.where(is_high, 1.0, 0.0)), is_low

    def gather_scale(slot):
        is_high, is_low = slot_ids(slot)
        total = jnp.zeros((128, SLOT), jnp.float32)
        for piece in split_three(table[...]):
            total = total + dot(piece, is_high, TN)
        row = column_sum(jnp.where(is_low, total, 0.0))
        put_column(slot_rows(slot), 5, jnp.transpose(jnp.broadcast_to(row, (128, SLOT))))

    def put_column(rows, at, column):
        stats[rows, :] = jnp.where(lane((SLOT, 128)) == at, column, stats[rows, :])

    def get_column(rows, at):
        return stats[rows, :][:, at : at + 1]

    def vector(ref, layer):
        return ref[pl.ds(layer, 1), :]

    def kv_copies(layer, slot):
        rows = block_rows(slot, core)
        return [
            remote(
                ref.at[layer, rows],
                ref.at[layer, rows],
                kv_send,
                kv_recv.at[layer],
                sibling,
            )
            for ref in (keys, values)
        ]

    def project_keys(layer, slot):
        rows = slot_rows(slot)
        if layer == 0:
            stream[rows, :] = wide(hidden[rows, :]) * get_column(rows, 5)
        x_b = low(stream[rows, :])
        x_round[layer, rows, :] = x_b
        weights = win.at[layer]
        mine = block_rows(slot, core)
        keys[layer, mine, :] = low(dot(x_b, weights[:, 512:1024], NN))
        values[layer, mine, :] = low(
            dot(x_b, weights[:, 1024:1536], NN) + vector(b_value, layer)
        )
        for copy in kv_copies(layer, slot):
            copy.start()

    def project_queries(layer):
        query = dot(x_round[layer], win[layer, :, 0:512], NN) + vector(b_query, layer)
        queries[layer] = low(wide(low(query)) * SCORE_SCALE)

    def own(ref, layer, columns):
        return jnp.concatenate(
            [ref[layer, block_rows(slot, core), columns] for slot in range(2)], axis=0
        )

    def attend(layer):
        first_half = lane((ROWS, 128)) < 64
        first_keys = lane((KEYS, 128)) < 64

        for pair in range(PAIRS):
            columns = slice(pair * 128, (pair + 1) * 128)
            q_pair = queries[layer, :, columns]
            k_pair = keys[layer, 0:KEYS, columns]
            v_pair = values[layer, 0:KEYS, columns]
            product = wide(q_pair) * wide(own(keys, layer, columns))
            found, self_terms = [], []
            for half in range(2):
                inside = first_half if half == 0 else jnp.logical_not(first_half)
                self_score = (
                    jnp.sum(jnp.where(inside, product, 0.0), axis=1, keepdims=True)
                    + stats[:, 0:1]
                )
                scores = dot(jnp.where(inside, q_pair, jnp.zeros_like(q_pair)), k_pair, NT)
                scores = scores + bias[0:1, :]
                top = jnp.maximum(jnp.max(scores, axis=1, keepdims=True), self_score)
                exponent = low(jnp.exp(scores - top))
                probs[2 * pair + half] = exponent
                with_ones = jnp.where(
                    first_keys if half == 0 else jnp.logical_not(first_keys),
                    v_pair,
                    jnp.ones_like(v_pair),
                )
                found.append(dot(exponent, with_ones, NN))
                self_terms.append(jnp.exp(self_score - top))
            self_low = low(jnp.where(first_half, self_terms[0], self_terms[1]))
            self_term = wide(self_low)
            sums = pltpu.roll(jnp.where(first_half, found[1], found[0]), 64, 1)
            inverse = 1.0 / (sums + self_term)
            total = jnp.where(first_half, found[0], found[1])
            total = total + self_term * wide(own(values, layer, columns))
            mixed[layer, :, columns] = total * inverse
            inverses[layer, :, columns] = inverse
            self_parts[layer, :, columns] = self_low

    def dense_forward(layer, slot):
        rows = slot_rows(slot)
        mixed_b = low(mixed[layer, rows, :])
        first = stream[rows, :] + (dot(mixed_b, wout[layer], NN) + vector(b_output, layer))
        normal, root = normalize(first)
        normal_one[layer, rows, :] = normal
        put_column(rows, 1 + 2 * layer, root)
        normed = normal * vector(gain_one, layer) + vector(shift_one, layer)
        inner = dot(low(normed), wup[layer], NN) + vector(b_up, layer)
        share = 0.5 * (1.0 + lax.erf(inner * 0.7071067811865476))
        slope[layer, rows, :] = share + inner * (
            0.3989422804014327 * jnp.exp(inner * inner * -0.5)
        )
        active_b = low(inner * share)
        active[layer, rows, :] = active_b
        second = normed + (dot(active_b, wdown[layer], NN) + vector(b_down, layer))
        normal, root = normalize(second)
        normal_two[layer, rows, :] = normal
        put_column(rows, 2 + 2 * layer, root)
        stream[rows, :] = normal * vector(gain_two, layer) + vector(shift_two, layer)

    def add_vector(member, layer, row):
        at = 2 * member + layer
        vectors[at : at + 1, :] = vectors[at : at + 1, :] + row

    def dense_backward(layer, slot):
        rows = slot_rows(slot)
        grad = stream[rows, :]
        normal = normal_two[layer, rows, :]
        add_vector(7, layer, column_sum(grad * normal))
        add_vector(8, layer, column_sum(grad))
        root = get_column(rows, 2 + 2 * layer)
        d_second = norm_back(grad, vector(gain_two, layer), normal, root)
        d_branch = low(d_second)
        d_packed[rows, 0:512] = d_branch
        add_vector(6, layer, column_sum(wide(d_branch)))
        d_inner = low(dot(d_branch, wdown[layer], NT) * slope[layer, rows, :])
        d_packed[rows, 512:1024] = d_inner
        add_vector(5, layer, column_sum(wide(d_inner)))
        d_normed = d_second + dot(d_inner, wup[layer], NT)
        normal = normal_one[layer, rows, :]
        add_vector(3, layer, column_sum(d_normed * normal))
        add_vector(4, layer, column_sum(d_normed))
        root = get_column(rows, 1 + 2 * layer)
        first = norm_back(d_normed, vector(gain_one, layer), normal, root)
        stream[rows, :] = first
        d_attn = low(first)
        d_packed[rows, 1024:1536] = d_attn
        add_vector(2, layer, column_sum(wide(d_attn)))
        d_mixed[rows, :] = low(dot(d_attn, wout[layer], NT))

    def put_tiles(batch, first_tile, matrix):
        for tile in range(4):
            at = (first_tile + tile) * 512
            batch[at : at + 512, :] = low(matrix[:, tile * 128 : (tile + 1) * 128])

    def dense_weights(layer, batch):
        put_tiles(batch, 0, dot(active[layer], d_packed[:, 0:512], TN))
        normed = normal_one[layer] * vector(gain_one, layer) + vector(shift_one, layer)
        put_tiles(batch, 4, dot(low(normed), d_packed[:, 512:1024], TN))
        put_tiles(batch, 8, dot(low(mixed[layer]), d_packed[:, 1024:1536], TN))

    def grad_copy(pair):
        return remote(
            sent.at[pair], received.at[pair], grad_send, grad_recv.at[pair], sibling
        )

    def attend_backward(layer, first_pair, last_pair):
        first_half = lane((ROWS, 128)) < 64

        for pair in range(first_pair, last_pair):
            columns = slice(pair * 128, (pair + 1) * 128)
            q_pair = queries[layer, :, columns]
            k_pair = keys[layer, 0:KEYS, columns]
            v_pair = values[layer, 0:KEYS, columns]
            d_out = low(wide(d_mixed[:, columns]) * inverses[layer, :, columns])
            d_wide = wide(d_out)
            d_turned = jnp.transpose(d_out)
            q_turned = jnp.transpose(q_pair)
            with_out = mixed[layer, :, columns] * d_wide
            with_own = wide(own(values, layer, columns)) * d_wide - with_out
            d_q, d_k, d_v, self_score, delta, d_probs = [], [], [], [], [], []
            for half in range(2):
                inside = first_half if half == 0 else jnp.logical_not(first_half)
                delta.append(jnp.sum(jnp.where(inside, with_out, 0.0), axis=1, keepdims=True))
                self_score.append(jnp.sum(jnp.where(inside, with_own, 0.0), axis=1, keepdims=True))
                d_probs.append(
                    dot(jnp.where(inside, d_out, jnp.zeros_like(d_out)), v_pair, NT)
                )
            for half in range(2):
                exponent = probs[2 * pair + half]
                d_scores = low(wide(exponent) * (d_probs[half] - delta[half]))
                d_q.append(dot(d_scores, k_pair, NN))
                d_k.append(dot(q_turned, d_scores, NN))
                d_v.append(dot(d_turned, exponent, NN))
            self_term = wide(self_parts[layer, :, columns])
            own_score = self_term * jnp.where(first_half, self_score[0], self_score[1])
            d_query = jnp.where(first_half, d_q[0], d_q[1]) + own_score * wide(
                own(keys, layer, columns)
            )
            d_packed[:, columns] = low(d_query * SCORE_SCALE)
            part_keys[0:KEYS, :] = jnp.transpose(
                jnp.concatenate([d_k[0][0:64], d_k[1][64:128]], axis=0)
            )
            part_values[0:KEYS, :] = jnp.transpose(
                jnp.concatenate([d_v[0][0:64], d_v[1][64:128]], axis=0)
            )
            own_keys = own_score * wide(q_pair)
            own_values = self_term * d_wide
            for slot in range(2):
                rows = slice(slot * SLOT, (slot + 1) * SLOT)
                mine = block_rows(slot, core)
                d_keys[rows, columns] = part_keys[mine, :] + own_keys[rows, :]
                d_values[rows, columns] = part_values[mine, :] + own_values[rows, :]
                other = block_rows(slot, 1 - core)
                sent[pair, 0, rows, :] = low(part_keys[other, :])
                sent[pair, 1, rows, :] = low(part_values[other, :])
            grad_copy(pair).start()

    def merge_grads(pairs):
        for pair in range(*pairs):
            grad_copy(pair).wait_recv()
            at = pair * 128
            columns = slice(at, at + 128)
            d_packed[:, 512 + at : 640 + at] = low(d_keys[:, columns] + wide(received[pair, 0]))
            d_packed[:, 1024 + at : 1152 + at] = low(d_values[:, columns] + wide(received[pair, 1]))

    def wait_sent():
        remote(sent, sent, grad_send, grad_recv.at[0], sibling).wait_send()

    def input_weights(layer, batch, first_row, third, pairs):
        first, last = pairs
        count = last - first
        columns = slice(third * 512 + first * 128, third * 512 + last * 128)
        product = dot(x_round[layer], d_packed[:, columns], TN)
        for tile in range(count):
            at = first_row + (third * count + tile) * 512
            batch[at : at + 512, :] = low(product[:, tile * 128 : (tile + 1) * 128])
        if third != 1:
            at = 2 * (third // 2) + layer
            inside = slice(first * 128, last * 128)
            vectors[at : at + 1, inside] = column_sum(wide(d_packed[:, columns]))

    def input_grad(layer, slot):
        rows = slot_rows(slot)
        stream[rows, :] = stream[rows, :] + dot(d_packed[rows, :], win[layer], NT)

    def reduction(index, batch, result, rows, deep):
        return Reduction(
            place, batch, result, rows, deep, reduction_refs[7 * index : 7 * index + 7]
        )

    group_rows = [1536 * (last - first) for first, last in GROUPS]
    group_at = [sum(group_rows[:index]) for index in range(len(GROUPS))]
    one_a = reduction(0, batch_a, reduced.at[0], BATCH_ROWS, True)
    one_b = reduction(1, batch_b, reduced.at[1], BATCH_ROWS, True)
    zero_a = reduction(2, batch_c, reduced.at[2], BATCH_ROWS, True)
    groups = [
        reduction(
            3 + index,
            batch_d.at[pl.ds(at, rows)],
            reduced.at[3, pl.ds(at, rows)],
            rows,
            index == 0,
        )
        for index, (at, rows) in enumerate(zip(group_at, group_rows))
    ]
    more = ExtraReduction(place, extra, extra_result, reduction_refs[7 * (3 + len(GROUPS)) :])
    running = {
        "one_a": one_a,
        "one_b": one_b,
        "zero_a": zero_a,
        "first": groups[0],
        "last": groups[1],
        "more": more,
    }

    def both_slots(work):
        def step(slot, _):
            work(slot)
            return 0

        lax.fori_loop(0, 2, step, 0)

    def after(piece):
        for name in PLAN.get(piece, ()):
            running[name].advance()

    load_hidden.wait()
    gather_scale(here)
    loads[0].wait()
    project_keys(0, here)
    swap_ids.wait()
    gather_scale(there)
    swap_hidden.wait()
    project_keys(0, there)
    project_queries(0)
    swap_cot.start()
    load_cot.start()
    for load in loads[4:]:
        load.start()
    probs_out = pltpu.make_async_copy(probs, kept_probs, probs_sem.at[0])
    probs_back = pltpu.make_async_copy(kept_probs, probs, probs_sem.at[1])

    def forward(layer, _):
        whole = keys.at[layer]
        remote(whole, whole, kv_send, kv_recv.at[layer], sibling).wait()

        @pl.when(layer == 1)
        def _():
            probs_out.wait()

        attend(layer)

        @pl.when(layer == 0)
        def _():
            probs_out.start()
            wait_rest.wait()
            wait_next.wait()

        def forward_slot(slot, _):
            dense_forward(layer, slot)

            @pl.when(layer == 0)
            def _():
                project_keys(1, slot)

            return 0

        lax.fori_loop(0, 2, forward_slot, 0)

        @pl.when(layer == 0)
        def _():
            project_queries(1)

        return 0

    lax.fori_loop(0, 2, forward, 0)

    out_round[...] = low(stream[...])
    keep_out = pltpu.make_async_copy(
        out_round.at[slot_rows(here)], layer_out.at[here], out_sems.at[0]
    )
    send_out = remote(
        out_round.at[slot_rows(there)],
        layer_out.at[here],
        swap_send.at[3],
        swap_recv.at[3],
        partner,
    )
    keep_out.start()
    send_out.start()

    load_cot.wait()
    swap_cot.wait()
    stream[...] = wide(cot[...])
    every = (0, PAIRS)
    both_slots(lambda slot: dense_backward(1, slot))
    dense_weights(1, batch_a)
    one_a.advance()
    for pair in range(PAIRS):
        attend_backward(1, pair, pair + 1)
        after(f"one pair {pair}")
    probs_back.start()
    input_weights(1, batch_b, 0, 0, every)
    after("one queries")
    merge_grads(every)
    after("one merge")
    input_weights(1, batch_b, 0, 1, every)
    after("one keys")
    input_weights(1, batch_b, 0, 2, every)
    one_b.advance()
    both_slots(lambda slot: input_grad(1, slot))
    after("one input")
    both_slots(lambda slot: dense_backward(0, slot))
    after("zero dense")
    dense_weights(0, batch_c)
    zero_a.advance()
    wait_sent()
    probs_back.wait()
    for pair in range(PAIRS):
        attend_backward(0, pair, pair + 1)
        after(f"zero pair {pair}")
        if pair == GROUPS[0][1]:
            merge_grads(GROUPS[0])
            for third in range(3):
                input_weights(0, batch_d, group_at[0], third, GROUPS[0])
            groups[0].advance()
    input_weights(0, batch_d, group_at[1], 0, GROUPS[1])
    after("zero queries")
    merge_grads(GROUPS[1])
    after("zero merge")
    for third in (1, 2):
        input_weights(0, batch_d, group_at[1], third, GROUPS[1])
    groups[1].advance()
    after("zero values")
    keep_grad = pltpu.make_async_copy(
        d_mixed.at[slot_rows(here)], grad_hidden.at[here], out_sems.at[1]
    )

    def grad_piece(start, count):
        return remote(
            d_mixed.at[pl.ds(pl.multiple_of(there * SLOT + start, 16), count)],
            grad_hidden.at[here, pl.ds(start, count)],
            swap_send.at[4],
            swap_recv.at[4],
            partner,
        )


    def hidden_grad(slot):
        rows = slot_rows(slot)
        input_grad(0, slot)
        d_mixed[rows, :] = low(stream[rows, :] * get_column(rows, 5))

    hidden_grad(there)
    after("zero there")
    hidden_grad(here)
    keep_grad.start()
    after("zero here")

    genes = jnp.zeros((GENE_ROWS, 128), jnp.float32)
    for slot in range(2):
        rows = slot_rows(slot)
        is_high, is_low = slot_ids(slot)
        per_token = jnp.sum(stream[rows, :] * wide(hidden[rows, :]), axis=1, keepdims=True)
        row = jnp.transpose(jnp.broadcast_to(per_token, (SLOT, 128)))
        for piece in split_three(jnp.where(is_low, row, 0.0)):
            genes = genes + dot(is_high, piece, NT)
    extra[0:GENE_ROWS, :] = genes
    for index in range(18):
        for tile in range(4):
            at = GENE_ROWS + 4 * index + tile
            extra[at : at + 1, :] = vectors[index : index + 1, tile * 128 : (tile + 1) * 128]
    after("genes")
    more.advance()
    for index, name in enumerate(ENDING):
        running[name].advance()
        if index % 2 == 0 and index < 16:
            grad_piece(index * 16, 32).start()
        if name == "more" and more.at == 7:
            extra_copy = pltpu.make_async_copy(extra_result, extra_out, out_sems.at[2])
            extra_copy.start()
    for one in running.values():
        assert one.at == one.last + 1
    wait_sent()
    keep_out.wait()
    send_out.wait()
    keep_grad.wait()
    grad_piece(0, SLOT).wait()
    extra_copy.wait()


def run_model(hidden_in, cotangent, gene_ids, unknown_count, table, weights, vector_args):
    f32, bf16 = jnp.float32, jnp.bfloat16
    vmem = pl.BlockSpec(memory_space=pltpu.VMEM)
    smem = pl.BlockSpec(memory_space=pltpu.SMEM)
    anywhere = pl.BlockSpec(memory_space=pl.ANY)
    scratch = [
        pltpu.VMEM((ROWS, 512), bf16),
        pltpu.VMEM((3, 8, SLOT), jnp.int32),
        pltpu.VMEM((2, 512, 1536), bf16),
        pltpu.VMEM((2, 512, 512), bf16),
        pltpu.VMEM((2, 512, 512), bf16),
        pltpu.VMEM((2, 512, 512), bf16),
        pltpu.VMEM((ROWS, 512), f32),
        pltpu.VMEM((2, ROWS, 512), bf16),
        pltpu.VMEM((2, ROWS, 512), bf16),
        pltpu.VMEM((2, GENES, 512), bf16),
        pltpu.VMEM((2, GENES, 512), bf16),
        pltpu.VMEM((HEADS, ROWS, KEYS), bf16),
        pltpu.VMEM((ROWS, 128), f32),
        pltpu.VMEM((2, ROWS, 512), f32),
        pltpu.VMEM((2, ROWS, 512), bf16),
        pltpu.VMEM((2, ROWS, 512), f32),
        pltpu.VMEM((2, ROWS, 512), f32),
        pltpu.VMEM((2, ROWS, 512), f32),
        pltpu.VMEM((2, ROWS, 512), f32),
        pltpu.VMEM((2, ROWS, 512), bf16),
        pltpu.VMEM((ROWS, 512), bf16),
        pltpu.VMEM((ROWS, 1536), bf16),
        pltpu.VMEM((ROWS, 512), f32),
        pltpu.VMEM((ROWS, 512), f32),
        pltpu.VMEM((GENES, 128), f32),
        pltpu.VMEM((GENES, 128), f32),
        pltpu.VMEM((PAIRS, 2, ROWS, 128), bf16),
        pltpu.VMEM((PAIRS, 2, ROWS, 128), bf16),
        pltpu.VMEM((8, KEYS), f32),
        pltpu.VMEM((24, 512), f32),
        pltpu.VMEM((ROWS, 512), bf16),
        pltpu.VMEM((EXTRA_ROWS, 128), f32),
        pltpu.VMEM((BATCH_ROWS, 128), bf16),
        pltpu.VMEM((BATCH_ROWS, 128), bf16),
        pltpu.VMEM((BATCH_ROWS, 128), bf16),
        pltpu.VMEM((BATCH_ROWS, 128), bf16),
        pltpu.VMEM((EXTRA_ROWS, 128), f32),
        pltpu.SemaphoreType.DMA((5,)),
        pltpu.SemaphoreType.DMA((5,)),
        pltpu.SemaphoreType.DMA((5,)),
        pltpu.SemaphoreType.DMA,
        pltpu.SemaphoreType.DMA((2,)),
        pltpu.SemaphoreType.DMA,
        pltpu.SemaphoreType.DMA((PAIRS,)),
        pltpu.SemaphoreType.DMA((2,)),
        pltpu.SemaphoreType.DMA((3,)),
    ]
    for _ in range(3):
        scratch += Reduction.scratch(BATCH_ROWS, True)
    for index, (first, last) in enumerate(GROUPS):
        scratch += Reduction.scratch(1536 * (last - first), index == 0)
    scratch += ExtraReduction.scratch()
    outs = (
        jax.ShapeDtypeStruct((2, SLOT, 512), bf16),
        jax.ShapeDtypeStruct((2, SLOT, 512), bf16),
        jax.ShapeDtypeStruct((4, BATCH_ROWS, 128), bf16),
        jax.ShapeDtypeStruct((EXTRA_ROWS, 128), f32),
        jax.ShapeDtypeStruct((HEADS, ROWS, KEYS), bf16),
    )
    return pl.pallas_call(
        model_kernel,
        out_shape=outs,
        in_specs=[anywhere, anywhere, vmem, smem, vmem] + [anywhere] * 4 + [vmem] * 9,
        out_specs=(anywhere,) * 5,
        scratch_shapes=scratch,
        compiler_params=pltpu.CompilerParams(
            collective_id=0, has_side_effects=True, vmem_limit_bytes=255 << 18
        ),
        name="model",
    )(hidden_in, cotangent, gene_ids, unknown_count, table, *weights, *vector_args)


def finish_kernel(layer_in, hidden_grad_in, reduced, extra, *refs):
    layer_out, hidden_out, g_inputs, g_output, g_up, g_down, genes = refs[:7]
    vector_outs = refs[7:16]
    rounded, narrow, rows_out, wide_in, wide_rest, extra_rows, in_sems, out_sems = refs[16:]
    sources = [layer_in, hidden_grad_in]
    loads = [
        pltpu.make_async_copy(sources[i], rounded.at[i], in_sems.at[i]) for i in range(2)
    ] + [pltpu.make_async_copy(reduced.at[i], narrow.at[i], in_sems.at[2 + i]) for i in range(4)]
    loads.append(pltpu.make_async_copy(extra, extra_rows, in_sems.at[6]))
    for load in loads[:1] + loads[6:] + loads[1:6]:
        load.start()
    stores = []

    def send(source, target):
        store = pltpu.make_async_copy(source, target, out_sems.at[len(stores)])
        store.start()
        stores.append(store)

    for index, target in enumerate((layer_out, hidden_out)):
        loads[index].wait()
        rows_out[index] = wide(rounded[index])
        send(rows_out.at[index], target)
    for layer in (1, 0):
        base = 2 * (1 - layer)
        loads[2 + base].wait()
        for index, target in enumerate((g_down, g_up, g_output)):
            for tile in range(4):
                at = (4 * index + tile) * 512
                wide_rest[layer, index, :, tile * 128 : (tile + 1) * 128] = wide(
                    narrow[base, at : at + 512, :]
                )
            send(wide_rest.at[layer, index], target.at[layer])
        loads[3 + base].wait()
        at = 0
        for first, last in GROUPS if layer == 0 else ((0, PAIRS),):
            for third in range(3):
                for pair in range(first, last):
                    column = third * 512 + pair * 128
                    wide_in[layer, :, column : column + 128] = wide(
                        narrow[base + 1, at : at + 512, :]
                    )
                    at += 512
        send(wide_in.at[layer], g_inputs.at[layer])
    loads[6].wait()
    genes[...] = extra_rows[0:GENE_ROWS, :]
    for member in range(9):
        for layer in range(2):
            for tile in range(4):
                at = GENE_ROWS + 4 * (2 * member + layer) + tile
                vector_outs[member][layer : layer + 1, tile * 128 : (tile + 1) * 128] = extra_rows[
                    at : at + 1, :
                ]
    for store in stores:
        store.wait()


def finish(layer_out, grad_hidden, reduced, extra):
    f32, bf16 = jnp.float32, jnp.bfloat16
    vmem = pl.BlockSpec(memory_space=pltpu.VMEM)
    anywhere = pl.BlockSpec(memory_space=pl.ANY)
    outs = [
        jax.ShapeDtypeStruct((2, SLOT, 512), f32),
        jax.ShapeDtypeStruct((2, SLOT, 512), f32),
        jax.ShapeDtypeStruct((2, 512, 1536), f32),
        jax.ShapeDtypeStruct((2, 512, 512), f32),
        jax.ShapeDtypeStruct((2, 512, 512), f32),
        jax.ShapeDtypeStruct((2, 512, 512), f32),
        jax.ShapeDtypeStruct((GENE_ROWS, 128), f32),
    ] + [jax.ShapeDtypeStruct((2, 512), f32)] * 9
    return pl.pallas_call(
        finish_kernel,
        out_shape=outs,
        in_specs=[anywhere] * 4,
        out_specs=[anywhere] * 6 + [vmem] * 10,
        scratch_shapes=[
            pltpu.VMEM((2, 2, SLOT, 512), bf16),
            pltpu.VMEM((4, BATCH_ROWS, 128), bf16),
            pltpu.VMEM((2, 2, SLOT, 512), f32),
            pltpu.VMEM((2, 512, 1536), f32),
            pltpu.VMEM((2, 3, 512, 512), f32),
            pltpu.VMEM((EXTRA_ROWS, 128), f32),
            pltpu.SemaphoreType.DMA((7,)),
            pltpu.SemaphoreType.DMA((10,)),
        ],
        compiler_params=pltpu.CompilerParams(vmem_limit_bytes=63 << 20),
        name="finish",
    )(layer_out, grad_hidden, reduced, extra)


def shards(
    hidden_in,
    gene_ids,
    unknown_count,
    gene_scale,
    w_inputs,
    b_query,
    b_value,
    w_output,
    b_output,
    gain_one,
    shift_one,
    w_up,
    b_up,
    w_down,
    b_down,
    gain_two,
    shift_two,
    cotangent,
):
    gene_count = gene_scale.shape[0]
    table = jnp.pad(gene_scale, (0, GENE_ROWS * 128 - gene_count)).reshape(GENE_ROWS, 128)
    layer_out, grad_hidden, reduced, extra, _ = run_model(
        hidden_in,
        cotangent,
        gene_ids,
        unknown_count,
        table,
        (w_inputs, w_output, w_up, w_down),
        (b_query, b_value, b_output, gain_one, shift_one, b_up, b_down, gain_two, shift_two),
    )
    (
        layer_out,
        grad_hidden,
        g_inputs,
        g_output,
        g_up,
        g_down,
        genes,
        g_b_query,
        g_b_value,
        g_b_output,
        g_gain_one,
        g_shift_one,
        g_b_up,
        g_b_down,
        g_gain_two,
        g_shift_two,
    ) = finish(layer_out, grad_hidden, reduced, extra)
    return (
        layer_out,
        grad_hidden,
        genes.reshape(-1)[:gene_count],
        g_inputs,
        g_b_query,
        g_b_value,
        g_output,
        g_b_output,
        g_gain_one,
        g_shift_one,
        g_up,
        g_b_up,
        g_down,
        g_b_down,
        g_gain_two,
        g_shift_two,
    )


def solution(mesh):
    placed = (
        P("dp", "blk", None),
        P("dp", "blk"),
        P("dp"),
        P(),
        P(),
        P(),
        P(),
        P(),
        P(),
        P(),
        P(),
        P(),
        P(),
        P(),
        P(),
        P(),
        P(),
        P("dp", "blk", None),
    )
    return jax.shard_map(
        shards,
        mesh=mesh,
        in_specs=placed,
        out_specs=(
            P("dp", "blk", None),
            P("dp", "blk", None),
            P(),
            P(),
            P(),
            P(),
            P(),
            P(),
            P(),
            P(),
            P(),
            P(),
            P(),
            P(),
            P(),
            P(),
        ),
        check_vma=False,
    )
```

```python
import jax
import jax.numpy as jnp
from jax import lax
from jax.experimental import pallas as pl
from jax.experimental.pallas import tpu as pltpu
from jax.sharding import PartitionSpec as P

HEADS = 8
MESH = pl.DeviceIdType.MESH
AXIS_ORDER = ((0, 1, 2), (1, 2, 0), (2, 0, 1))
BATCH_ROWS = 6144
EXTRA_ROWS = 576
EXTRA_HALF = EXTRA_ROWS // 2
EXTRA_PIECE = EXTRA_HALF // 4


class Place:
    def __init__(self):
        dp = lax.axis_index("dp")
        blk = lax.axis_index("blk")
        self.core = blk & 1
        self.x_hi = blk >> 1
        self.coord = (self.x_hi * 2 + (dp & 1), dp >> 3, (dp >> 1) & 3)
        self.next = [
            [(coord + distance) & 3 for distance in range(4)] for coord in self.coord
        ]
        self.peers = [
            [self.device(axis, self.next[axis][distance]) for distance in range(4)]
            for axis in range(3)
        ]
        self.other_core = (dp, blk ^ 1)

    def device(self, axis, place):
        x, y, z = (place if axis == index else self.coord[index] for index in range(3))
        return (y * 8 + z * 2 + (x & 1), (x & 2) + self.core)

    def sibling(self):
        return self.other_core

    def peer(self, axis, distance):
        return self.peers[axis][distance]


def greet(place):
    barrier = pltpu.get_barrier_semaphore()
    others = [place.sibling()]
    for axis in range(3):
        for distance in (1, 2, 3):
            others.append(place.peer(axis, distance))
    for other in others:
        pl.semaphore_signal(barrier, inc=1, device_id=other, device_id_type=MESH)
    pl.semaphore_wait(barrier, len(others))


def remote(src, dst, send_sem, recv_sem, device):
    return pltpu.make_async_remote_copy(
        src_ref=src,
        dst_ref=dst,
        send_sem=send_sem,
        recv_sem=recv_sem,
        device_id=device,
        device_id_type=MESH,
    )


class Reduction:
    def __init__(self, place, batch, result, rows, deep, refs):
        self.place = place
        self.batch = batch
        self.result = result
        self.half = rows // 2
        self.part = rows // 6
        self.first = self.part // 4
        self.piece = self.first // 4 if deep else self.first
        self.from_core, self.from_first, self.from_second, self.from_third = refs[:4]
        self.send, self.recv, self.local = refs[4:]
        self.mine = place.core * self.half
        self.other = (1 - place.core) * self.half
        if deep:
            self.steps = ["core", "scatter0", "scatter1", "exchange2", "gather1", "gather0", "share"]
        else:
            self.steps = ["core", "scatter0", "exchange1", "exchange2", "gather0", "share"]
        self.deep = deep
        self.at = 0
        self.last = len(self.steps)

    def scratch(rows, deep):
        first = rows // 24
        piece = first // 4 if deep else first
        second = (3, 3, piece, 128) if deep else (3, 4, piece, 128)
        return [
            pltpu.VMEM((rows // 2, 128), jnp.bfloat16),
            pltpu.VMEM((3, 3, first, 128), jnp.bfloat16),
            pltpu.VMEM(second, jnp.bfloat16),
            pltpu.VMEM((3, 4, piece, 128), jnp.bfloat16),
            pltpu.SemaphoreType.DMA,
            pltpu.SemaphoreType.DMA((7,)),
            pltpu.SemaphoreType.DMA((3,)),
        ]

    def advance(self):
        if self.at > 0:
            name = self.steps[self.at - 1]
            self.run(name, "finish", self.at - 1)
        if self.at < len(self.steps):
            self.run(self.steps[self.at], "start", self.at)
        self.at += 1

    def run(self, name, action, index):
        if name[-1] in "012":
            getattr(self, name[:-1] + "_" + action)(int(name[-1]), index)
        else:
            getattr(self, name + "_" + action)(index)

    def wait_bytes(self, like, index):
        remote(like, like, self.send, self.recv.at[index], self.place.sibling()).wait()

    def base(self, part, steps):
        rows = self.mine + part * self.part
        if steps > 0:
            rows = rows + self.place.coord[AXIS_ORDER[part][0]] * self.first
        if steps > 1 and self.deep:
            rows = rows + self.place.coord[AXIS_ORDER[part][1]] * self.piece
        return pl.multiple_of(rows, 16)

    def block(self, part):
        return pl.ds(self.base(part, 2), self.piece)

    def core_copy(self, index):
        rows = pl.ds(pl.multiple_of(self.other, 16), self.half)
        return remote(
            self.batch.at[rows], self.from_core, self.send, self.recv.at[index], self.place.sibling()
        )

    def core_start(self, index):
        self.core_copy(index).start()

    def core_finish(self, index):
        self.core_copy(index).wait()
        size = self.half // 12

        def add(i, _):
            here = pl.ds(pl.multiple_of(self.mine + i * size, 16), size)
            there = pl.ds(pl.multiple_of(i * size, 16), size)
            self.batch[here] = (
                self.batch[here].astype(jnp.float32) + self.from_core[there].astype(jnp.float32)
            ).astype(jnp.bfloat16)
            return 0

        lax.fori_loop(0, 12, add, 0)

    def scatter_start(self, step, index):
        size = self.first if step == 0 else self.piece
        landing = self.from_first if step == 0 else self.from_second
        for part in range(3):
            axis = AXIS_ORDER[part][step]
            for distance in (1, 2, 3):
                target = self.place.next[axis][distance]
                rows = pl.multiple_of(self.base(part, step) + target * size, 16)
                remote(
                    self.batch.at[pl.ds(rows, size)],
                    landing.at[part, distance - 1],
                    self.send,
                    self.recv.at[index],
                    self.place.peer(axis, distance),
                ).start()

    def scatter_finish(self, step, index):
        size = self.first if step == 0 else self.piece
        landing = self.from_first if step == 0 else self.from_second
        self.wait_bytes(landing, index)
        for part in range(3):
            rows = pl.ds(self.base(part, step + 1), size)
            total = self.batch[rows].astype(jnp.float32)
            for distance in (1, 2, 3):
                total = total + landing[part, distance - 1].astype(jnp.float32)
            self.batch[rows] = total.astype(jnp.bfloat16)

    def exchange_start(self, step, index):
        landing = self.from_second if step == 1 else self.from_third
        for part in range(3):
            axis = AXIS_ORDER[part][step]
            for distance in (1, 2, 3):
                remote(
                    self.batch.at[self.block(part)],
                    landing.at[part, self.place.coord[axis]],
                    self.send,
                    self.recv.at[index],
                    self.place.peer(axis, distance),
                ).start()

    def exchange_finish(self, step, index):
        landing = self.from_second if step == 1 else self.from_third
        for part in range(3):
            landing[part, self.place.coord[AXIS_ORDER[part][step]]] = self.batch[self.block(part)]
        self.wait_bytes(self.from_second if self.deep else self.from_first, index)
        for part in range(3):
            terms = [landing[part, place].astype(jnp.float32) for place in range(4)]
            total = (terms[0] + terms[1]) + (terms[2] + terms[3])
            self.batch[self.block(part)] = total.astype(jnp.bfloat16)

    def local_copies(self):
        return [
            pltpu.make_async_copy(
                self.batch.at[self.block(part)],
                self.result.at[self.block(part)],
                self.local.at[part],
            )
            for part in range(3)
        ]

    def gather_start(self, step, index):
        from_batch = step == 1 or not self.deep
        size = self.first if step == 0 else self.piece
        if from_batch:
            for copy in self.local_copies():
                copy.start()
        source = self.batch if from_batch else self.result
        for part in range(3):
            axis = AXIS_ORDER[part][step]
            rows = pl.ds(self.base(part, step + 1), size)
            for distance in (1, 2, 3):
                remote(
                    source.at[rows],
                    self.result.at[rows],
                    self.send,
                    self.recv.at[index],
                    self.place.peer(axis, distance),
                ).start()

    def gather_finish(self, step, index):
        if step == 1 or not self.deep:
            for copy in self.local_copies():
                copy.wait()
        self.wait_bytes(self.from_first if step == 0 else self.from_second, index)

    def share_copy(self, index):
        rows = pl.ds(pl.multiple_of(self.mine, 16), self.half)
        return remote(
            self.result.at[rows],
            self.result.at[rows],
            self.send,
            self.recv.at[index],
            self.place.sibling(),
        )

    def share_start(self, index):
        self.share_copy(index).start()

    def share_finish(self, index):
        self.share_copy(index).wait()


class ExtraReduction:
    def __init__(self, place, rows_ref, result, out, refs):
        self.place = place
        self.ref = rows_ref
        self.result = result
        self.out = out
        self.from_core, self.from_x, self.from_plane, self.send, self.recv, self.local = refs
        self.mine = place.core * EXTRA_HALF
        self.other = (1 - place.core) * EXTRA_HALF
        self.at = 0
        self.last = 6

    def scratch():
        return [
            pltpu.VMEM((EXTRA_HALF, 128), jnp.float32),
            pltpu.VMEM((3, EXTRA_PIECE, 128), jnp.float32),
            pltpu.VMEM((2, 4, EXTRA_PIECE, 128), jnp.float32),
            pltpu.SemaphoreType.DMA,
            pltpu.SemaphoreType.DMA((6,)),
            pltpu.SemaphoreType.DMA,
        ]

    def advance(self):
        if self.at > 0:
            self.finish(self.at - 1)
        if self.at < 6:
            self.start(self.at)
        self.at += 1

    def piece(self, quarter):
        return pl.ds(pl.multiple_of(self.mine + quarter * EXTRA_PIECE, 8), EXTRA_PIECE)

    def copy(self, index, source, target, device):
        return remote(source, target, self.send, self.recv.at[index], device)

    def core_copy(self):
        rows = pl.ds(pl.multiple_of(self.other, 8), EXTRA_HALF)
        return self.copy(0, self.ref.at[rows], self.from_core, self.place.sibling())

    def share_copy(self):
        rows = pl.ds(pl.multiple_of(self.mine, 8), EXTRA_HALF)
        return self.copy(5, self.result.at[rows], self.out.at[rows], self.place.sibling())

    def keep_copy(self):
        rows = pl.ds(pl.multiple_of(self.mine, 8), EXTRA_HALF)
        return pltpu.make_async_copy(self.result.at[rows], self.out.at[rows], self.local)

    def start(self, index):
        rows = self.piece(self.place.coord[0])
        if index == 0:
            self.core_copy().start()
            return
        if index == 5:
            self.share_copy().start()
            self.keep_copy().start()
            return
        for distance in (1, 2, 3):
            if index == 1:
                target = self.place.next[0][distance]
                source, target, axis = self.ref.at[self.piece(target)], self.from_x.at[distance - 1], 0
            elif index == 4:
                source, target, axis = self.result.at[rows], self.result.at[rows], 0
            else:
                axis = index - 1
                source = self.ref.at[rows]
                target = self.from_plane.at[axis - 1, self.place.coord[axis]]
            self.copy(index, source, target, self.place.peer(axis, distance)).start()

    def finish(self, index):
        rows = self.piece(self.place.coord[0])
        if index == 0:
            self.core_copy().wait()
            half = pl.ds(pl.multiple_of(self.mine, 8), EXTRA_HALF)
            self.ref[half] = self.ref[half] + self.from_core[...]
            return
        if index == 5:
            self.share_copy().wait()
            self.keep_copy().wait()
            return
        if index in (2, 3):
            self.from_plane[index - 2, self.place.coord[index - 1]] = self.ref[rows]
        self.copy(index, self.from_x, self.from_x, self.place.sibling()).wait()
        if index == 1:
            self.ref[rows] = self.ref[rows] + self.from_x[0] + self.from_x[1] + self.from_x[2]
        elif index in (2, 3):
            terms = [self.from_plane[index - 2, place] for place in range(4)]
            target = self.ref if index == 2 else self.result
            target[rows] = (terms[0] + terms[1]) + (terms[2] + terms[3])


ROWS = 512
SLOT = 256
KEYS = 768
GENES = 1024
GENE_ROWS = 480
PAIRS = 4
GROUPS = ((0, 2), (2, 4))
PLAN = {
    "one pair 1": ("one_a",),
    "one keys": ("one_a",),
    "zero dense": ("one_b", "one_a"),
    "zero pair 1": ("zero_a",),
    "zero pair 2": ("one_b", "one_a"),
    "zero queries": ("first",),
    "zero merge": ("zero_a",),
    "zero values": ("one_b", "one_a"),
    "zero here": ("last", "first"),
    "genes": ("zero_a",),
}
ENDING = (
    "more", "last", "first", "one_b", "one_a",
    "zero_a", "last", "more", "first", "one_b",
    "last", "more", "zero_a", "first", "one_a", "one_b",
    "last", "more", "zero_a", "first",
    "more", "one_b", "zero_a", "first", "last", "more",
)
NEG = -1e30
SCORE_SCALE = 0.125
NN = (((1,), (0,)), ((), ()))
NT = (((1,), (1,)), ((), ()))
TN = (((0,), (0,)), ((), ()))


def dot(left, right, dims):
    return lax.dot_general(left, right, dims, preferred_element_type=jnp.float32)


def low(values):
    return values.astype(jnp.bfloat16)


def wide(values):
    return values.astype(jnp.float32)


def lane(shape):
    return lax.broadcasted_iota(jnp.int32, shape, 1)


def normalize(values):
    center = values - jnp.mean(values, axis=1, keepdims=True)
    root = lax.rsqrt(jnp.mean(center * center, axis=1, keepdims=True) + 1e-05)
    return center * root, root


def norm_back(grad, gain, normal, root):
    u = grad * gain
    mean = jnp.mean(u, axis=1, keepdims=True)
    along = jnp.mean(u * normal, axis=1, keepdims=True)
    return (u - mean - normal * along) * root


def column_sum(values):
    return jnp.sum(values, axis=0, keepdims=True)


def split_three(values):
    first = low(values)
    rest = values - wide(first)
    second = low(rest)
    third = low(rest - wide(second))
    return first, second, third


def model_kernel(
    hidden_in,
    cotangent,
    ids_far,
    unknown,
    table_far,
    w_inputs,
    w_output,
    w_up,
    w_down,
    *more_refs,
):
    vectors_far, rest = more_refs[:9], more_refs[9:]
    near, rest = rest[-11:], rest[:-11]
    model_body(
        hidden_in,
        cotangent,
        unknown,
        w_inputs,
        w_output,
        w_up,
        w_down,
        (ids_far, table_far) + tuple(vectors_far),
        near,
        *rest,
    )


def model_body(
    hidden_in,
    cotangent,
    unknown,
    w_inputs,
    w_output,
    w_up,
    w_down,
    far,
    near,
    layer_out,
    grad_hidden,
    reduced,
    extra_out,
    kept_probs,
    hidden,
    ids,
    win,
    wout,
    wup,
    wdown,
    stream,
    x_round,
    queries,
    keys,
    values,
    probs,
    stats,
    inverses,
    self_parts,
    mixed,
    normal_one,
    normal_two,
    slope,
    active,
    d_mixed,
    d_packed,
    d_keys,
    d_values,
    part_keys,
    part_values,
    sent,
    received,
    bias,
    vectors,
    out_round,
    extra,
    batch_a,
    batch_b,
    batch_c,
    batch_d,
    extra_result,
    load_sems,
    swap_send,
    swap_recv,
    kv_send,
    kv_recv,
    grad_send,
    grad_recv,
    probs_sem,
    out_sems,
    *reduction_refs,
):
    small = [
        pltpu.make_async_copy(source, target, load_sems.at[5 + index])
        for index, (source, target) in enumerate(zip(far, near))
    ]
    for copy in small:
        copy.start()
    ids_in, table, b_query, b_value, b_output, gain_one, shift_one = near[:7]
    b_up, b_down, gain_two, shift_two = near[7:]
    place = Place()
    cot = d_mixed
    core, here = place.core, place.x_hi
    there = 1 - here
    partner = place.peer(0, 2)
    sibling = place.sibling()

    def slot_rows(slot):
        return pl.ds(pl.multiple_of(slot * SLOT, SLOT), SLOT)

    def block_rows(slot, which):
        return pl.ds(pl.multiple_of((2 * slot + which) * SLOT, SLOT), SLOT)

    load_hidden = pltpu.make_async_copy(
        hidden_in.at[here], hidden.at[slot_rows(here)], load_sems.at[0]
    )
    load_cot = pltpu.make_async_copy(cotangent.at[here], cot.at[slot_rows(here)], load_sems.at[1])
    loads = []
    for layer in range(2):
        for index, (source, target) in enumerate(
            ((w_inputs, win), (w_output, wout), (w_up, wup), (w_down, wdown))
        ):
            loads.append(
                pltpu.make_async_copy(
                    source.at[layer],
                    target.at[layer],
                    load_sems.at[4 if layer == 1 else 2 if index == 0 else 3],
                )
            )
    load_hidden.start()
    for load in loads[0:4]:
        load.start()
    wait_rest = pltpu.make_async_copy(w_inputs.at[0], win.at[0], load_sems.at[3])
    wait_next = pltpu.make_async_copy(w_inputs, win, load_sems.at[4])
    greet(place)
    small[0].wait()
    for cell in range(2):
        ids[cell] = jnp.broadcast_to(ids_in[cell : cell + 1, :], (8, SLOT))
    known = GENES - unknown[here]

    swap_hidden = remote(
        hidden_in.at[there],
        hidden.at[slot_rows(here)],
        swap_send.at[0],
        swap_recv.at[0],
        partner,
    )
    swap_ids = remote(ids.at[there], ids.at[2], swap_send.at[1], swap_recv.at[1], partner)
    swap_cot = remote(
        cotangent.at[there],
        cot.at[slot_rows(here)],
        swap_send.at[2],
        swap_recv.at[2],
        partner,
    )
    swap_ids.start()
    swap_hidden.start()

    bias[...] = jnp.where(lane((8, KEYS)) < known, 0.0, NEG)
    for slot in range(2):
        position = (2 * slot + core) * SLOT + lax.broadcasted_iota(jnp.int32, (SLOT, 128), 0)
        stats[slot * SLOT : (slot + 1) * SLOT, :] = jnp.where(position >= known, 0.0, NEG)
    part_keys[KEYS:GENES, :] = jnp.zeros((GENES - KEYS, 128), jnp.float32)
    part_values[KEYS:GENES, :] = jnp.zeros((GENES - KEYS, 128), jnp.float32)
    vectors[...] = jnp.zeros_like(vectors)
    extra[...] = jnp.zeros_like(extra)

    def slot_ids(slot):
        row = jnp.where(slot == here, ids[here, 0:1, :], ids[2, 0:1, :])
        high = lax.shift_right_logical(row, 7)
        lowest = lax.bitwise_and(row, 127)
        is_high = lax.broadcasted_iota(jnp.int32, (GENE_ROWS, SLOT), 0) == high
        is_low = lax.broadcasted_iota(jnp.int32, (128, SLOT), 0) == lowest
        return low(jnp.where(is_high, 1.0, 0.0)), is_low

    def gather_scale(slot):
        is_high, is_low = slot_ids(slot)
        total = jnp.zeros((128, SLOT), jnp.float32)
        for piece in split_three(table[...]):
            total = total + dot(piece, is_high, TN)
        row = column_sum(jnp.where(is_low, total, 0.0))
        put_column(slot_rows(slot), 5, jnp.transpose(jnp.broadcast_to(row, (128, SLOT))))

    def put_column(rows, at, column):
        stats[rows, :] = jnp.where(lane((SLOT, 128)) == at, column, stats[rows, :])

    def get_column(rows, at):
        return stats[rows, :][:, at : at + 1]

    def vector(ref, layer):
        return ref[pl.ds(layer, 1), :]

    def kv_copies(layer, slot):
        rows = block_rows(slot, core)
        return [
            remote(
                ref.at[layer, rows],
                ref.at[layer, rows],
                kv_send,
                kv_recv.at[layer],
                sibling,
            )
            for ref in (keys, values)
        ]

    def project_keys(layer, slot):
        rows = slot_rows(slot)
        if layer == 0:
            stream[rows, :] = wide(hidden[rows, :]) * get_column(rows, 5)
        x_b = low(stream[rows, :])
        x_round[layer, rows, :] = x_b
        weights = win.at[layer]
        mine = block_rows(slot, core)
        keys[layer, mine, :] = low(dot(x_b, weights[:, 512:1024], NN))
        values[layer, mine, :] = low(
            dot(x_b, weights[:, 1024:1536], NN) + vector(b_value, layer)
        )
        for copy in kv_copies(layer, slot):
            copy.start()

    def project_queries(layer):
        query = dot(x_round[layer], win[layer, :, 0:512], NN) + vector(b_query, layer)
        queries[layer] = low(wide(low(query)) * SCORE_SCALE)

    def own(ref, layer, columns):
        return jnp.concatenate(
            [ref[layer, block_rows(slot, core), columns] for slot in range(2)], axis=0
        )

    def attend(layer):
        first_half = lane((ROWS, 128)) < 64
        first_keys = lane((KEYS, 128)) < 64

        for pair in range(PAIRS):
            columns = slice(pair * 128, (pair + 1) * 128)
            q_pair = queries[layer, :, columns]
            k_pair = keys[layer, 0:KEYS, columns]
            v_pair = values[layer, 0:KEYS, columns]
            product = wide(q_pair) * wide(own(keys, layer, columns))
            found, self_terms = [], []
            for half in range(2):
                inside = first_half if half == 0 else jnp.logical_not(first_half)
                self_score = (
                    jnp.sum(jnp.where(inside, product, 0.0), axis=1, keepdims=True)
                    + stats[:, 0:1]
                )
                scores = dot(jnp.where(inside, q_pair, jnp.zeros_like(q_pair)), k_pair, NT)
                scores = scores + bias[0:1, :]
                top = jnp.maximum(jnp.max(scores, axis=1, keepdims=True), self_score)
                exponent = low(jnp.exp(scores - top))
                probs[2 * pair + half] = exponent
                with_ones = jnp.where(
                    first_keys if half == 0 else jnp.logical_not(first_keys),
                    v_pair,
                    jnp.ones_like(v_pair),
                )
                found.append(dot(exponent, with_ones, NN))
                self_terms.append(jnp.exp(self_score - top))
            self_low = low(jnp.where(first_half, self_terms[0], self_terms[1]))
            self_term = wide(self_low)
            sums = pltpu.roll(jnp.where(first_half, found[1], found[0]), 64, 1)
            inverse = 1.0 / (sums + self_term)
            total = jnp.where(first_half, found[0], found[1])
            total = total + self_term * wide(own(values, layer, columns))
            mixed[layer, :, columns] = total * inverse
            inverses[layer, :, columns] = inverse
            self_parts[layer, :, columns] = self_low

    def dense_forward(layer, slot):
        rows = slot_rows(slot)
        mixed_b = low(mixed[layer, rows, :])
        first = stream[rows, :] + (dot(mixed_b, wout[layer], NN) + vector(b_output, layer))
        normal, root = normalize(first)
        normal_one[layer, rows, :] = normal
        put_column(rows, 1 + 2 * layer, root)
        normed = normal * vector(gain_one, layer) + vector(shift_one, layer)
        inner = dot(low(normed), wup[layer], NN) + vector(b_up, layer)
        share = 0.5 * (1.0 + lax.erf(inner * 0.7071067811865476))
        slope[layer, rows, :] = share + inner * (
            0.3989422804014327 * jnp.exp(inner * inner * -0.5)
        )
        active_b = low(inner * share)
        active[layer, rows, :] = active_b
        second = normed + (dot(active_b, wdown[layer], NN) + vector(b_down, layer))
        normal, root = normalize(second)
        normal_two[layer, rows, :] = normal
        put_column(rows, 2 + 2 * layer, root)
        stream[rows, :] = normal * vector(gain_two, layer) + vector(shift_two, layer)

    def add_vector(member, layer, row):
        at = 2 * member + layer
        vectors[at : at + 1, :] = vectors[at : at + 1, :] + row

    def dense_backward(layer, slot):
        rows = slot_rows(slot)
        grad = stream[rows, :]
        normal = normal_two[layer, rows, :]
        add_vector(7, layer, column_sum(grad * normal))
        add_vector(8, layer, column_sum(grad))
        root = get_column(rows, 2 + 2 * layer)
        d_second = norm_back(grad, vector(gain_two, layer), normal, root)
        d_branch = low(d_second)
        d_packed[rows, 0:512] = d_branch
        add_vector(6, layer, column_sum(wide(d_branch)))
        d_inner = low(dot(d_branch, wdown[layer], NT) * slope[layer, rows, :])
        d_packed[rows, 512:1024] = d_inner
        add_vector(5, layer, column_sum(wide(d_inner)))
        d_normed = d_second + dot(d_inner, wup[layer], NT)
        normal = normal_one[layer, rows, :]
        add_vector(3, layer, column_sum(d_normed * normal))
        add_vector(4, layer, column_sum(d_normed))
        root = get_column(rows, 1 + 2 * layer)
        first = norm_back(d_normed, vector(gain_one, layer), normal, root)
        stream[rows, :] = first
        d_attn = low(first)
        d_packed[rows, 1024:1536] = d_attn
        add_vector(2, layer, column_sum(wide(d_attn)))
        d_mixed[rows, :] = low(dot(d_attn, wout[layer], NT))

    def put_tiles(batch, first_tile, matrix):
        for tile in range(4):
            at = (first_tile + tile) * 512
            batch[at : at + 512, :] = low(matrix[:, tile * 128 : (tile + 1) * 128])

    def dense_weights(layer, batch):
        put_tiles(batch, 0, dot(active[layer], d_packed[:, 0:512], TN))
        normed = normal_one[layer] * vector(gain_one, layer) + vector(shift_one, layer)
        put_tiles(batch, 4, dot(low(normed), d_packed[:, 512:1024], TN))
        put_tiles(batch, 8, dot(low(mixed[layer]), d_packed[:, 1024:1536], TN))

    def grad_copy(pair):
        return remote(
            sent.at[pair], received.at[pair], grad_send, grad_recv.at[pair], sibling
        )

    def attend_backward(layer, first_pair, last_pair):
        first_half = lane((ROWS, 128)) < 64

        for pair in range(first_pair, last_pair):
            columns = slice(pair * 128, (pair + 1) * 128)
            q_pair = queries[layer, :, columns]
            k_pair = keys[layer, 0:KEYS, columns]
            v_pair = values[layer, 0:KEYS, columns]
            d_out = low(wide(d_mixed[:, columns]) * inverses[layer, :, columns])
            d_wide = wide(d_out)
            d_turned = jnp.transpose(d_out)
            q_turned = jnp.transpose(q_pair)
            with_out = mixed[layer, :, columns] * d_wide
            with_own = wide(own(values, layer, columns)) * d_wide - with_out
            d_q, d_k, d_v, self_score, delta, d_probs = [], [], [], [], [], []
            for half in range(2):
                inside = first_half if half == 0 else jnp.logical_not(first_half)
                delta.append(jnp.sum(jnp.where(inside, with_out, 0.0), axis=1, keepdims=True))
                self_score.append(jnp.sum(jnp.where(inside, with_own, 0.0), axis=1, keepdims=True))
                d_probs.append(
                    dot(jnp.where(inside, d_out, jnp.zeros_like(d_out)), v_pair, NT)
                )
            for half in range(2):
                exponent = probs[2 * pair + half]
                d_scores = low(wide(exponent) * (d_probs[half] - delta[half]))
                d_q.append(dot(d_scores, k_pair, NN))
                d_k.append(dot(q_turned, d_scores, NN))
                d_v.append(dot(d_turned, exponent, NN))
            self_term = wide(self_parts[layer, :, columns])
            own_score = self_term * jnp.where(first_half, self_score[0], self_score[1])
            d_query = jnp.where(first_half, d_q[0], d_q[1]) + own_score * wide(
                own(keys, layer, columns)
            )
            d_packed[:, columns] = low(d_query * SCORE_SCALE)
            part_keys[0:KEYS, :] = jnp.transpose(
                jnp.concatenate([d_k[0][0:64], d_k[1][64:128]], axis=0)
            )
            part_values[0:KEYS, :] = jnp.transpose(
                jnp.concatenate([d_v[0][0:64], d_v[1][64:128]], axis=0)
            )
            own_keys = own_score * wide(q_pair)
            own_values = self_term * d_wide
            for slot in range(2):
                rows = slice(slot * SLOT, (slot + 1) * SLOT)
                mine = block_rows(slot, core)
                d_keys[rows, columns] = part_keys[mine, :] + own_keys[rows, :]
                d_values[rows, columns] = part_values[mine, :] + own_values[rows, :]
                other = block_rows(slot, 1 - core)
                sent[pair, 0, rows, :] = low(part_keys[other, :])
                sent[pair, 1, rows, :] = low(part_values[other, :])
            grad_copy(pair).start()

    def merge_grads(pairs):
        for pair in range(*pairs):
            grad_copy(pair).wait_recv()
            at = pair * 128
            columns = slice(at, at + 128)
            d_packed[:, 512 + at : 640 + at] = low(d_keys[:, columns] + wide(received[pair, 0]))
            d_packed[:, 1024 + at : 1152 + at] = low(d_values[:, columns] + wide(received[pair, 1]))

    def wait_sent():
        remote(sent, sent, grad_send, grad_recv.at[0], sibling).wait_send()

    def input_weights(layer, batch, first_row, third, pairs):
        first, last = pairs
        count = last - first
        columns = slice(third * 512 + first * 128, third * 512 + last * 128)
        product = dot(x_round[layer], d_packed[:, columns], TN)
        for tile in range(count):
            at = first_row + (third * count + tile) * 512
            batch[at : at + 512, :] = low(product[:, tile * 128 : (tile + 1) * 128])
        if third != 1:
            at = 2 * (third // 2) + layer
            inside = slice(first * 128, last * 128)
            vectors[at : at + 1, inside] = column_sum(wide(d_packed[:, columns]))

    def input_grad(layer, slot):
        rows = slot_rows(slot)
        stream[rows, :] = stream[rows, :] + dot(d_packed[rows, :], win[layer], NT)

    def reduction(index, batch, result, rows, deep):
        return Reduction(
            place, batch, result, rows, deep, reduction_refs[7 * index : 7 * index + 7]
        )

    group_rows = [1536 * (last - first) for first, last in GROUPS]
    group_at = [sum(group_rows[:index]) for index in range(len(GROUPS))]
    one_a = reduction(0, batch_a, reduced.at[0], BATCH_ROWS, True)
    one_b = reduction(1, batch_b, reduced.at[1], BATCH_ROWS, True)
    zero_a = reduction(2, batch_c, reduced.at[2], BATCH_ROWS, True)
    groups = [
        reduction(
            3 + index,
            batch_d.at[pl.ds(at, rows)],
            reduced.at[3, pl.ds(at, rows)],
            rows,
            index == 0,
        )
        for index, (at, rows) in enumerate(zip(group_at, group_rows))
    ]
    more = ExtraReduction(
        place, extra, extra_result, extra_out, reduction_refs[7 * (3 + len(GROUPS)) :]
    )
    running = {
        "one_a": one_a,
        "one_b": one_b,
        "zero_a": zero_a,
        "first": groups[0],
        "last": groups[1],
        "more": more,
    }

    def both_slots(work):
        def step(slot, _):
            work(slot)
            return 0

        lax.fori_loop(0, 2, step, 0)

    def after(piece):
        for name in PLAN.get(piece, ()):
            running[name].advance()

    for copy in small[1:]:
        copy.wait()
    load_hidden.wait()
    gather_scale(here)
    loads[0].wait()
    project_keys(0, here)
    swap_ids.wait()
    gather_scale(there)
    swap_hidden.wait()
    project_keys(0, there)
    project_queries(0)
    swap_cot.start()
    load_cot.start()
    for load in loads[4:]:
        load.start()
    probs_out = pltpu.make_async_copy(probs, kept_probs, probs_sem.at[0])
    probs_back = pltpu.make_async_copy(kept_probs, probs, probs_sem.at[1])

    def forward(layer, _):
        whole = keys.at[layer]
        remote(whole, whole, kv_send, kv_recv.at[layer], sibling).wait()

        @pl.when(layer == 1)
        def _():
            probs_out.wait()

        attend(layer)

        @pl.when(layer == 0)
        def _():
            probs_out.start()
            wait_rest.wait()
            wait_next.wait()

        def forward_slot(slot, _):
            dense_forward(layer, slot)

            @pl.when(layer == 0)
            def _():
                project_keys(1, slot)

            return 0

        lax.fori_loop(0, 2, forward_slot, 0)

        @pl.when(layer == 0)
        def _():
            project_queries(1)

        return 0

    lax.fori_loop(0, 2, forward, 0)

    out_round[...] = low(stream[...])
    keep_out = pltpu.make_async_copy(
        out_round.at[slot_rows(here)], layer_out.at[here], out_sems.at[0]
    )
    send_out = remote(
        out_round.at[slot_rows(there)],
        layer_out.at[here],
        swap_send.at[3],
        swap_recv.at[3],
        partner,
    )
    keep_out.start()
    send_out.start()

    load_cot.wait()
    swap_cot.wait()
    stream[...] = wide(cot[...])
    every = (0, PAIRS)
    both_slots(lambda slot: dense_backward(1, slot))
    dense_weights(1, batch_a)
    one_a.advance()
    for pair in range(PAIRS):
        attend_backward(1, pair, pair + 1)
        after(f"one pair {pair}")
    probs_back.start()
    input_weights(1, batch_b, 0, 0, every)
    after("one queries")
    merge_grads(every)
    after("one merge")
    input_weights(1, batch_b, 0, 1, every)
    after("one keys")
    input_weights(1, batch_b, 0, 2, every)
    one_b.advance()
    both_slots(lambda slot: input_grad(1, slot))
    after("one input")
    both_slots(lambda slot: dense_backward(0, slot))
    after("zero dense")
    dense_weights(0, batch_c)
    zero_a.advance()
    wait_sent()
    probs_back.wait()
    for pair in range(PAIRS):
        attend_backward(0, pair, pair + 1)
        after(f"zero pair {pair}")
        if pair == GROUPS[0][1]:
            merge_grads(GROUPS[0])
            for third in range(3):
                input_weights(0, batch_d, group_at[0], third, GROUPS[0])
            groups[0].advance()
    input_weights(0, batch_d, group_at[1], 0, GROUPS[1])
    after("zero queries")
    merge_grads(GROUPS[1])
    after("zero merge")
    for third in (1, 2):
        input_weights(0, batch_d, group_at[1], third, GROUPS[1])
    groups[1].advance()
    after("zero values")
    keep_grad = pltpu.make_async_copy(
        d_mixed.at[slot_rows(here)], grad_hidden.at[here], out_sems.at[1]
    )

    def grad_piece(start, count):
        return remote(
            d_mixed.at[pl.ds(pl.multiple_of(there * SLOT + start, 16), count)],
            grad_hidden.at[here, pl.ds(start, count)],
            swap_send.at[4],
            swap_recv.at[4],
            partner,
        )


    def hidden_grad(slot):
        rows = slot_rows(slot)
        input_grad(0, slot)
        d_mixed[rows, :] = low(stream[rows, :] * get_column(rows, 5))

    hidden_grad(there)
    after("zero there")
    hidden_grad(here)
    keep_grad.start()
    after("zero here")

    genes = jnp.zeros((GENE_ROWS, 128), jnp.float32)
    for slot in range(2):
        rows = slot_rows(slot)
        is_high, is_low = slot_ids(slot)
        per_token = jnp.sum(stream[rows, :] * wide(hidden[rows, :]), axis=1, keepdims=True)
        row = jnp.transpose(jnp.broadcast_to(per_token, (SLOT, 128)))
        for piece in split_three(jnp.where(is_low, row, 0.0)):
            genes = genes + dot(is_high, piece, NT)
    extra[0:GENE_ROWS, :] = genes
    for index in range(18):
        for tile in range(4):
            at = GENE_ROWS + 4 * index + tile
            extra[at : at + 1, :] = vectors[index : index + 1, tile * 128 : (tile + 1) * 128]
    after("genes")
    more.advance()
    for index, name in enumerate(ENDING):
        running[name].advance()
        if index % 2 == 0 and index < 16:
            grad_piece(index * 16, 32).start()
    for one in running.values():
        assert one.at == one.last + 1
    wait_sent()
    keep_out.wait()
    send_out.wait()
    keep_grad.wait()
    grad_piece(0, SLOT).wait()


def run_model(hidden_in, cotangent, gene_ids, unknown_count, table, weights, vector_args):
    f32, bf16 = jnp.float32, jnp.bfloat16
    smem = pl.BlockSpec(memory_space=pltpu.SMEM)
    anywhere = pl.BlockSpec(memory_space=pl.ANY)
    scratch = [
        pltpu.VMEM((ROWS, 512), bf16),
        pltpu.VMEM((3, 8, SLOT), jnp.int32),
        pltpu.VMEM((2, 512, 1536), bf16),
        pltpu.VMEM((2, 512, 512), bf16),
        pltpu.VMEM((2, 512, 512), bf16),
        pltpu.VMEM((2, 512, 512), bf16),
        pltpu.VMEM((ROWS, 512), f32),
        pltpu.VMEM((2, ROWS, 512), bf16),
        pltpu.VMEM((2, ROWS, 512), bf16),
        pltpu.VMEM((2, GENES, 512), bf16),
        pltpu.VMEM((2, GENES, 512), bf16),
        pltpu.VMEM((HEADS, ROWS, KEYS), bf16),
        pltpu.VMEM((ROWS, 128), f32),
        pltpu.VMEM((2, ROWS, 512), f32),
        pltpu.VMEM((2, ROWS, 512), bf16),
        pltpu.VMEM((2, ROWS, 512), f32),
        pltpu.VMEM((2, ROWS, 512), f32),
        pltpu.VMEM((2, ROWS, 512), f32),
        pltpu.VMEM((2, ROWS, 512), f32),
        pltpu.VMEM((2, ROWS, 512), bf16),
        pltpu.VMEM((ROWS, 512), bf16),
        pltpu.VMEM((ROWS, 1536), bf16),
        pltpu.VMEM((ROWS, 512), f32),
        pltpu.VMEM((ROWS, 512), f32),
        pltpu.VMEM((GENES, 128), f32),
        pltpu.VMEM((GENES, 128), f32),
        pltpu.VMEM((PAIRS, 2, ROWS, 128), bf16),
        pltpu.VMEM((PAIRS, 2, ROWS, 128), bf16),
        pltpu.VMEM((8, KEYS), f32),
        pltpu.VMEM((24, 512), f32),
        pltpu.VMEM((ROWS, 512), bf16),
        pltpu.VMEM((EXTRA_ROWS, 128), f32),
        pltpu.VMEM((BATCH_ROWS, 128), bf16),
        pltpu.VMEM((BATCH_ROWS, 128), bf16),
        pltpu.VMEM((BATCH_ROWS, 128), bf16),
        pltpu.VMEM((BATCH_ROWS, 128), bf16),
        pltpu.VMEM((EXTRA_ROWS, 128), f32),
        pltpu.SemaphoreType.DMA((16,)),
        pltpu.SemaphoreType.DMA((5,)),
        pltpu.SemaphoreType.DMA((5,)),
        pltpu.SemaphoreType.DMA,
        pltpu.SemaphoreType.DMA((2,)),
        pltpu.SemaphoreType.DMA,
        pltpu.SemaphoreType.DMA((PAIRS,)),
        pltpu.SemaphoreType.DMA((2,)),
        pltpu.SemaphoreType.DMA((2,)),
    ]
    for _ in range(3):
        scratch += Reduction.scratch(BATCH_ROWS, True)
    for index, (first, last) in enumerate(GROUPS):
        scratch += Reduction.scratch(1536 * (last - first), index == 0)
    scratch += ExtraReduction.scratch()
    scratch += [pltpu.VMEM((2, SLOT), jnp.int32), pltpu.VMEM((GENE_ROWS, 128), f32)]
    scratch += [pltpu.VMEM((2, 512), f32)] * 9
    outs = (
        jax.ShapeDtypeStruct((2, SLOT, 512), bf16),
        jax.ShapeDtypeStruct((2, SLOT, 512), bf16),
        jax.ShapeDtypeStruct((4, BATCH_ROWS, 128), bf16),
        jax.ShapeDtypeStruct((EXTRA_ROWS, 128), f32),
        jax.ShapeDtypeStruct((HEADS, ROWS, KEYS), bf16),
    )
    return pl.pallas_call(
        model_kernel,
        out_shape=outs,
        in_specs=[anywhere] * 3 + [smem] + [anywhere] * 14,
        out_specs=(anywhere,) * 5,
        scratch_shapes=scratch,
        compiler_params=pltpu.CompilerParams(
            collective_id=0, has_side_effects=True, vmem_limit_bytes=255 << 18
        ),
        name="model",
    )(hidden_in, cotangent, gene_ids, unknown_count, table, *weights, *vector_args)


def finish_kernel(layer_in, hidden_grad_in, reduced, extra, *refs):
    layer_out, hidden_out, g_inputs, g_output, g_up, g_down, genes = refs[:7]
    vector_outs = refs[7:16]
    rounded, narrow, rows_out, wide_in, wide_rest, extra_rows, in_sems, out_sems = refs[16:]
    sources = [layer_in, hidden_grad_in]
    loads = [
        pltpu.make_async_copy(sources[i], rounded.at[i], in_sems.at[i]) for i in range(2)
    ] + [pltpu.make_async_copy(reduced.at[i], narrow.at[i], in_sems.at[2 + i]) for i in range(4)]
    loads.append(pltpu.make_async_copy(extra, extra_rows, in_sems.at[6]))
    for load in loads[:1] + loads[6:] + loads[1:6]:
        load.start()
    stores = []

    def send(source, target):
        store = pltpu.make_async_copy(source, target, out_sems.at[len(stores)])
        store.start()
        stores.append(store)

    for index, target in enumerate((layer_out, hidden_out)):
        loads[index].wait()
        rows_out[index] = wide(rounded[index])
        send(rows_out.at[index], target)
    for layer in (1, 0):
        base = 2 * (1 - layer)
        loads[2 + base].wait()
        for index, target in enumerate((g_down, g_up, g_output)):
            for tile in range(4):
                at = (4 * index + tile) * 512
                wide_rest[layer, index, :, tile * 128 : (tile + 1) * 128] = wide(
                    narrow[base, at : at + 512, :]
                )
            send(wide_rest.at[layer, index], target.at[layer])
        loads[3 + base].wait()
        at = 0
        for first, last in GROUPS if layer == 0 else ((0, PAIRS),):
            for third in range(3):
                for pair in range(first, last):
                    column = third * 512 + pair * 128
                    wide_in[layer, :, column : column + 128] = wide(
                        narrow[base + 1, at : at + 512, :]
                    )
                    at += 512
        send(wide_in.at[layer], g_inputs.at[layer])
    loads[6].wait()
    genes[...] = extra_rows[0:GENE_ROWS, :]
    for member in range(9):
        for layer in range(2):
            for tile in range(4):
                at = GENE_ROWS + 4 * (2 * member + layer) + tile
                vector_outs[member][layer : layer + 1, tile * 128 : (tile + 1) * 128] = extra_rows[
                    at : at + 1, :
                ]
    for store in stores:
        store.wait()


def finish(layer_out, grad_hidden, reduced, extra):
    f32, bf16 = jnp.float32, jnp.bfloat16
    vmem = pl.BlockSpec(memory_space=pltpu.VMEM)
    anywhere = pl.BlockSpec(memory_space=pl.ANY)
    outs = [
        jax.ShapeDtypeStruct((2, SLOT, 512), f32),
        jax.ShapeDtypeStruct((2, SLOT, 512), f32),
        jax.ShapeDtypeStruct((2, 512, 1536), f32),
        jax.ShapeDtypeStruct((2, 512, 512), f32),
        jax.ShapeDtypeStruct((2, 512, 512), f32),
        jax.ShapeDtypeStruct((2, 512, 512), f32),
        jax.ShapeDtypeStruct((GENE_ROWS, 128), f32),
    ] + [jax.ShapeDtypeStruct((2, 512), f32)] * 9
    return pl.pallas_call(
        finish_kernel,
        out_shape=outs,
        in_specs=[anywhere] * 4,
        out_specs=[anywhere] * 6 + [vmem] * 10,
        scratch_shapes=[
            pltpu.VMEM((2, 2, SLOT, 512), bf16),
            pltpu.VMEM((4, BATCH_ROWS, 128), bf16),
            pltpu.VMEM((2, 2, SLOT, 512), f32),
            pltpu.VMEM((2, 512, 1536), f32),
            pltpu.VMEM((2, 3, 512, 512), f32),
            pltpu.VMEM((EXTRA_ROWS, 128), f32),
            pltpu.SemaphoreType.DMA((7,)),
            pltpu.SemaphoreType.DMA((10,)),
        ],
        compiler_params=pltpu.CompilerParams(vmem_limit_bytes=63 << 20),
        name="finish",
    )(layer_out, grad_hidden, reduced, extra)


def shards(
    hidden_in,
    gene_ids,
    unknown_count,
    gene_scale,
    w_inputs,
    b_query,
    b_value,
    w_output,
    b_output,
    gain_one,
    shift_one,
    w_up,
    b_up,
    w_down,
    b_down,
    gain_two,
    shift_two,
    cotangent,
):
    gene_count = gene_scale.shape[0]
    table = jnp.pad(gene_scale, (0, GENE_ROWS * 128 - gene_count)).reshape(GENE_ROWS, 128)
    layer_out, grad_hidden, reduced, extra, _ = run_model(
        hidden_in,
        cotangent,
        gene_ids,
        unknown_count,
        table,
        (w_inputs, w_output, w_up, w_down),
        (b_query, b_value, b_output, gain_one, shift_one, b_up, b_down, gain_two, shift_two),
    )
    (
        layer_out,
        grad_hidden,
        g_inputs,
        g_output,
        g_up,
        g_down,
        genes,
        g_b_query,
        g_b_value,
        g_b_output,
        g_gain_one,
        g_shift_one,
        g_b_up,
        g_b_down,
        g_gain_two,
        g_shift_two,
    ) = finish(layer_out, grad_hidden, reduced, extra)
    return (
        layer_out,
        grad_hidden,
        genes.reshape(-1)[:gene_count],
        g_inputs,
        g_b_query,
        g_b_value,
        g_output,
        g_b_output,
        g_gain_one,
        g_shift_one,
        g_up,
        g_b_up,
        g_down,
        g_b_down,
        g_gain_two,
        g_shift_two,
    )


def solution(mesh):
    placed = (
        P("dp", "blk", None),
        P("dp", "blk"),
        P("dp"),
        P(),
        P(),
        P(),
        P(),
        P(),
        P(),
        P(),
        P(),
        P(),
        P(),
        P(),
        P(),
        P(),
        P(),
        P("dp", "blk", None),
    )
    return jax.shard_map(
        shards,
        mesh=mesh,
        in_specs=placed,
        out_specs=(
            P("dp", "blk", None),
            P("dp", "blk", None),
            P(),
            P(),
            P(),
            P(),
            P(),
            P(),
            P(),
            P(),
            P(),
            P(),
            P(),
            P(),
            P(),
            P(),
        ),
        check_vma=False,
    )
```

```python
import jax
import jax.numpy as jnp
from jax import lax
from jax.experimental import pallas as pl
from jax.experimental.pallas import tpu as pltpu
from jax.sharding import PartitionSpec as P

HEADS = 8
MESH = pl.DeviceIdType.MESH
AXIS_ORDER = ((0, 1, 2), (1, 2, 0), (2, 0, 1))
BATCH_ROWS = 6144
EXTRA_ROWS = 576
EXTRA_HALF = EXTRA_ROWS // 2
EXTRA_PIECE = EXTRA_HALF // 4


class Place:
    def __init__(self):
        dp = lax.axis_index("dp")
        blk = lax.axis_index("blk")
        self.core = blk & 1
        self.x_hi = blk >> 1
        self.coord = (self.x_hi * 2 + (dp & 1), dp >> 3, (dp >> 1) & 3)
        self.next = [
            [(coord + distance) & 3 for distance in range(4)] for coord in self.coord
        ]
        self.peers = [
            [self.device(axis, self.next[axis][distance]) for distance in range(4)]
            for axis in range(3)
        ]
        self.other_core = (dp, blk ^ 1)

    def device(self, axis, place):
        x, y, z = (place if axis == index else self.coord[index] for index in range(3))
        return (y * 8 + z * 2 + (x & 1), (x & 2) + self.core)

    def sibling(self):
        return self.other_core

    def peer(self, axis, distance):
        return self.peers[axis][distance]


def greet(place):
    barrier = pltpu.get_barrier_semaphore()
    others = [place.sibling()]
    for axis in range(3):
        for distance in (1, 2, 3):
            others.append(place.peer(axis, distance))
    for other in others:
        pl.semaphore_signal(barrier, inc=1, device_id=other, device_id_type=MESH)
    pl.semaphore_wait(barrier, len(others))


def remote(src, dst, send_sem, recv_sem, device):
    return pltpu.make_async_remote_copy(
        src_ref=src,
        dst_ref=dst,
        send_sem=send_sem,
        recv_sem=recv_sem,
        device_id=device,
        device_id_type=MESH,
    )


class Reduction:
    def __init__(self, place, batch, result, rows, deep, refs):
        self.place = place
        self.batch = batch
        self.result = result
        self.half = rows // 2
        self.part = rows // 6
        self.first = self.part // 4
        self.piece = self.first // 4 if deep else self.first
        self.from_core, self.from_first, self.from_second, self.from_third = refs[:4]
        self.send, self.recv, self.local = refs[4:]
        self.mine = place.core * self.half
        self.other = (1 - place.core) * self.half
        if deep:
            self.steps = ["core", "scatter0", "scatter1", "exchange2", "gather1", "gather0", "share"]
        else:
            self.steps = ["core", "scatter0", "exchange1", "exchange2", "gather0", "share"]
        self.deep = deep
        self.at = 0
        self.last = len(self.steps)

    def scratch(rows, deep):
        first = rows // 24
        piece = first // 4 if deep else first
        second = (3, 3, piece, 128) if deep else (3, 4, piece, 128)
        return [
            pltpu.VMEM((rows // 2, 128), jnp.bfloat16),
            pltpu.VMEM((3, 3, first, 128), jnp.bfloat16),
            pltpu.VMEM(second, jnp.bfloat16),
            pltpu.VMEM((3, 4, piece, 128), jnp.bfloat16),
            pltpu.SemaphoreType.DMA,
            pltpu.SemaphoreType.DMA((7,)),
            pltpu.SemaphoreType.DMA((3,)),
        ]

    def advance(self):
        if self.at > 0:
            name = self.steps[self.at - 1]
            self.run(name, "finish", self.at - 1)
        if self.at < len(self.steps):
            self.run(self.steps[self.at], "start", self.at)
        self.at += 1

    def run(self, name, action, index):
        if name[-1] in "012":
            getattr(self, name[:-1] + "_" + action)(int(name[-1]), index)
        else:
            getattr(self, name + "_" + action)(index)

    def wait_bytes(self, like, index):
        remote(like, like, self.send, self.recv.at[index], self.place.sibling()).wait()

    def base(self, part, steps):
        rows = self.mine + part * self.part
        if steps > 0:
            rows = rows + self.place.coord[AXIS_ORDER[part][0]] * self.first
        if steps > 1 and self.deep:
            rows = rows + self.place.coord[AXIS_ORDER[part][1]] * self.piece
        return pl.multiple_of(rows, 16)

    def block(self, part):
        return pl.ds(self.base(part, 2), self.piece)

    def core_copy(self, index):
        rows = pl.ds(pl.multiple_of(self.other, 16), self.half)
        return remote(
            self.batch.at[rows], self.from_core, self.send, self.recv.at[index], self.place.sibling()
        )

    def core_start(self, index):
        self.core_copy(index).start()

    def core_finish(self, index):
        self.core_copy(index).wait()
        size = self.half // 12

        def add(i, _):
            here = pl.ds(pl.multiple_of(self.mine + i * size, 16), size)
            there = pl.ds(pl.multiple_of(i * size, 16), size)
            self.batch[here] = (
                self.batch[here].astype(jnp.float32) + self.from_core[there].astype(jnp.float32)
            ).astype(jnp.bfloat16)
            return 0

        lax.fori_loop(0, 12, add, 0)

    def scatter_start(self, step, index):
        size = self.first if step == 0 else self.piece
        landing = self.from_first if step == 0 else self.from_second
        for part in range(3):
            axis = AXIS_ORDER[part][step]
            for distance in (1, 2, 3):
                target = self.place.next[axis][distance]
                rows = pl.multiple_of(self.base(part, step) + target * size, 16)
                remote(
                    self.batch.at[pl.ds(rows, size)],
                    landing.at[part, distance - 1],
                    self.send,
                    self.recv.at[index],
                    self.place.peer(axis, distance),
                ).start()

    def scatter_finish(self, step, index):
        size = self.first if step == 0 else self.piece
        landing = self.from_first if step == 0 else self.from_second
        self.wait_bytes(landing, index)
        for part in range(3):
            rows = pl.ds(self.base(part, step + 1), size)
            total = self.batch[rows].astype(jnp.float32)
            for distance in (1, 2, 3):
                total = total + landing[part, distance - 1].astype(jnp.float32)
            self.batch[rows] = total.astype(jnp.bfloat16)

    def exchange_start(self, step, index):
        landing = self.from_second if step == 1 else self.from_third
        for part in range(3):
            axis = AXIS_ORDER[part][step]
            for distance in (1, 2, 3):
                remote(
                    self.batch.at[self.block(part)],
                    landing.at[part, self.place.coord[axis]],
                    self.send,
                    self.recv.at[index],
                    self.place.peer(axis, distance),
                ).start()

    def exchange_finish(self, step, index):
        landing = self.from_second if step == 1 else self.from_third
        for part in range(3):
            landing[part, self.place.coord[AXIS_ORDER[part][step]]] = self.batch[self.block(part)]
        self.wait_bytes(self.from_second if self.deep else self.from_first, index)
        for part in range(3):
            terms = [landing[part, place].astype(jnp.float32) for place in range(4)]
            total = (terms[0] + terms[1]) + (terms[2] + terms[3])
            self.batch[self.block(part)] = total.astype(jnp.bfloat16)

    def local_copies(self):
        return [
            pltpu.make_async_copy(
                self.batch.at[self.block(part)],
                self.result.at[self.block(part)],
                self.local.at[part],
            )
            for part in range(3)
        ]

    def gather_start(self, step, index):
        from_batch = step == 1 or not self.deep
        size = self.first if step == 0 else self.piece
        if from_batch:
            for copy in self.local_copies():
                copy.start()
        source = self.batch if from_batch else self.result
        for part in range(3):
            axis = AXIS_ORDER[part][step]
            rows = pl.ds(self.base(part, step + 1), size)
            for distance in (1, 2, 3):
                remote(
                    source.at[rows],
                    self.result.at[rows],
                    self.send,
                    self.recv.at[index],
                    self.place.peer(axis, distance),
                ).start()

    def gather_finish(self, step, index):
        if step == 1 or not self.deep:
            for copy in self.local_copies():
                copy.wait()
        self.wait_bytes(self.from_first if step == 0 else self.from_second, index)

    def share_copy(self, index):
        rows = pl.ds(pl.multiple_of(self.mine, 16), self.half)
        return remote(
            self.result.at[rows],
            self.result.at[rows],
            self.send,
            self.recv.at[index],
            self.place.sibling(),
        )

    def share_start(self, index):
        self.share_copy(index).start()

    def share_finish(self, index):
        self.share_copy(index).wait()


class ExtraReduction:
    def __init__(self, place, rows_ref, result, out, refs):
        self.place = place
        self.ref = rows_ref
        self.result = result
        self.out = out
        self.from_core, self.from_x, self.from_plane, self.send, self.recv, self.local = refs
        self.mine = place.core * EXTRA_HALF
        self.other = (1 - place.core) * EXTRA_HALF
        self.at = 0
        self.last = 6

    def scratch():
        return [
            pltpu.VMEM((EXTRA_HALF, 128), jnp.float32),
            pltpu.VMEM((3, EXTRA_PIECE, 128), jnp.float32),
            pltpu.VMEM((2, 4, EXTRA_PIECE, 128), jnp.float32),
            pltpu.SemaphoreType.DMA,
            pltpu.SemaphoreType.DMA((6,)),
            pltpu.SemaphoreType.DMA,
        ]

    def advance(self):
        if self.at > 0:
            self.finish(self.at - 1)
        if self.at < 6:
            self.start(self.at)
        self.at += 1

    def piece(self, quarter):
        return pl.ds(pl.multiple_of(self.mine + quarter * EXTRA_PIECE, 8), EXTRA_PIECE)

    def copy(self, index, source, target, device):
        return remote(source, target, self.send, self.recv.at[index], device)

    def core_copy(self):
        rows = pl.ds(pl.multiple_of(self.other, 8), EXTRA_HALF)
        return self.copy(0, self.ref.at[rows], self.from_core, self.place.sibling())

    def share_copy(self):
        rows = pl.ds(pl.multiple_of(self.mine, 8), EXTRA_HALF)
        return self.copy(5, self.result.at[rows], self.out.at[rows], self.place.sibling())

    def keep_copy(self):
        rows = pl.ds(pl.multiple_of(self.mine, 8), EXTRA_HALF)
        return pltpu.make_async_copy(self.result.at[rows], self.out.at[rows], self.local)

    def start(self, index):
        rows = self.piece(self.place.coord[0])
        if index == 0:
            self.core_copy().start()
            return
        if index == 5:
            self.share_copy().start()
            self.keep_copy().start()
            return
        for distance in (1, 2, 3):
            if index == 1:
                target = self.place.next[0][distance]
                source, target, axis = self.ref.at[self.piece(target)], self.from_x.at[distance - 1], 0
            elif index == 4:
                source, target, axis = self.result.at[rows], self.result.at[rows], 0
            else:
                axis = index - 1
                source = self.ref.at[rows]
                target = self.from_plane.at[axis - 1, self.place.coord[axis]]
            self.copy(index, source, target, self.place.peer(axis, distance)).start()

    def finish(self, index):
        rows = self.piece(self.place.coord[0])
        if index == 0:
            self.core_copy().wait()
            half = pl.ds(pl.multiple_of(self.mine, 8), EXTRA_HALF)
            self.ref[half] = self.ref[half] + self.from_core[...]
            return
        if index == 5:
            self.share_copy().wait()
            self.keep_copy().wait()
            return
        if index in (2, 3):
            self.from_plane[index - 2, self.place.coord[index - 1]] = self.ref[rows]
        self.copy(index, self.from_x, self.from_x, self.place.sibling()).wait()
        if index == 1:
            self.ref[rows] = self.ref[rows] + self.from_x[0] + self.from_x[1] + self.from_x[2]
        elif index in (2, 3):
            terms = [self.from_plane[index - 2, place] for place in range(4)]
            target = self.ref if index == 2 else self.result
            target[rows] = (terms[0] + terms[1]) + (terms[2] + terms[3])


ROWS = 512
SLOT = 256
KEYS = 768
GENES = 1024
GENE_ROWS = 480
PAIRS = 4
GROUPS = ((0, 2), (2, 4))
PLAN = {
    "one pair 1": ("one_a",),
    "one keys": ("one_a",),
    "zero dense": ("one_b", "one_a"),
    "zero pair 1": ("zero_a",),
    "zero pair 2": ("one_b", "one_a"),
    "zero queries": ("first",),
    "zero merge": ("zero_a",),
    "zero values": ("one_b", "one_a"),
    "zero here": ("last", "first"),
    "genes": ("zero_a",),
}
ENDING = (
    "more", "last", "first", "one_b", "one_a",
    "zero_a", "last", "more", "first", "one_b",
    "last", "more", "zero_a", "first", "one_a", "one_b",
    "last", "more", "zero_a", "first",
    "more", "one_b", "zero_a", "first", "last", "more",
)
NEG = -1e30
SCORE_SCALE = 0.125
NN = (((1,), (0,)), ((), ()))
NT = (((1,), (1,)), ((), ()))
TN = (((0,), (0,)), ((), ()))


def dot(left, right, dims):
    return lax.dot_general(left, right, dims, preferred_element_type=jnp.float32)


def low(values):
    return values.astype(jnp.bfloat16)


def wide(values):
    return values.astype(jnp.float32)


def lane(shape):
    return lax.broadcasted_iota(jnp.int32, shape, 1)


def normalize(values):
    center = values - jnp.mean(values, axis=1, keepdims=True)
    root = lax.rsqrt(jnp.mean(center * center, axis=1, keepdims=True) + 1e-05)
    return center * root, root


def norm_back(grad, gain, normal, root):
    u = grad * gain
    mean = jnp.mean(u, axis=1, keepdims=True)
    along = jnp.mean(u * normal, axis=1, keepdims=True)
    return (u - mean - normal * along) * root


def column_sum(values):
    return jnp.sum(values, axis=0, keepdims=True)


def split_three(values):
    first = low(values)
    rest = values - wide(first)
    second = low(rest)
    third = low(rest - wide(second))
    return first, second, third


def model_kernel(
    hidden_in,
    cotangent,
    ids_far,
    unknown,
    table_far,
    w_inputs,
    w_output,
    w_up,
    w_down,
    *more_refs,
):
    vectors_far, rest = more_refs[:9], more_refs[9:]
    near, rest = rest[-11:], rest[:-11]
    model_body(
        hidden_in,
        cotangent,
        unknown,
        w_inputs,
        w_output,
        w_up,
        w_down,
        (ids_far, table_far) + tuple(vectors_far),
        near,
        *rest,
    )


def model_body(
    hidden_in,
    cotangent,
    unknown,
    w_inputs,
    w_output,
    w_up,
    w_down,
    far,
    near,
    layer_out,
    grad_hidden,
    reduced,
    extra_out,
    kept_probs,
    hidden,
    ids,
    win,
    wout,
    wup,
    wdown,
    stream,
    x_round,
    queries,
    keys,
    values,
    probs,
    stats,
    inverses,
    self_parts,
    mixed,
    normal_one,
    normal_two,
    slope,
    active,
    d_mixed,
    d_packed,
    d_keys,
    d_values,
    part_keys,
    part_values,
    sent,
    received,
    bias,
    vectors,
    out_round,
    extra,
    batch_a,
    batch_b,
    batch_c,
    batch_d,
    extra_result,
    load_sems,
    swap_send,
    swap_recv,
    kv_send,
    kv_recv,
    grad_send,
    grad_recv,
    probs_sem,
    out_sems,
    *reduction_refs,
):
    small = [
        pltpu.make_async_copy(source, target, load_sems.at[5 + index])
        for index, (source, target) in enumerate(zip(far, near))
    ]
    for copy in small:
        copy.start()
    ids_in, table, b_query, b_value, b_output, gain_one, shift_one = near[:7]
    b_up, b_down, gain_two, shift_two = near[7:]
    place = Place()
    cot = d_mixed
    core, here = place.core, place.x_hi
    there = 1 - here
    partner = place.peer(0, 2)
    sibling = place.sibling()

    def slot_rows(slot):
        return pl.ds(pl.multiple_of(slot * SLOT, SLOT), SLOT)

    def block_rows(slot, which):
        return pl.ds(pl.multiple_of((2 * slot + which) * SLOT, SLOT), SLOT)

    load_hidden = pltpu.make_async_copy(
        hidden_in.at[here], hidden.at[slot_rows(here)], load_sems.at[0]
    )
    load_cot = pltpu.make_async_copy(cotangent.at[here], cot.at[slot_rows(here)], load_sems.at[1])
    loads = []
    for layer in range(2):
        for index, (source, target) in enumerate(
            ((w_inputs, win), (w_output, wout), (w_up, wup), (w_down, wdown))
        ):
            loads.append(
                pltpu.make_async_copy(
                    source.at[layer],
                    target.at[layer],
                    load_sems.at[4 if layer == 1 else 2 if index == 0 else 3],
                )
            )
    load_hidden.start()
    for load in loads[0:4]:
        load.start()
    wait_rest = pltpu.make_async_copy(w_inputs.at[0], win.at[0], load_sems.at[3])
    wait_next = pltpu.make_async_copy(w_inputs, win, load_sems.at[4])
    greet(place)
    small[0].wait()
    for cell in range(2):
        ids[cell] = jnp.broadcast_to(ids_in[cell : cell + 1, :], (8, SLOT))
    known = GENES - unknown[here]

    half_slot = SLOT // 2

    def swap_hidden(index):
        start = pl.multiple_of(index * half_slot, half_slot)
        return remote(
            hidden_in.at[there, pl.ds(start, half_slot)],
            hidden.at[pl.ds(pl.multiple_of(here * SLOT + start, half_slot), half_slot)],
            swap_send.at[5 * index],
            swap_recv.at[5 * index],
            partner,
        )

    swap_ids = remote(ids.at[there], ids.at[2], swap_send.at[1], swap_recv.at[1], partner)
    swap_cot = remote(
        cotangent.at[there],
        cot.at[slot_rows(here)],
        swap_send.at[2],
        swap_recv.at[2],
        partner,
    )
    swap_ids.start()
    for index in range(2):
        swap_hidden(index).start()

    bias[...] = jnp.where(lane((8, KEYS)) < known, 0.0, NEG)
    for slot in range(2):
        position = (2 * slot + core) * SLOT + lax.broadcasted_iota(jnp.int32, (SLOT, 128), 0)
        stats[slot * SLOT : (slot + 1) * SLOT, :] = jnp.where(position >= known, 0.0, NEG)
    part_keys[KEYS:GENES, :] = jnp.zeros((GENES - KEYS, 128), jnp.float32)
    part_values[KEYS:GENES, :] = jnp.zeros((GENES - KEYS, 128), jnp.float32)
    vectors[...] = jnp.zeros_like(vectors)
    extra[...] = jnp.zeros_like(extra)

    def slot_ids(slot):
        row = jnp.where(slot == here, ids[here, 0:1, :], ids[2, 0:1, :])
        high = lax.shift_right_logical(row, 7)
        lowest = lax.bitwise_and(row, 127)
        is_high = lax.broadcasted_iota(jnp.int32, (GENE_ROWS, SLOT), 0) == high
        is_low = lax.broadcasted_iota(jnp.int32, (128, SLOT), 0) == lowest
        return low(jnp.where(is_high, 1.0, 0.0)), is_low

    def gather_scale(slot):
        is_high, is_low = slot_ids(slot)
        total = jnp.zeros((128, SLOT), jnp.float32)
        for piece in split_three(table[...]):
            total = total + dot(piece, is_high, TN)
        row = column_sum(jnp.where(is_low, total, 0.0))
        put_column(slot_rows(slot), 5, jnp.transpose(jnp.broadcast_to(row, (128, SLOT))))

    def put_column(rows, at, column):
        stats[rows, :] = jnp.where(lane((SLOT, 128)) == at, column, stats[rows, :])

    def get_column(rows, at):
        return stats[rows, :][:, at : at + 1]

    def vector(ref, layer):
        return ref[pl.ds(layer, 1), :]

    def project_part(layer, slot, start, count):
        rows = pl.ds(pl.multiple_of(slot * SLOT + start, count), count)
        mine = pl.ds(pl.multiple_of((2 * slot + core) * SLOT + start, count), count)
        if layer == 0:
            stream[rows, :] = wide(hidden[rows, :]) * get_column(rows, 5)
        x_b = low(stream[rows, :])
        x_round[layer, rows, :] = x_b
        weights = win.at[layer]
        keys[layer, mine, :] = low(dot(x_b, weights[:, 512:1024], NN))
        values[layer, mine, :] = low(
            dot(x_b, weights[:, 1024:1536], NN) + vector(b_value, layer)
        )
        for ref in (keys, values):
            remote(
                ref.at[layer, mine], ref.at[layer, mine], kv_send, kv_recv.at[layer], sibling
            ).start()

    def project_keys(layer, slot):
        project_part(layer, slot, 0, SLOT)

    def project_halves(slot, arrives):
        def step(index, _):
            if arrives:
                swap_hidden(index).wait()
            project_part(0, slot, index * half_slot, half_slot)
            return 0

        lax.fori_loop(0, 2, step, 0)

    def project_queries(layer):
        query = dot(x_round[layer], win[layer, :, 0:512], NN) + vector(b_query, layer)
        queries[layer] = low(wide(low(query)) * SCORE_SCALE)

    def own(ref, layer, columns):
        return jnp.concatenate(
            [ref[layer, block_rows(slot, core), columns] for slot in range(2)], axis=0
        )

    def attend(layer):
        first_half = lane((ROWS, 128)) < 64
        first_keys = lane((KEYS, 128)) < 64

        for pair in range(PAIRS):
            columns = slice(pair * 128, (pair + 1) * 128)
            q_pair = queries[layer, :, columns]
            k_pair = keys[layer, 0:KEYS, columns]
            v_pair = values[layer, 0:KEYS, columns]
            product = wide(q_pair) * wide(own(keys, layer, columns))
            found, self_terms = [], []
            for half in range(2):
                inside = first_half if half == 0 else jnp.logical_not(first_half)
                self_score = (
                    jnp.sum(jnp.where(inside, product, 0.0), axis=1, keepdims=True)
                    + stats[:, 0:1]
                )
                scores = dot(jnp.where(inside, q_pair, jnp.zeros_like(q_pair)), k_pair, NT)
                scores = scores + bias[0:1, :]
                top = jnp.maximum(jnp.max(scores, axis=1, keepdims=True), self_score)
                exponent = low(jnp.exp(scores - top))
                probs[2 * pair + half] = exponent
                with_ones = jnp.where(
                    first_keys if half == 0 else jnp.logical_not(first_keys),
                    v_pair,
                    jnp.ones_like(v_pair),
                )
                found.append(dot(exponent, with_ones, NN))
                self_terms.append(jnp.exp(self_score - top))
            self_low = low(jnp.where(first_half, self_terms[0], self_terms[1]))
            self_term = wide(self_low)
            sums = pltpu.roll(jnp.where(first_half, found[1], found[0]), 64, 1)
            inverse = 1.0 / (sums + self_term)
            total = jnp.where(first_half, found[0], found[1])
            total = total + self_term * wide(own(values, layer, columns))
            mixed[layer, :, columns] = total * inverse
            inverses[layer, :, columns] = inverse
            self_parts[layer, :, columns] = self_low

    def dense_forward(layer, slot):
        rows = slot_rows(slot)
        mixed_b = low(mixed[layer, rows, :])
        first = stream[rows, :] + (dot(mixed_b, wout[layer], NN) + vector(b_output, layer))
        normal, root = normalize(first)
        normal_one[layer, rows, :] = normal
        put_column(rows, 1 + 2 * layer, root)
        normed = normal * vector(gain_one, layer) + vector(shift_one, layer)
        inner = dot(low(normed), wup[layer], NN) + vector(b_up, layer)
        share = 0.5 * (1.0 + lax.erf(inner * 0.7071067811865476))
        slope[layer, rows, :] = share + inner * (
            0.3989422804014327 * jnp.exp(inner * inner * -0.5)
        )
        active_b = low(inner * share)
        active[layer, rows, :] = active_b
        second = normed + (dot(active_b, wdown[layer], NN) + vector(b_down, layer))
        normal, root = normalize(second)
        normal_two[layer, rows, :] = normal
        put_column(rows, 2 + 2 * layer, root)
        stream[rows, :] = normal * vector(gain_two, layer) + vector(shift_two, layer)

    def add_vector(member, layer, row):
        at = 2 * member + layer
        vectors[at : at + 1, :] = vectors[at : at + 1, :] + row

    def dense_backward(layer, slot):
        rows = slot_rows(slot)
        grad = stream[rows, :]
        normal = normal_two[layer, rows, :]
        add_vector(7, layer, column_sum(grad * normal))
        add_vector(8, layer, column_sum(grad))
        root = get_column(rows, 2 + 2 * layer)
        d_second = norm_back(grad, vector(gain_two, layer), normal, root)
        d_branch = low(d_second)
        d_packed[rows, 0:512] = d_branch
        add_vector(6, layer, column_sum(wide(d_branch)))
        d_inner = low(dot(d_branch, wdown[layer], NT) * slope[layer, rows, :])
        d_packed[rows, 512:1024] = d_inner
        add_vector(5, layer, column_sum(wide(d_inner)))
        d_normed = d_second + dot(d_inner, wup[layer], NT)
        normal = normal_one[layer, rows, :]
        add_vector(3, layer, column_sum(d_normed * normal))
        add_vector(4, layer, column_sum(d_normed))
        root = get_column(rows, 1 + 2 * layer)
        first = norm_back(d_normed, vector(gain_one, layer), normal, root)
        stream[rows, :] = first
        d_attn = low(first)
        d_packed[rows, 1024:1536] = d_attn
        add_vector(2, layer, column_sum(wide(d_attn)))
        d_mixed[rows, :] = low(dot(d_attn, wout[layer], NT))

    def put_tiles(batch, first_tile, matrix):
        for tile in range(4):
            at = (first_tile + tile) * 512
            batch[at : at + 512, :] = low(matrix[:, tile * 128 : (tile + 1) * 128])

    def dense_weights(layer, batch):
        put_tiles(batch, 0, dot(active[layer], d_packed[:, 0:512], TN))
        normed = normal_one[layer] * vector(gain_one, layer) + vector(shift_one, layer)
        put_tiles(batch, 4, dot(low(normed), d_packed[:, 512:1024], TN))
        put_tiles(batch, 8, dot(low(mixed[layer]), d_packed[:, 1024:1536], TN))

    def grad_copy(pair):
        return remote(
            sent.at[pair], received.at[pair], grad_send, grad_recv.at[pair], sibling
        )

    def attend_backward(layer, first_pair, last_pair):
        first_half = lane((ROWS, 128)) < 64

        for pair in range(first_pair, last_pair):
            columns = slice(pair * 128, (pair + 1) * 128)
            q_pair = queries[layer, :, columns]
            k_pair = keys[layer, 0:KEYS, columns]
            v_pair = values[layer, 0:KEYS, columns]
            d_out = low(wide(d_mixed[:, columns]) * inverses[layer, :, columns])
            d_wide = wide(d_out)
            d_turned = jnp.transpose(d_out)
            q_turned = jnp.transpose(q_pair)
            with_out = mixed[layer, :, columns] * d_wide
            with_own = wide(own(values, layer, columns)) * d_wide - with_out
            d_q, d_k, d_v, self_score, delta, d_probs = [], [], [], [], [], []
            for half in range(2):
                inside = first_half if half == 0 else jnp.logical_not(first_half)
                delta.append(jnp.sum(jnp.where(inside, with_out, 0.0), axis=1, keepdims=True))
                self_score.append(jnp.sum(jnp.where(inside, with_own, 0.0), axis=1, keepdims=True))
                d_probs.append(
                    dot(jnp.where(inside, d_out, jnp.zeros_like(d_out)), v_pair, NT)
                )
            for half in range(2):
                exponent = probs[2 * pair + half]
                d_scores = low(wide(exponent) * (d_probs[half] - delta[half]))
                d_q.append(dot(d_scores, k_pair, NN))
                d_k.append(dot(q_turned, d_scores, NN))
                d_v.append(dot(d_turned, exponent, NN))
            self_term = wide(self_parts[layer, :, columns])
            own_score = self_term * jnp.where(first_half, self_score[0], self_score[1])
            d_query = jnp.where(first_half, d_q[0], d_q[1]) + own_score * wide(
                own(keys, layer, columns)
            )
            d_packed[:, columns] = low(d_query * SCORE_SCALE)
            part_keys[0:KEYS, :] = jnp.transpose(
                jnp.concatenate([d_k[0][0:64], d_k[1][64:128]], axis=0)
            )
            part_values[0:KEYS, :] = jnp.transpose(
                jnp.concatenate([d_v[0][0:64], d_v[1][64:128]], axis=0)
            )
            own_keys = own_score * wide(q_pair)
            own_values = self_term * d_wide
            for slot in range(2):
                rows = slice(slot * SLOT, (slot + 1) * SLOT)
                mine = block_rows(slot, core)
                d_keys[rows, columns] = part_keys[mine, :] + own_keys[rows, :]
                d_values[rows, columns] = part_values[mine, :] + own_values[rows, :]
                other = block_rows(slot, 1 - core)
                sent[pair, 0, rows, :] = low(part_keys[other, :])
                sent[pair, 1, rows, :] = low(part_values[other, :])
            grad_copy(pair).start()

    def merge_grads(pairs):
        for pair in range(*pairs):
            grad_copy(pair).wait_recv()
            at = pair * 128
            columns = slice(at, at + 128)
            d_packed[:, 512 + at : 640 + at] = low(d_keys[:, columns] + wide(received[pair, 0]))
            d_packed[:, 1024 + at : 1152 + at] = low(d_values[:, columns] + wide(received[pair, 1]))

    def wait_sent():
        remote(sent, sent, grad_send, grad_recv.at[0], sibling).wait_send()

    def input_weights(layer, batch, first_row, third, pairs):
        first, last = pairs
        count = last - first
        columns = slice(third * 512 + first * 128, third * 512 + last * 128)
        product = dot(x_round[layer], d_packed[:, columns], TN)
        for tile in range(count):
            at = first_row + (third * count + tile) * 512
            batch[at : at + 512, :] = low(product[:, tile * 128 : (tile + 1) * 128])
        if third != 1:
            at = 2 * (third // 2) + layer
            inside = slice(first * 128, last * 128)
            vectors[at : at + 1, inside] = column_sum(wide(d_packed[:, columns]))

    def input_grad(layer, slot):
        rows = slot_rows(slot)
        stream[rows, :] = stream[rows, :] + dot(d_packed[rows, :], win[layer], NT)

    def reduction(index, batch, result, rows, deep):
        return Reduction(
            place, batch, result, rows, deep, reduction_refs[7 * index : 7 * index + 7]
        )

    group_rows = [1536 * (last - first) for first, last in GROUPS]
    group_at = [sum(group_rows[:index]) for index in range(len(GROUPS))]
    one_a = reduction(0, batch_a, reduced.at[0], BATCH_ROWS, True)
    one_b = reduction(1, batch_b, reduced.at[1], BATCH_ROWS, True)
    zero_a = reduction(2, batch_c, reduced.at[2], BATCH_ROWS, True)
    groups = [
        reduction(
            3 + index,
            batch_d.at[pl.ds(at, rows)],
            reduced.at[3, pl.ds(at, rows)],
            rows,
            index == 0,
        )
        for index, (at, rows) in enumerate(zip(group_at, group_rows))
    ]
    more = ExtraReduction(
        place, extra, extra_result, extra_out, reduction_refs[7 * (3 + len(GROUPS)) :]
    )
    running = {
        "one_a": one_a,
        "one_b": one_b,
        "zero_a": zero_a,
        "first": groups[0],
        "last": groups[1],
        "more": more,
    }

    def both_slots(work):
        def step(slot, _):
            work(slot)
            return 0

        lax.fori_loop(0, 2, step, 0)

    def after(piece):
        for name in PLAN.get(piece, ()):
            running[name].advance()

    for copy in small[1:]:
        copy.wait()
    load_hidden.wait()
    gather_scale(here)
    loads[0].wait()
    project_halves(here, False)
    swap_ids.wait()
    gather_scale(there)
    project_halves(there, True)
    project_queries(0)
    swap_cot.start()
    load_cot.start()
    for load in loads[4:]:
        load.start()
    probs_out = pltpu.make_async_copy(probs, kept_probs, probs_sem.at[0])
    probs_back = pltpu.make_async_copy(kept_probs, probs, probs_sem.at[1])

    def forward(layer, _):
        whole = keys.at[layer]
        remote(whole, whole, kv_send, kv_recv.at[layer], sibling).wait()

        @pl.when(layer == 1)
        def _():
            probs_out.wait()

        attend(layer)

        @pl.when(layer == 0)
        def _():
            probs_out.start()
            wait_rest.wait()
            wait_next.wait()

        def forward_slot(slot, _):
            dense_forward(layer, slot)

            @pl.when(layer == 0)
            def _():
                project_keys(1, slot)

            return 0

        lax.fori_loop(0, 2, forward_slot, 0)

        @pl.when(layer == 0)
        def _():
            project_queries(1)

        return 0

    lax.fori_loop(0, 2, forward, 0)

    out_round[...] = low(stream[...])
    keep_out = pltpu.make_async_copy(
        out_round.at[slot_rows(here)], layer_out.at[here], out_sems.at[0]
    )
    send_out = remote(
        out_round.at[slot_rows(there)],
        layer_out.at[here],
        swap_send.at[3],
        swap_recv.at[3],
        partner,
    )
    keep_out.start()
    send_out.start()

    load_cot.wait()
    swap_cot.wait()
    stream[...] = wide(cot[...])
    every = (0, PAIRS)
    both_slots(lambda slot: dense_backward(1, slot))
    dense_weights(1, batch_a)
    one_a.advance()
    for pair in range(PAIRS):
        attend_backward(1, pair, pair + 1)
        after(f"one pair {pair}")
    probs_back.start()
    input_weights(1, batch_b, 0, 0, every)
    after("one queries")
    merge_grads(every)
    after("one merge")
    input_weights(1, batch_b, 0, 1, every)
    after("one keys")
    input_weights(1, batch_b, 0, 2, every)
    one_b.advance()
    both_slots(lambda slot: input_grad(1, slot))
    after("one input")
    both_slots(lambda slot: dense_backward(0, slot))
    after("zero dense")
    dense_weights(0, batch_c)
    zero_a.advance()
    wait_sent()
    probs_back.wait()
    for pair in range(PAIRS):
        attend_backward(0, pair, pair + 1)
        after(f"zero pair {pair}")
        if pair == GROUPS[0][1]:
            merge_grads(GROUPS[0])
            for third in range(3):
                input_weights(0, batch_d, group_at[0], third, GROUPS[0])
            groups[0].advance()
    input_weights(0, batch_d, group_at[1], 0, GROUPS[1])
    after("zero queries")
    merge_grads(GROUPS[1])
    after("zero merge")
    for third in (1, 2):
        input_weights(0, batch_d, group_at[1], third, GROUPS[1])
    groups[1].advance()
    after("zero values")
    keep_grad = pltpu.make_async_copy(
        d_mixed.at[slot_rows(here)], grad_hidden.at[here], out_sems.at[1]
    )

    def grad_piece(start, count):
        return remote(
            d_mixed.at[pl.ds(pl.multiple_of(there * SLOT + start, 16), count)],
            grad_hidden.at[here, pl.ds(start, count)],
            swap_send.at[4],
            swap_recv.at[4],
            partner,
        )


    def hidden_grad(slot):
        rows = slot_rows(slot)
        input_grad(0, slot)
        d_mixed[rows, :] = low(stream[rows, :] * get_column(rows, 5))

    hidden_grad(there)
    after("zero there")
    hidden_grad(here)
    keep_grad.start()
    after("zero here")

    genes = jnp.zeros((GENE_ROWS, 128), jnp.float32)
    for slot in range(2):
        rows = slot_rows(slot)
        is_high, is_low = slot_ids(slot)
        per_token = jnp.sum(stream[rows, :] * wide(hidden[rows, :]), axis=1, keepdims=True)
        row = jnp.transpose(jnp.broadcast_to(per_token, (SLOT, 128)))
        for piece in split_three(jnp.where(is_low, row, 0.0)):
            genes = genes + dot(is_high, piece, NT)
    extra[0:GENE_ROWS, :] = genes
    for index in range(18):
        for tile in range(4):
            at = GENE_ROWS + 4 * index + tile
            extra[at : at + 1, :] = vectors[index : index + 1, tile * 128 : (tile + 1) * 128]
    after("genes")
    more.advance()
    for index, name in enumerate(ENDING):
        running[name].advance()
        if index % 2 == 0 and index < 16:
            grad_piece(index * 16, 32).start()
    for one in running.values():
        assert one.at == one.last + 1
    wait_sent()
    keep_out.wait()
    send_out.wait()
    keep_grad.wait()
    grad_piece(0, SLOT).wait()


def run_model(hidden_in, cotangent, gene_ids, unknown_count, table, weights, vector_args):
    f32, bf16 = jnp.float32, jnp.bfloat16
    smem = pl.BlockSpec(memory_space=pltpu.SMEM)
    anywhere = pl.BlockSpec(memory_space=pl.ANY)
    scratch = [
        pltpu.VMEM((ROWS, 512), bf16),
        pltpu.VMEM((3, 8, SLOT), jnp.int32),
        pltpu.VMEM((2, 512, 1536), bf16),
        pltpu.VMEM((2, 512, 512), bf16),
        pltpu.VMEM((2, 512, 512), bf16),
        pltpu.VMEM((2, 512, 512), bf16),
        pltpu.VMEM((ROWS, 512), f32),
        pltpu.VMEM((2, ROWS, 512), bf16),
        pltpu.VMEM((2, ROWS, 512), bf16),
        pltpu.VMEM((2, GENES, 512), bf16),
        pltpu.VMEM((2, GENES, 512), bf16),
        pltpu.VMEM((HEADS, ROWS, KEYS), bf16),
        pltpu.VMEM((ROWS, 128), f32),
        pltpu.VMEM((2, ROWS, 512), f32),
        pltpu.VMEM((2, ROWS, 512), bf16),
        pltpu.VMEM((2, ROWS, 512), f32),
        pltpu.VMEM((2, ROWS, 512), f32),
        pltpu.VMEM((2, ROWS, 512), f32),
        pltpu.VMEM((2, ROWS, 512), f32),
        pltpu.VMEM((2, ROWS, 512), bf16),
        pltpu.VMEM((ROWS, 512), bf16),
        pltpu.VMEM((ROWS, 1536), bf16),
        pltpu.VMEM((ROWS, 512), f32),
        pltpu.VMEM((ROWS, 512), f32),
        pltpu.VMEM((GENES, 128), f32),
        pltpu.VMEM((GENES, 128), f32),
        pltpu.VMEM((PAIRS, 2, ROWS, 128), bf16),
        pltpu.VMEM((PAIRS, 2, ROWS, 128), bf16),
        pltpu.VMEM((8, KEYS), f32),
        pltpu.VMEM((24, 512), f32),
        pltpu.VMEM((ROWS, 512), bf16),
        pltpu.VMEM((EXTRA_ROWS, 128), f32),
        pltpu.VMEM((BATCH_ROWS, 128), bf16),
        pltpu.VMEM((BATCH_ROWS, 128), bf16),
        pltpu.VMEM((BATCH_ROWS, 128), bf16),
        pltpu.VMEM((BATCH_ROWS, 128), bf16),
        pltpu.VMEM((EXTRA_ROWS, 128), f32),
        pltpu.SemaphoreType.DMA((16,)),
        pltpu.SemaphoreType.DMA((6,)),
        pltpu.SemaphoreType.DMA((6,)),
        pltpu.SemaphoreType.DMA,
        pltpu.SemaphoreType.DMA((2,)),
        pltpu.SemaphoreType.DMA,
        pltpu.SemaphoreType.DMA((PAIRS,)),
        pltpu.SemaphoreType.DMA((2,)),
        pltpu.SemaphoreType.DMA((2,)),
    ]
    for _ in range(3):
        scratch += Reduction.scratch(BATCH_ROWS, True)
    for index, (first, last) in enumerate(GROUPS):
        scratch += Reduction.scratch(1536 * (last - first), index == 0)
    scratch += ExtraReduction.scratch()
    scratch += [pltpu.VMEM((2, SLOT), jnp.int32), pltpu.VMEM((GENE_ROWS, 128), f32)]
    scratch += [pltpu.VMEM((2, 512), f32)] * 9
    outs = (
        jax.ShapeDtypeStruct((2, SLOT, 512), bf16),
        jax.ShapeDtypeStruct((2, SLOT, 512), bf16),
        jax.ShapeDtypeStruct((4, BATCH_ROWS, 128), bf16),
        jax.ShapeDtypeStruct((EXTRA_ROWS, 128), f32),
        jax.ShapeDtypeStruct((HEADS, ROWS, KEYS), bf16),
    )
    return pl.pallas_call(
        model_kernel,
        out_shape=outs,
        in_specs=[anywhere] * 3 + [smem] + [anywhere] * 14,
        out_specs=(anywhere,) * 5,
        scratch_shapes=scratch,
        compiler_params=pltpu.CompilerParams(
            collective_id=0, has_side_effects=True, vmem_limit_bytes=255 << 18
        ),
        name="model",
    )(hidden_in, cotangent, gene_ids, unknown_count, table, *weights, *vector_args)


def finish_kernel(layer_in, hidden_grad_in, reduced, extra, *refs):
    layer_out, hidden_out, g_inputs, g_output, g_up, g_down, genes = refs[:7]
    vector_outs = refs[7:16]
    rounded, narrow, rows_out, wide_in, wide_rest, extra_rows, in_sems, out_sems = refs[16:]
    sources = [layer_in, hidden_grad_in]
    loads = [
        pltpu.make_async_copy(sources[i], rounded.at[i], in_sems.at[i]) for i in range(2)
    ] + [pltpu.make_async_copy(reduced.at[i], narrow.at[i], in_sems.at[2 + i]) for i in range(4)]
    loads.append(pltpu.make_async_copy(extra, extra_rows, in_sems.at[6]))
    for load in loads[:1] + loads[6:] + loads[1:6]:
        load.start()
    stores = []

    def send(source, target):
        store = pltpu.make_async_copy(source, target, out_sems.at[len(stores)])
        store.start()
        stores.append(store)

    for index, target in enumerate((layer_out, hidden_out)):
        loads[index].wait()
        rows_out[index] = wide(rounded[index])
        send(rows_out.at[index], target)
    for layer in (1, 0):
        base = 2 * (1 - layer)
        loads[2 + base].wait()
        for index, target in enumerate((g_down, g_up, g_output)):
            for tile in range(4):
                at = (4 * index + tile) * 512
                wide_rest[layer, index, :, tile * 128 : (tile + 1) * 128] = wide(
                    narrow[base, at : at + 512, :]
                )
            send(wide_rest.at[layer, index], target.at[layer])
        loads[3 + base].wait()
        at = 0
        for first, last in GROUPS if layer == 0 else ((0, PAIRS),):
            for third in range(3):
                for pair in range(first, last):
                    column = third * 512 + pair * 128
                    wide_in[layer, :, column : column + 128] = wide(
                        narrow[base + 1, at : at + 512, :]
                    )
                    at += 512
        send(wide_in.at[layer], g_inputs.at[layer])
    loads[6].wait()
    genes[...] = extra_rows[0:GENE_ROWS, :]
    for member in range(9):
        for layer in range(2):
            for tile in range(4):
                at = GENE_ROWS + 4 * (2 * member + layer) + tile
                vector_outs[member][layer : layer + 1, tile * 128 : (tile + 1) * 128] = extra_rows[
                    at : at + 1, :
                ]
    for store in stores:
        store.wait()


def finish(layer_out, grad_hidden, reduced, extra):
    f32, bf16 = jnp.float32, jnp.bfloat16
    vmem = pl.BlockSpec(memory_space=pltpu.VMEM)
    anywhere = pl.BlockSpec(memory_space=pl.ANY)
    outs = [
        jax.ShapeDtypeStruct((2, SLOT, 512), f32),
        jax.ShapeDtypeStruct((2, SLOT, 512), f32),
        jax.ShapeDtypeStruct((2, 512, 1536), f32),
        jax.ShapeDtypeStruct((2, 512, 512), f32),
        jax.ShapeDtypeStruct((2, 512, 512), f32),
        jax.ShapeDtypeStruct((2, 512, 512), f32),
        jax.ShapeDtypeStruct((GENE_ROWS, 128), f32),
    ] + [jax.ShapeDtypeStruct((2, 512), f32)] * 9
    return pl.pallas_call(
        finish_kernel,
        out_shape=outs,
        in_specs=[anywhere] * 4,
        out_specs=[anywhere] * 6 + [vmem] * 10,
        scratch_shapes=[
            pltpu.VMEM((2, 2, SLOT, 512), bf16),
            pltpu.VMEM((4, BATCH_ROWS, 128), bf16),
            pltpu.VMEM((2, 2, SLOT, 512), f32),
            pltpu.VMEM((2, 512, 1536), f32),
            pltpu.VMEM((2, 3, 512, 512), f32),
            pltpu.VMEM((EXTRA_ROWS, 128), f32),
            pltpu.SemaphoreType.DMA((7,)),
            pltpu.SemaphoreType.DMA((10,)),
        ],
        compiler_params=pltpu.CompilerParams(vmem_limit_bytes=63 << 20),
        name="finish",
    )(layer_out, grad_hidden, reduced, extra)


def shards(
    hidden_in,
    gene_ids,
    unknown_count,
    gene_scale,
    w_inputs,
    b_query,
    b_value,
    w_output,
    b_output,
    gain_one,
    shift_one,
    w_up,
    b_up,
    w_down,
    b_down,
    gain_two,
    shift_two,
    cotangent,
):
    gene_count = gene_scale.shape[0]
    table = jnp.pad(gene_scale, (0, GENE_ROWS * 128 - gene_count)).reshape(GENE_ROWS, 128)
    layer_out, grad_hidden, reduced, extra, _ = run_model(
        hidden_in,
        cotangent,
        gene_ids,
        unknown_count,
        table,
        (w_inputs, w_output, w_up, w_down),
        (b_query, b_value, b_output, gain_one, shift_one, b_up, b_down, gain_two, shift_two),
    )
    (
        layer_out,
        grad_hidden,
        g_inputs,
        g_output,
        g_up,
        g_down,
        genes,
        g_b_query,
        g_b_value,
        g_b_output,
        g_gain_one,
        g_shift_one,
        g_b_up,
        g_b_down,
        g_gain_two,
        g_shift_two,
    ) = finish(layer_out, grad_hidden, reduced, extra)
    return (
        layer_out,
        grad_hidden,
        genes.reshape(-1)[:gene_count],
        g_inputs,
        g_b_query,
        g_b_value,
        g_output,
        g_b_output,
        g_gain_one,
        g_shift_one,
        g_up,
        g_b_up,
        g_down,
        g_b_down,
        g_gain_two,
        g_shift_two,
    )


def solution(mesh):
    placed = (
        P("dp", "blk", None),
        P("dp", "blk"),
        P("dp"),
        P(),
        P(),
        P(),
        P(),
        P(),
        P(),
        P(),
        P(),
        P(),
        P(),
        P(),
        P(),
        P(),
        P(),
        P("dp", "blk", None),
    )
    return jax.shard_map(
        shards,
        mesh=mesh,
        in_specs=placed,
        out_specs=(
            P("dp", "blk", None),
            P("dp", "blk", None),
            P(),
            P(),
            P(),
            P(),
            P(),
            P(),
            P(),
            P(),
            P(),
            P(),
            P(),
            P(),
            P(),
            P(),
        ),
        check_vma=False,
    )
```
